32 devices in a mesh: row: 8 (over z, x), dp: 4 (over y, core).
Axes of the slice: x: 2, y: 2, z: 4, core: 2. Of those that a mesh axis runs over, the one named last changes fastest.
Arguments:
- enc_input: bfloat16 [32, 768, 768], P(('row', 'dp')), may hold values from -6 to 6
- dec_input: bfloat16 [32, 256, 768], P(('row', 'dp')), may hold values from -6 to 6
- memory_table: bfloat16 [4096, 768], P('dp'), may hold values from -6 to 6
- memory_ids: int32 [32, 8, 10], P(('row', 'dp')), may hold values from 0 to 4095, as said below
- enc_segments: int32 [32, 768], P(('row', 'dp')), may hold values from 0 to 7, never falling along the last dimension, each value on 1 to 576 neighbouring positions
- dec_segments: int32 [32, 256], P(('row', 'dp')), may hold values from 0 to 7, never falling along the last dimension, each value on 1 to 192 neighbouring positions
- enc_qkv: bfloat16 [3, 768, 768], replicated, may hold values from -0.21875 to 0.21875
- enc_attn_out: bfloat16 [768, 768], replicated, may hold values from -2 to 2
- mem_proj: bfloat16 [2, 768, 768], replicated, may hold values from -0.21875 to 0.21875
- enc_gains: bfloat16 [2, 768], replicated, may hold values from 0.5 to 1.5
- enc_ff_in: bfloat16 [768, 3072], replicated, may hold values from -0.21875 to 0.21875
- enc_ff_out: bfloat16 [3072, 768], replicated, may hold values from -0.109375 to 0.109375
- dec_qkv: bfloat16 [3, 768, 768], replicated, may hold values from -0.21875 to 0.21875
- dec_self_out: bfloat16 [768, 768], replicated, may hold values from -0.875 to 0.875
- dec_cross: bfloat16 [3, 768, 768], replicated, may hold values from -0.21875 to 0.21875
- dec_cross_out: bfloat16 [768, 768], replicated, may hold values from -2 to 2
- dec_gains: bfloat16 [3, 768], replicated, may hold values from 0.5 to 1.5
- dec_ff_in: bfloat16 [768, 3072], replicated, may hold values from -0.21875 to 0.21875
- dec_ff_out: bfloat16 [3072, 768], replicated, may hold values from -0.109375 to 0.109375
- out_grad: bfloat16 [32, 256, 768], P(('row', 'dp')), may hold values from -6 to 6
Outputs:
- dec_out: bfloat16 [32, 256, 768], P(('row', 'dp'))
- enc_input_grad: float32 [32, 768, 768], P(('row', 'dp'))
- dec_input_grad: float32 [32, 256, 768], P(('row', 'dp'))
- enc_qkv_grad: float32 [3, 768, 768], P(None, None, 'dp')
- enc_attn_out_grad: float32 [768, 768], P(None, 'dp')
- mem_proj_grad: float32 [2, 768, 768], P(None, None, 'dp')
- enc_gains_grad: float32 [2, 768], P(None, 'dp')
- enc_ff_in_grad: float32 [768, 3072], P(None, 'dp')
- enc_ff_out_grad: float32 [3072, 768], P(None, 'dp')
- dec_qkv_grad: float32 [3, 768, 768], P(None, None, 'dp')
- dec_self_out_grad: float32 [768, 768], P(None, 'dp')
- dec_cross_grad: float32 [3, 768, 768], P(None, None, 'dp')
- dec_cross_out_grad: float32 [768, 768], P(None, 'dp')
- dec_gains_grad: float32 [2, 768], P(None, 'dp')
- dec_ff_in_grad: float32 [768, 3072], P(None, 'dp')
- dec_ff_out_grad: float32 [3072, 768], P(None, 'dp')
- dec_ffn_gain_grad: float32 [768], P('dp')
The draws below stay inside these ranges and needn't reach their ends.
Inputs may be any that keep to these rules, and one draw needn't show every extreme that they name: `memory_ids`: each entry names one row of memory_table; the last row is named in every draw. `enc_segments`: never falls along a row; each of the 8 questions has 1 to 576 tokens in every packed row. `dec_segments`: never falls along a row; each of the 8 questions has 1 to 192 answer tokens in every row, in the same order as in enc_segments.
All inputs are finite; a program needn't handle non-finite values.
Results may differ from the reference program's by a relative error of at most 0.035.
The reference program's roundings to bfloat16 on the way count: a program that leaves them out, or rounds other values in their place, can miss the bound.
Values may be sent and summed in bfloat16 or wider, within the bound.
A program may use at most 320 MiB of HBM per device.

```python
import math
import jax
import jax.numpy as jnp
import numpy as np
from jax import lax

D = 768
HEADS = 12
HD = 64
FF = 3072
ENC_LEN = 768
DEC_LEN = 256
SEGS = 8
TOPK = 10
ROWS = 32
MEM = 4096


def draw_memory_ids(key, part):
    key = jax.random.fold_in(key, 7)
    first, second = jax.random.split(key)
    picked = jax.random.randint(first, (ROWS, SEGS, TOPK), 0, MEM)
    place = jax.random.randint(second, (), 0, ROWS * SEGS * TOPK)
    position = jnp.arange(ROWS * SEGS * TOPK).reshape(ROWS, SEGS, TOPK)
    return jnp.where(position == place, MEM - 1, picked).astype(jnp.int32)


def spiked(array, stream_key, source, target, parts, factor):
    owner, partner = [(jnp.arange(array.shape[axis_at]) // (array.shape[axis_at] // parts)).reshape([-1 if axis == axis_at else 1 for axis in range(array.ndim)]) for axis_at in (source, target)]
    chosen = jax.random.permutation(stream_key, parts)[partner]
    strong = (owner == chosen) | (owner == (partner + parts // 2) % parts)
    return jnp.where(strong, factor * array, array)


def levels(stream_key, dims, cuts, low, largest):
    level = 1.0
    for dim, parts in cuts:
        steps = jax.random.uniform(jax.random.fold_in(jax.random.fold_in(stream_key, 6), dim), (parts,), jnp.float32, low / len(cuts), largest / len(cuts))
        level = level * jnp.repeat(jnp.exp(steps), dims[dim] // parts).reshape((-1,) + (1,) * (len(dims) - 1 - dim))
    return level


def split_up(count, total, limit, slope):
    portions = [(1 << 20) // math.isqrt(standing ** slope) + 1 for standing in range(2, count + 1)]
    surplus, holding = total - limit - (count - 1), [1] * (count - 1)
    while surplus > 0:
        candidates = [i for i in range(count - 1) if holding[i] < limit]
        mass, budget = sum([portions[i] for i in candidates]), surplus
        for i in candidates:
            addition = min(limit - holding[i], max(1, budget * portions[i] // mass), surplus)
            holding[i] = holding[i] + addition
            surplus = surplus - addition
    return np.array([limit] + holding)


def uneven(key, number_of, total, most, skew):
    if number_of == 2:
        one = jax.random.randint(key, (), max(1, total - most), min(most, total - 1) + 1)
        return jnp.stack([one, total - one])
    sizes = jnp.asarray(split_up(number_of, total, most, skew), jnp.int32)
    couples = (number_of - 1) // 2
    giver, receiver = sizes[1:1 + 2 * couples:2], sizes[2:2 + 2 * couples:2]
    room = jnp.minimum(giver - 1, most - receiver)
    moved = jax.random.randint(jax.random.fold_in(key, 1), (couples,), 0, 1 << 20) % (room + 1)
    sizes = sizes.at[1:1 + 2 * couples:2].set(giver - moved).at[2:2 + 2 * couples:2].set(receiver + moved)
    return sizes[jax.random.permutation(jax.random.fold_in(key, 2), number_of)]


def normal_values(stream_key, shape, scale, bound, pieces=(), kind=jnp.bfloat16):
    level = levels(stream_key, shape, pieces, -0.22, 0.18) if pieces else 1.0
    result = jax.random.normal(stream_key, shape, jnp.float32) * scale * level
    return jnp.minimum(jnp.maximum(result, -bound), bound).astype(kind)


def bell_draw_with(own_key, extent, width, reach, cuts, heavy, kind=jnp.bfloat16):
    drawn = width * jax.random.normal(own_key, extent, jnp.float32)
    if cuts:
        drawn = drawn * levels(own_key, extent, cuts, -0.22, 0.18)
    return jnp.clip(spiked(drawn, jax.random.fold_in(own_key, 3), *heavy), -reach, reach).astype(kind)


def setup_inputs(seed: int = 0) -> dict:
    key_of = jax.random.split(jax.random.key(seed), 21)
    enc_input = normal_values(key_of[0], (ROWS, ENC_LEN, D), 1.0, 6.0, ((0, 32),))
    dec_input = normal_values(key_of[1], (ROWS, DEC_LEN, D), 1.0, 6.0, ((0, 32),))
    memory_table = normal_values(key_of[2], (MEM, D), 1.0, 6.0, ((0, 4),))
    memory_ids = draw_memory_ids(jax.random.fold_in(key_of[20], 71), 0)
    enc_segments = jax.vmap(lambda own: jnp.searchsorted(jnp.cumsum(uneven(own, SEGS, ENC_LEN, 3 * ENC_LEN // 4, 1)), jnp.arange(ENC_LEN), side="right"))(jax.random.split(key_of[4], ROWS)).reshape((ROWS, ENC_LEN)).astype(jnp.int32)
    dec_segments = jax.vmap(lambda own: jnp.searchsorted(jnp.cumsum(uneven(own, SEGS, DEC_LEN, 3 * DEC_LEN // 4, 1)), jnp.arange(DEC_LEN), side="right"))(jax.random.split(key_of[5], ROWS)).reshape((ROWS, DEC_LEN)).astype(jnp.int32)
    enc_qkv = normal_values(key_of[6], (3, D, D), D ** -0.5, 0.21875)
    enc_attn_out = normal_values(key_of[7], (D, D), (max(D * SEGS // ENC_LEN, 1)) ** -0.5, 2.0)
    mem_proj = normal_values(key_of[8], (2, D, D), D ** -0.5, 0.21875)
    enc_gains = jnp.clip(1.0 + 0.1 * jax.random.normal(key_of[9], (2, D), jnp.float32), 0.5, 1.5).astype(jnp.bfloat16)
    enc_ff_in = normal_values(key_of[10], (D, FF), D ** -0.5, 0.21875)
    enc_ff_out = normal_values(key_of[11], (FF, D), FF ** -0.5, 0.109375)
    dec_qkv = normal_values(key_of[12], (3, D, D), D ** -0.5, 0.21875)
    dec_self_out = normal_values(key_of[13], (D, D), (max(2 * D * SEGS // DEC_LEN, 1)) ** -0.5, 0.875)
    dec_cross = normal_values(key_of[14], (3, D, D), D ** -0.5, 0.21875)
    dec_cross_out = normal_values(key_of[15], (D, D), (max(D * SEGS // ENC_LEN, 1)) ** -0.5, 2.0)
    dec_gains = jnp.clip(1.0 + 0.1 * jax.random.normal(key_of[16], (3, D), jnp.float32), 0.5, 1.5).astype(jnp.bfloat16)
    dec_ff_in = normal_values(key_of[17], (D, FF), D ** -0.5, 0.21875)
    dec_ff_out = normal_values(key_of[18], (FF, D), FF ** -0.5, 0.109375)
    out_grad = bell_draw_with(key_of[19], (ROWS, DEC_LEN, D), 1.0, 6.0, ((0, 32),), (0, 2, 32, 2.75))
    return dict(enc_input=enc_input, dec_input=dec_input, memory_table=memory_table, memory_ids=memory_ids, enc_segments=enc_segments, dec_segments=dec_segments, enc_qkv=enc_qkv, enc_attn_out=enc_attn_out, mem_proj=mem_proj, enc_gains=enc_gains, enc_ff_in=enc_ff_in, enc_ff_out=enc_ff_out, dec_qkv=dec_qkv, dec_self_out=dec_self_out, dec_cross=dec_cross, dec_cross_out=dec_cross_out, dec_gains=dec_gains, dec_ff_in=dec_ff_in, dec_ff_out=dec_ff_out, out_grad=out_grad)


@jax.custom_vjp
def low(v):
    return lax.optimization_barrier(v.astype(jnp.bfloat16)).astype(jnp.float32)

@jax.custom_vjp
def low_back(v):
    return v

def low_keep(v):
    return (low(v), None)

def low_pass(kept, grad):
    return (grad,)

def back_keep(v):
    return (v, None)

def back_low(kept, grad):
    return (low(grad),)
low.defvjp(low_keep, low_pass)
low_back.defvjp(back_keep, back_low)

def matmul(left, right):
    return jnp.dot(left, right, precision=lax.Precision.HIGHEST, preferred_element_type=jnp.float32)

def rms_norm(inputs, gain):
    return inputs * lax.rsqrt(lax.optimization_barrier(jnp.mean(inputs * inputs, axis=-1, keepdims=True)) + 1e-06) * gain

def project(inputs, weight):
    return low(low_back(matmul(inputs, weight)))

def attend(queries, keys, values, allowed):
    heads_query = queries.reshape(queries.shape[0], HEADS, HD)
    heads_key = keys.reshape(keys.shape[0], HEADS, HD)
    heads_value = values.reshape(values.shape[0], HEADS, HD)
    scores = low_back(jnp.einsum('qhd,khd->hqk', heads_query, heads_key, precision=lax.Precision.HIGHEST) * HD ** (-0.5))
    scores = jnp.where(allowed[None], scores, -1e+30)
    exponent = jnp.exp(scores - lax.optimization_barrier(jnp.max(scores, axis=-1, keepdims=True)))
    probs = low(exponent / lax.optimization_barrier(jnp.sum(exponent, axis=-1, keepdims=True)))
    mixed = jnp.einsum('hqk,khd->qhd', probs, heads_value, precision=lax.Precision.HIGHEST)
    return low(low_back(mixed.reshape(queries.shape[0], -1)))

def encoder(tokens, fetched, questions, weights):
    qkv_weight, attn_out, memory_proj, gains, ff_in, ff_out = weights
    normed = low(rms_norm(tokens, gains[0]))
    memory_keys = project(fetched, memory_proj[0])
    memory_values = project(fetched, memory_proj[1])
    owner = jnp.arange(fetched.shape[0]) // TOPK
    allowed = jnp.concatenate([questions[:, None] == questions[None, :], questions[:, None] == owner[None, :]], axis=1)
    keys = jnp.concatenate([project(normed, qkv_weight[1]), memory_keys], axis=0)
    values = jnp.concatenate([project(normed, qkv_weight[2]), memory_values], axis=0)
    mixed = attend(project(normed, qkv_weight[0]), keys, values, allowed)
    middle = tokens + low_back(matmul(mixed, attn_out))
    hidden = low(jax.nn.gelu(low_back(matmul(low(rms_norm(middle, gains[1])), ff_in))))
    return middle + low_back(matmul(hidden, ff_out))

def decoder(answers, encoded, questions, answer_questions, weights):
    qkv_weight, self_out, cross, cross_out, gains, ff_in, ff_out = weights
    normed = low(rms_norm(answers, gains[0]))
    position = jnp.arange(answers.shape[0])
    self_allowed = (answer_questions[:, None] == answer_questions[None, :]) & (position[None, :] <= position[:, None])
    mixed = attend(project(normed, qkv_weight[0]), project(normed, qkv_weight[1]), project(normed, qkv_weight[2]), self_allowed)
    first = answers + low_back(matmul(mixed, self_out))
    normed = low(rms_norm(first, gains[1]))
    encoded_low = low(encoded)
    cross_allowed = answer_questions[:, None] == questions[None, :]
    mixed = attend(project(normed, cross[0]), project(encoded_low, cross[1]), project(encoded_low, cross[2]), cross_allowed)
    second = first + low_back(matmul(mixed, cross_out))
    hidden = low(jax.nn.gelu(low_back(matmul(low(rms_norm(second, gains[2])), ff_in))))
    return second + low_back(matmul(hidden, ff_out))

def reference(enc_input, dec_input, memory_table, memory_ids, enc_segments, dec_segments, enc_qkv, enc_attn_out, mem_proj, enc_gains, enc_ff_in, enc_ff_out, dec_qkv, dec_self_out, dec_cross, dec_cross_out, dec_gains, dec_ff_in, dec_ff_out, out_grad):
    fetched = memory_table[memory_ids.reshape(memory_ids.shape[0], -1)].astype(jnp.float32)
    weights = (enc_qkv.astype(jnp.float32), enc_attn_out.astype(jnp.float32), mem_proj.astype(jnp.float32), enc_gains.astype(jnp.float32), enc_ff_in.astype(jnp.float32), enc_ff_out.astype(jnp.float32), dec_qkv.astype(jnp.float32), dec_self_out.astype(jnp.float32), dec_cross.astype(jnp.float32), dec_cross_out.astype(jnp.float32), dec_gains.astype(jnp.float32), dec_ff_in.astype(jnp.float32), dec_ff_out.astype(jnp.float32))

    def forward(params, tokens, answers):

        def one_row(items):
            row_tokens, row_answers, row_fetched, row_questions, row_answer_questions = items
            encoded = encoder(row_tokens, row_fetched, row_questions, params[:6])
            return decoder(row_answers, encoded, row_questions, row_answer_questions, params[6:])
        return lax.map(jax.checkpoint(one_row), (tokens, answers, fetched, enc_segments, dec_segments))
    final, pullback = jax.vjp(forward, weights, enc_input.astype(jnp.float32), dec_input.astype(jnp.float32))
    weight_grads, enc_input_grad, dec_input_grad = pullback(out_grad.astype(jnp.float32))
    return (final.astype(jnp.bfloat16), enc_input_grad, dec_input_grad, weight_grads[0], weight_grads[1], weight_grads[2], weight_grads[3], weight_grads[4], weight_grads[5], weight_grads[6], weight_grads[7], weight_grads[8], weight_grads[9], weight_grads[10][0:2], weight_grads[11], weight_grads[12], weight_grads[10][2])
```

```python
import functools

import jax
import jax.numpy as jnp
from jax import lax
from jax.experimental import pallas as pl
from jax.experimental.pallas import tpu as pltpu
from jax.sharding import PartitionSpec as P

HD = 64
TOPK = 10
LANES = 128
MASKED = -1e30
BF = jnp.bfloat16
F32 = jnp.float32


def nn(left, right):
    return lax.dot_general(left, right, (((1,), (0,)), ((), ())), preferred_element_type=F32)


def nt(left, right):
    return lax.dot_general(left, right, (((1,), (1,)), ((), ())), preferred_element_type=F32)


def tn(left, right):
    return lax.dot_general(left, right, (((0,), (0,)), ((), ())), preferred_element_type=F32)


def full(shape):
    return pl.BlockSpec(shape, lambda *_: (0,) * len(shape))


def params(mib=48):
    return pltpu.CompilerParams(vmem_limit_bytes=mib * 2**20)


def cost(flops, nbytes, exps=0):
    return pl.CostEstimate(flops=int(flops), bytes_accessed=int(nbytes), transcendentals=int(exps))


def rms_scale(x):
    return lax.rsqrt(jnp.mean(x * x, axis=-1, keepdims=True) + 1e-06)


def rms_back(x, gain, dy):
    scale = rms_scale(x)
    gain_grad = jnp.sum(dy * x * scale, axis=0, keepdims=True)
    inner = dy * gain
    mixed = jnp.mean(inner * x, axis=-1, keepdims=True)
    return scale * (inner - x * (scale * scale) * mixed), gain_grad


def proj_kernel(residual, x, gain, *refs):
    if residual:
        mixed, wo, w, mid, low, out = refs
    else:
        w, low, out = refs

    @pl.when(pl.program_id(0) == 0)
    def _():
        value = x[...].astype(F32)
        if residual:
            value = value + nn(mixed[...], wo[...])
            mid[...] = value
        low[...] = (value * rms_scale(value) * gain[...]).astype(BF)

    out[...] = nn(low[...], w[...]).astype(BF)


def project(x, gain, w, first, count, mixed=None, wo=None):
    t, d = x.shape
    residual = mixed is not None
    args = [x, gain]
    specs = [full((t, d)), full((1, d))]
    outs = [jax.ShapeDtypeStruct((t, d), BF), jax.ShapeDtypeStruct((count, t, d), BF)]
    out_specs = [full((t, d)), pl.BlockSpec((None, t, d), lambda j: (j, 0, 0))]
    if residual:
        args += [mixed, wo]
        specs += [full((t, d)), full((d, d))]
        outs = [jax.ShapeDtypeStruct((t, d), F32)] + outs
        out_specs = [full((t, d))] + out_specs
    args.append(w)
    specs.append(pl.BlockSpec((None, d, d), lambda j: (first + j, 0, 0)))
    return pl.pallas_call(
        functools.partial(proj_kernel, residual),
        grid=(count,),
        in_specs=specs,
        out_specs=out_specs,
        out_shape=outs,
        compiler_params=params(),
        cost_estimate=cost(2 * t * d * d * (count + residual), 2 * d * (t + d) * (count + 2)),
        name="project",
    )(*args)


def pairs_kernel(x, w, out):
    out[...] = nn(x[...], w[...]).astype(BF)


def project_plain(x, w, first, count):
    t, d = x.shape
    return pl.pallas_call(
        pairs_kernel,
        grid=(count,),
        in_specs=[full((t, d)), pl.BlockSpec((None, d, d), lambda j: (first + j, 0, 0))],
        out_specs=pl.BlockSpec((None, t, d), lambda j: (j, 0, 0)),
        out_shape=jax.ShapeDtypeStruct((count, t, d), BF),
        compiler_params=params(),
        cost_estimate=cost(2 * t * d * d * count, 2 * d * (t + d) * count),
        name="project_plain",
    )(x, w)


def proj_back_kernel(count, x, gain, grad, w, *refs):
    parts = refs[:count]
    new, low, gain_grad, total = refs[count:]
    step = pl.program_id(0)
    for j in range(count):

        @pl.when(step == j)
        def _(j=j):
            value = nt(parts[j][...], w[...])
            total[...] = value if j == 0 else total[...] + value

    @pl.when(step == count - 1)
    def _():
        back, gain_grad[...] = rms_back(x[...].astype(F32), gain[...], total[...])
        value = grad[...] + back
        new[...] = value
        low[...] = value.astype(BF)


def proj_back(x, gain, grad, w, parts):
    t, d = x.shape
    count = len(parts)
    return pl.pallas_call(
        functools.partial(proj_back_kernel, count),
        grid=(count,),
        in_specs=[full((t, d)), full((1, d)), full((t, d))]
        + [pl.BlockSpec((None, d, d), lambda j: (j, 0, 0))]
        + [full((t, d))] * count,
        out_specs=[full((t, d)), full((t, d)), full((1, d))],
        out_shape=[
            jax.ShapeDtypeStruct((t, d), F32),
            jax.ShapeDtypeStruct((t, d), BF),
            jax.ShapeDtypeStruct((1, d), F32),
        ],
        scratch_shapes=[pltpu.VMEM((t, d), F32)],
        compiler_params=params(),
        cost_estimate=cost(2 * t * d * d * count, 2 * d * (t + d) * count + 12 * t * d),
        name="proj_back",
    )(x, gain, grad, w, *parts)


GELU_A = 0.7978845608028654
GELU_B = 0.044715


def ffn_kernel(res, mixed, wo, gain, w_in, w_out, mid, low, hidden, slope, out, total):
    step = pl.program_id(0)

    @pl.when(step == 0)
    def _():
        value = res[...].astype(F32) + nn(mixed[...], wo[...])
        mid[...] = value
        low[...] = (value * rms_scale(value) * gain[...]).astype(BF)
        total[...] = value

    pre = nn(low[...], w_in[...])
    square = pre * pre
    bent = jnp.tanh(GELU_A * pre * (1.0 + GELU_B * square))
    half = 0.5 * (1.0 + bent)
    act = (pre * half).astype(BF)
    hidden[...] = act
    slope[...] = (
        half + (0.5 * GELU_A) * pre * (1.0 - bent * bent) * (1.0 + (3.0 * GELU_B) * square)
    ).astype(BF)
    total[...] += nn(act, w_out[...])

    @pl.when(step == pl.num_programs(0) - 1)
    def _():
        out[...] = total[...].astype(BF)


def ffn_forward(res, mixed, wo, gain, w_in, w_out, block=512):
    t, d = res.shape
    ff = w_in.shape[1]
    return pl.pallas_call(
        ffn_kernel,
        grid=(ff // block,),
        in_specs=[
            full((t, d)),
            full((t, d)),
            full((d, d)),
            full((1, d)),
            pl.BlockSpec((d, block), lambda j: (0, j)),
            pl.BlockSpec((block, d), lambda j: (j, 0)),
        ],
        out_specs=[
            full((t, d)),
            full((t, d)),
            pl.BlockSpec((t, block), lambda j: (0, j)),
            pl.BlockSpec((t, block), lambda j: (0, j)),
            full((t, d)),
        ],
        out_shape=[
            jax.ShapeDtypeStruct((t, d), F32),
            jax.ShapeDtypeStruct((t, d), BF),
            jax.ShapeDtypeStruct((t, ff), BF),
            jax.ShapeDtypeStruct((t, ff), BF),
            jax.ShapeDtypeStruct((t, d), BF),
        ],
        scratch_shapes=[pltpu.VMEM((t, d), F32)],
        compiler_params=params(),
        cost_estimate=cost(2 * t * d * (2 * ff + d), 4 * d * ff + 4 * t * ff + 12 * t * d, t * ff),
        name="ffn_forward",
    )(res, mixed, wo, gain, w_in, w_out)


def ffn_back_kernel(sourced, *refs):
    if sourced:
        dk, dv, wk, wv, w_in, w_out, slope, mid, gain, pre_grad, g_low, new, low, gain_grad, g, total = refs
    else:
        grad, w_in, w_out, slope, mid, gain, pre_grad, g_low, new, low, gain_grad, g, total = refs
    step = pl.program_id(0)

    @pl.when(step == 0)
    def _():
        if sourced:
            value = nt(dk[...], wk[...]) + nt(dv[...], wv[...])
        else:
            value = grad[...].astype(F32)
        g[...] = value
        g_low[...] = value.astype(BF)
        total[...] = jnp.zeros_like(total)

    block = (nt(g_low[...], w_out[...]) * slope[...].astype(F32)).astype(BF)
    pre_grad[...] = block
    total[...] += nt(block, w_in[...])

    @pl.when(step == pl.num_programs(0) - 1)
    def _():
        back, gain_grad[...] = rms_back(mid[...], gain[...], total[...])
        value = g[...] + back
        new[...] = value
        low[...] = value.astype(BF)


def ffn_back(grads, weights, w_in, w_out, slope, mid, gain, block=512):
    t, d = mid.shape
    ff = w_in.shape[1]
    sourced = weights is not None
    if sourced:
        args = [grads[0], grads[1], weights, weights]
        specs = [
            full((t, d)),
            full((t, d)),
            pl.BlockSpec((None, d, d), lambda j: (1, 0, 0)),
            pl.BlockSpec((None, d, d), lambda j: (2, 0, 0)),
        ]
    else:
        args = [grads]
        specs = [full((t, d))]
    return pl.pallas_call(
        functools.partial(ffn_back_kernel, sourced),
        grid=(ff // block,),
        in_specs=specs
        + [
            pl.BlockSpec((d, block), lambda j: (0, j)),
            pl.BlockSpec((block, d), lambda j: (j, 0)),
            pl.BlockSpec((t, block), lambda j: (0, j)),
            full((t, d)),
            full((1, d)),
        ],
        out_specs=[
            pl.BlockSpec((t, block), lambda j: (0, j)),
            full((t, d)),
            full((t, d)),
            full((t, d)),
            full((1, d)),
        ],
        out_shape=[
            jax.ShapeDtypeStruct((t, ff), BF),
            jax.ShapeDtypeStruct((t, d), BF),
            jax.ShapeDtypeStruct((t, d), F32),
            jax.ShapeDtypeStruct((t, d), BF),
            jax.ShapeDtypeStruct((1, d), F32),
        ],
        scratch_shapes=[pltpu.VMEM((t, d), F32), pltpu.VMEM((t, d), F32)],
        compiler_params=params(),
        cost_estimate=cost(4 * t * d * ff, 4 * d * ff + 4 * t * ff + 16 * t * d),
        name="ffn_back",
    )(*args, w_in, w_out, slope, mid, gain)


def fill_bias(q_seg, k_seg, bias, causal, rows):
    length, width = bias.shape
    for begin in range(0, length, rows):
        allowed = q_seg[begin : begin + rows, :] == k_seg[...]
        if causal:
            at = lax.broadcasted_iota(jnp.int32, (rows, width), 0) + begin
            key = lax.broadcasted_iota(jnp.int32, (rows, width), 1)
            allowed = allowed & (key <= at)
        bias[begin : begin + rows, :] = jnp.where(allowed, 0.0, MASKED)


def join_keys(refs, count, extra, width):
    keys, values, mem_keys, mem_values, all_keys, all_values = refs
    for source, more, target in ((keys, mem_keys, all_keys), (values, mem_values, all_values)):
        target[:count, :] = source[...]
        target[count : count + extra, :] = more[...]


def attend_kernel(extra, causal, rows, *refs):
    if extra:
        q_seg, k_seg, q, k, v, mk, mv, out, logs, bias, ks, vs = refs
    else:
        q_seg, k_seg, q, k, v, out, logs, bias = refs
    length, width = bias.shape
    count = k.shape[0]
    step = pl.program_id(0)

    @pl.when(step == 0)
    def _():
        fill_bias(q_seg, k_seg, bias, causal, rows)
        logs[...] = jnp.zeros_like(logs)
        if extra:
            ks[count:, :] = jnp.zeros((width - count, LANES), BF)
            vs[count:, :] = jnp.zeros((width - count, LANES), BF)

    if extra:
        join_keys((k, v, mk, mv, ks, vs), count, extra, width)
        k, v = ks, vs
    lane = lax.broadcasted_iota(jnp.int32, (rows, LANES), 1)
    for begin in range(0, length, rows):
        here = slice(begin, begin + rows)
        queries = q[here, :] * BF(HD**-0.5)
        sides = []
        kept = logs[here, :]
        for head in range(2):
            mine = (lane < HD) if head == 0 else (lane >= HD)
            scores = nt(jnp.where(mine, queries, BF(0)), k[...]) + bias[here, :]
            top = jnp.max(scores, axis=1, keepdims=True)
            exponent = jnp.exp(scores - top)
            sums = jnp.sum(exponent, axis=1, keepdims=True)
            sides.append(nn(exponent.astype(BF), v[...]) * (1.0 / sums))
            kept = jnp.where(lane == 2 * step + head, top + jnp.log(sums), kept)
        logs[here, :] = kept
        out[here, :] = jnp.where(lane < HD, sides[0], sides[1]).astype(BF)


def part_of(stack, index):
    rows = stack.shape[1]
    return pl.BlockSpec((None, rows, LANES), lambda p: (index, 0, p))


def attend(q, k, v, q_seg, k_seg, memory=None, causal=False, rows=256):
    t, d = q[0].shape[1:]
    count = k[0].shape[1]
    width = k_seg.shape[1]
    args = [q_seg, k_seg, q[0], k[0], v[0]]
    specs = [full(q_seg.shape), full(k_seg.shape), part_of(*q), part_of(*k), part_of(*v)]
    scratch = [pltpu.VMEM((t, width), F32)]
    extra = 0
    if memory is not None:
        extra = memory.shape[1]
        args += [memory, memory]
        specs += [part_of(memory, 0), part_of(memory, 1)]
        scratch += [pltpu.VMEM((width, LANES), BF)] * 2
    return pl.pallas_call(
        functools.partial(attend_kernel, extra, causal, rows),
        grid=(d // LANES,),
        in_specs=specs,
        out_specs=[pl.BlockSpec((t, LANES), lambda p: (0, p)), full((t, LANES))],
        out_shape=[jax.ShapeDtypeStruct((t, d), BF), jax.ShapeDtypeStruct((t, LANES), F32)],
        scratch_shapes=scratch,
        compiler_params=params(),
        cost_estimate=cost(16 * t * width * d, 8 * d * (t + count), t * width * d // HD),
        name="attend",
    )(*args)


def attend_back_kernel(extra, causal, rows, *refs):
    if extra:
        q_seg, k_seg, q, k, v, out, logs, grad, wo, mk, mv = refs[:11]
        dq, dk, dv, dmk, dmv, bias, dks, dvs, ks, vs = refs[11:]
    else:
        q_seg, k_seg, q, k, v, out, logs, grad, wo, dq, dk, dv, bias, dks, dvs = refs
    length, width = bias.shape
    count = k.shape[0]
    step = pl.program_id(0)

    @pl.when(step == 0)
    def _():
        fill_bias(q_seg, k_seg, bias, causal, rows)
        if extra:
            ks[count:, :] = jnp.zeros((width - count, LANES), BF)
            vs[count:, :] = jnp.zeros((width - count, LANES), BF)

    if extra:
        join_keys((k, v, mk, mv, ks, vs), count, extra, width)
        k, v = ks, vs
    lane = lax.broadcasted_iota(jnp.int32, (rows, LANES), 1)
    for begin in range(0, length, rows):
        here = slice(begin, begin + rows)
        queries = q[here, :] * BF(HD**-0.5)
        mixed = nt(grad[here, :], wo[...]).astype(BF)
        product = mixed.astype(F32) * out[here, :].astype(F32)
        kept = logs[here, :]
        sides = []
        for head in range(2):
            mine = (lane < HD) if head == 0 else (lane >= HD)
            own_q = jnp.where(mine, queries, BF(0))
            own_grad = jnp.where(mine, mixed, BF(0))
            log_sum = jnp.sum(jnp.where(lane == 2 * step + head, kept, 0.0), axis=1, keepdims=True)
            center = jnp.sum(jnp.where(mine, product, 0.0), axis=1, keepdims=True)
            probs = jnp.exp(nt(own_q, k[...]) + bias[here, :] - log_sum)
            score_grad = (probs * (nt(own_grad, v[...]) - center)).astype(BF)
            sides.append(nn(score_grad, k[...]))
            value_part = nn(own_grad.T, probs.astype(BF))
            key_part = nn(own_q.T, score_grad)
            if begin == 0 and head == 0:
                dvs[...] = value_part
                dks[...] = key_part
            else:
                dvs[...] += value_part
                dks[...] += key_part
        dq[here, :] = (jnp.where(lane < HD, sides[0], sides[1]) * HD**-0.5).astype(BF)
    dk[...] = dks[:, :count].T.astype(BF)
    dv[...] = dvs[:, :count].T.astype(BF)
    if extra:
        dmk[...] = dks[:, count:].T[:extra].astype(BF)
        dmv[...] = dvs[:, count:].T[:extra].astype(BF)


def attend_back(q, k, v, out, logs, grad, wo, q_seg, k_seg, memory=None, causal=False, rows=256):
    t, d = q[0].shape[1:]
    count = k[0].shape[1]
    width = k_seg.shape[1]
    column = lambda n: pl.BlockSpec((n, LANES), lambda p: (0, p))
    args = [q_seg, k_seg, q[0], k[0], v[0], out, logs, grad, wo]
    specs = [full(q_seg.shape), full(k_seg.shape), part_of(*q), part_of(*k), part_of(*v)]
    specs += [column(t), full((t, LANES)), full((t, d)), pl.BlockSpec((LANES, d), lambda p: (p, 0))]
    scratch = [pltpu.VMEM((t, width), F32)] + [pltpu.VMEM((LANES, width), F32)] * 2
    lengths = [t, count, count]
    extra = 0
    if memory is not None:
        extra = memory.shape[1]
        args += [memory, memory]
        specs += [part_of(memory, 0), part_of(memory, 1)]
        scratch += [pltpu.VMEM((width, LANES), BF)] * 2
        lengths += [extra, extra]
    return pl.pallas_call(
        functools.partial(attend_back_kernel, extra, causal, rows),
        grid=(d // LANES,),
        in_specs=specs,
        out_specs=[column(n) for n in lengths],
        out_shape=[jax.ShapeDtypeStruct((n, d), BF) for n in lengths],
        scratch_shapes=scratch,
        compiler_params=params(),
        cost_estimate=cost(32 * t * width * d, 12 * d * (t + count), t * width * d // HD),
        name="attend_back",
    )(*args)


def share_rows(index, acc, out, shards, size):
    for turn in range(shards):
        shard = index[0] ^ turn
        start = pl.multiple_of(shard * size, 16)
        out[turn] = acc[pl.ds(start, size), :].astype(BF)


def squares_kernel(items, shards, index, *refs):
    out, acc = refs[-2:]
    size = acc.shape[0] // shards
    for j, (a, g) in enumerate(items):

        @pl.when(pl.program_id(0) == j)
        def _(a=a, g=g):
            acc[...] = tn(refs[g][...], refs[a][...])
            share_rows(index, acc, out, shards, size)


def pad_rows(rows):
    return -(-rows // CHUNK) * CHUNK


def square_grads(place, products):
    arrays, items = [], []

    def at(array):
        for i, other in enumerate(arrays):
            if other is array:
                return i
        arrays.append(array)
        return len(arrays) - 1

    for acts, grads in products:
        for grad in grads:
            items.append((at(acts), at(grad)))
    shards = place.sizes["dp"]
    d = products[0][0].shape[1]
    size = d // shards
    work = sum(2 * arrays[a].shape[0] * d * d for a, _ in items)
    return pl.pallas_call(
        functools.partial(squares_kernel, items, shards),
        grid=(len(items),),
        in_specs=[pl.BlockSpec(memory_space=pltpu.SMEM)] + [full(x.shape) for x in arrays],
        out_specs=pl.BlockSpec((shards, size, d), lambda j: (0, j, 0)),
        out_shape=jax.ShapeDtypeStruct((shards, pad_rows(len(items) * size), d), BF),
        scratch_shapes=[pltpu.VMEM((d, d), F32)],
        compiler_params=params(),
        cost_estimate=cost(work, sum(2 * x.size for x in arrays) + 2 * len(items) * d * d),
        name="square_grads",
    )(place.index, *arrays)


def out_kernel(shards, index, acts, grad, out, acc):
    acc[...] = tn(grad[...], acts[...])
    share_rows(index, acc, out, shards, acc.shape[0] // shards)


def ff_out_grads(place, acts, grad):
    shards = place.sizes["dp"]
    t, d = grad.shape
    blocks = acts.shape[1] // d
    size = d // shards
    return pl.pallas_call(
        functools.partial(out_kernel, shards),
        grid=(blocks,),
        in_specs=[
            pl.BlockSpec(memory_space=pltpu.SMEM),
            pl.BlockSpec((t, d), lambda j: (0, j)),
            full((t, d)),
        ],
        out_specs=pl.BlockSpec((shards, size, d), lambda j: (0, j, 0)),
        out_shape=jax.ShapeDtypeStruct((shards, blocks * size, d), BF),
        scratch_shapes=[pltpu.VMEM((d, d), F32)],
        compiler_params=params(),
        cost_estimate=cost(2 * t * d * d * blocks, 2 * (t + d) * d * (blocks + 1)),
        name="ff_out_grads",
    )(place.index, acts, grad)


def in_kernel(per_block, index, grad, acts, out):
    acc = tn(grad[...], acts[...]).astype(BF)
    size = acc.shape[0] // per_block
    for i in range(per_block):
        shard = pl.program_id(0) * per_block + i
        out[index[0] ^ shard] = acc[i * size : (i + 1) * size]


def ff_in_grads(place, acts, grad):
    shards = place.sizes["dp"]
    t, d = acts.shape
    ff = grad.shape[1]
    blocks = ff // d
    size = ff // shards
    return pl.pallas_call(
        functools.partial(in_kernel, d // size),
        grid=(blocks,),
        in_specs=[
            pl.BlockSpec(memory_space=pltpu.SMEM),
            pl.BlockSpec((t, d), lambda j: (0, j)),
            full((t, d)),
        ],
        out_specs=full((shards, size, d)),
        out_shape=jax.ShapeDtypeStruct((shards, size, d), BF),
        compiler_params=params(),
        cost_estimate=cost(2 * t * d * ff, 2 * (t + d) * d * (blocks + 1)),
        name="ff_in_grads",
    )(place.index, grad, acts)


def flip(index, bit):
    return index + bit - 2 * bit * ((index // bit) % 2)


class Place:
    def __init__(self, sizes):
        self.sizes = sizes
        self.dp = lax.axis_index("dp")
        self.row = lax.axis_index("row")
        self.index = self.dp.astype(jnp.int32)[None]

    def swap(self, value, axis, turn):
        return lax.ppermute(value, axis, [(i, i ^ turn) for i in range(self.sizes[axis])])

    def bits(self, axis):
        return [1 << i for i in range(self.sizes[axis].bit_length() - 1)]


QUARTER = 48
CHUNK = 4 * QUARTER
AHEAD = 3
DELAY = 4
FAR_RING = DELAY + 2
Y_RING = DELAY + 4
RING = 5
MESH_ID = pl.DeviceIdType.MESH


def add(left, right):
    return (left.astype(F32) + right.astype(F32)).astype(BF)


class Reducer:
    def __init__(self, groups, counts, row_bits, out, refs):
        self.groups, self.counts, self.out = groups, counts, out
        self.total = sum(counts)
        others = len(row_bits) - 2
        (self.own, self.core_in, self.far, self.near, self.y_in, self.x_in, self.z_in, self.kept) = refs[:8]
        self.w_in = refs[8 : 8 + others]
        sems = list(refs[8 + others :])
        self.load_sem, self.kept_sem, self.core_send, self.core_recv = sems[:4]
        self.core_free, self.send, self.recv, self.free = sems[4], sems[5::3], sems[6::3], sems[7::3]
        row, dp = lax.axis_index("row"), lax.axis_index("dp")
        self.x, self.z = row % 2, (row // 2) % 2
        self.core_peer = (row, flip(dp, 1))
        self.y_peer = (row, flip(dp, 2))
        self.row_peers = [(flip(row, bit), dp) for bit in row_bits]
        self.x_peer, self.z_peer = self.row_peers[:2]
        self.peers = [self.core_peer, self.y_peer] + self.row_peers
        self.stages = [self.y_stage, self.x_stage, self.z_stage]
        self.stages += [functools.partial(self.w_stage, i) for i in range(others)]
        self.stages += [self.back_z_stage, self.back_x_stage]
        self.steps = self.total + DELAY + len(self.stages) - 1

    @staticmethod
    def scratch(row_bits, d):
        others = len(row_bits) - 2
        chunk = (2, 2, QUARTER, d)
        shapes = [
            (AHEAD, 2) + chunk,
            (AHEAD, 2) + chunk,
            (FAR_RING,) + chunk,
            (FAR_RING,) + chunk,
            (Y_RING,) + chunk,
            (RING,) + chunk[1:],
            (RING,) + chunk[2:],
            (RING,) + chunk[2:],
        ] + [(RING,) + chunk[2:]] * others
        dma = pltpu.SemaphoreType.DMA
        regular = pltpu.SemaphoreType.REGULAR
        rings = [Y_RING, RING, RING] + [RING] * others + [RING, RING]
        sems = [dma((AHEAD, 2)), dma((RING,)), dma((AHEAD, 2)), dma((AHEAD, 2)), regular]
        for ring in rings:
            sems += [dma((ring,)), dma((ring,)), regular]
        return [pltpu.VMEM(shape, BF) for shape in shapes] + sems

    def greet(self):
        barrier = pltpu.get_barrier_semaphore()
        for peer in self.peers:
            pl.semaphore_signal(barrier, inc=1, device_id=peer, device_id_type=MESH_ID)
        pl.semaphore_wait(barrier, len(self.peers))

    def start(self):
        for c in range(min(AHEAD, self.total)):
            self.begin(c)

    def step(self, t):
        @pl.when(t < self.total)
        def _():
            self.core_stage(t)

        for i, stage in enumerate(self.stages):
            c = t - DELAY - i

            @pl.when((c >= 0) & (c < self.total))
            def _(c=c, stage=stage):
                stage(c)

        @pl.when(t + AHEAD < self.total)
        def _():
            pl.semaphore_wait(self.core_free, 1)
            self.begin(t + AHEAD)

    def remote(self, stage, ring, c, source, target, peer):
        return pltpu.make_async_remote_copy(
            src_ref=source,
            dst_ref=target,
            send_sem=self.send[stage].at[c % ring],
            recv_sem=self.recv[stage].at[c % ring],
            device_id=peer,
            device_id_type=MESH_ID,
        )

    def give(self, stage, ring, c, peer):
        @pl.when(c + ring < self.total)
        def _():
            pl.semaphore_signal(
                self.free[stage], inc=1, device_id=peer, device_id_type=MESH_ID
            )

    def take(self, stage, ring, c):
        @pl.when(c >= ring)
        def _():
            pl.semaphore_wait(self.free[stage], 1)

    def core_copy(self, c, side, source):
        return pltpu.make_async_remote_copy(
            src_ref=source,
            dst_ref=self.core_in.at[c % AHEAD, side],
            send_sem=self.core_send.at[c % AHEAD, side],
            recv_sem=self.core_recv.at[c % AHEAD, side],
            device_id=self.core_peer,
            device_id_type=MESH_ID,
        )

    def load(self, c, side, source):
        return pltpu.make_async_copy(
            source, self.own.at[c % AHEAD, side], self.load_sem.at[c % AHEAD, side]
        )

    def begin(self, c):
        first = 0
        for group, count in zip(self.groups, self.counts):

            @pl.when((c >= first) & (c < first + count))
            def _(group=group, first=first):
                at = c - first
                for side in range(2):
                    self.core_copy(c, side, group.at[2 * side + 1, at]).start()
                for side in range(2):
                    self.load(c, side, group.at[2 * side, at]).start()

            first += count

    def y_copy(self, c):
        return self.remote(0, Y_RING, c, self.far.at[c % FAR_RING], self.y_in.at[c % Y_RING], self.y_peer)

    def x_copy(self, c):
        source = self.y_in.at[c % Y_RING, 1 - self.x]
        return self.remote(1, RING, c, source, self.x_in.at[c % RING], self.x_peer)

    def z_copy(self, c):
        source = self.x_in.at[c % RING, 1 - self.z]
        return self.remote(2, RING, c, source, self.z_in.at[c % RING], self.z_peer)

    def w_copy(self, i, c):
        source = self.z_in if i == 0 else self.w_in[i - 1]
        return self.remote(
            3 + i, RING, c, source.at[c % RING], self.w_in[i].at[c % RING], self.row_peers[2 + i]
        )

    def back_z_copy(self, c, place):
        at = self.out.at[c, self.x, place]
        return self.remote(3 + len(self.w_in), RING, c, self.kept.at[c % RING], at, self.z_peer)

    def kept_copy(self, c):
        at = self.out.at[c, self.x, self.z]
        return pltpu.make_async_copy(self.kept.at[c % RING], at, self.kept_sem.at[c % RING])

    def back_x_copy(self, c, place):
        at = self.out.at[c, place]
        return self.remote(4 + len(self.w_in), RING, c, at, at, self.x_peer)

    def core_stage(self, c):
        slot, at = c % AHEAD, c % FAR_RING
        for side in range(2):
            self.load(c, side, self.own.at[slot, side]).wait()
            self.core_copy(c, side, self.own.at[slot, side]).wait()
        self.far[at] = add(self.own[slot, 1], self.core_in[slot, 1])
        self.take(0, Y_RING, c)
        self.y_copy(c).start()
        self.near[at] = add(self.own[slot, 0], self.core_in[slot, 0])

        @pl.when(c + AHEAD < self.total)
        def _():
            pl.semaphore_signal(
                self.core_free, inc=1, device_id=self.core_peer, device_id_type=MESH_ID
            )

    def y_stage(self, c):
        self.y_copy(c).wait()
        slot = c % Y_RING
        self.y_in[slot] = add(self.y_in[slot], self.near[c % FAR_RING])
        self.take(1, RING, c)
        self.x_copy(c).start()

    def x_stage(self, c):
        self.x_copy(c).wait()
        slot = c % RING
        self.x_in[slot] = add(self.x_in[slot], self.y_in[c % Y_RING, self.x])
        self.give(0, Y_RING, c, self.y_peer)
        self.take(2, RING, c)
        self.z_copy(c).start()

    def z_stage(self, c):
        self.z_copy(c).wait()
        slot = c % RING
        self.z_in[slot] = add(self.z_in[slot], self.x_in[slot, self.z])
        self.give(1, RING, c, self.x_peer)
        self.take(3, RING, c)
        self.w_copy(0, c).start()

    def w_stage(self, i, c):
        self.w_copy(i, c).wait()
        slot = c % RING
        source = self.z_in if i == 0 else self.w_in[i - 1]
        value = add(self.w_in[i][slot], source[slot])
        giver = self.z_peer if i == 0 else self.row_peers[1 + i]
        self.give(2 + i, RING, c, giver)
        if i + 1 < len(self.w_in):
            self.w_in[i][slot] = value
            self.take(4 + i, RING, c)
            self.w_copy(i + 1, c).start()
        else:
            self.kept[slot] = value
            self.give(3 + i, RING, c, self.row_peers[2 + i])
            self.kept_copy(c).start()
            self.back_z_copy(c, self.z).start()

    def back_z_stage(self, c):
        self.kept_copy(c).wait()
        self.back_z_copy(c, self.z).wait_send()
        self.back_z_copy(c, 1 - self.z).wait_recv()
        self.back_x_copy(c, self.x).start()

    def back_x_stage(self, c):
        self.back_x_copy(c, self.x).wait_send()
        self.back_x_copy(c, 1 - self.x).wait_recv()


def reduce_kernel(counts, row_bits, *refs):
    count = len(counts)
    reducer = Reducer(refs[:count], counts, row_bits, refs[count], refs[count + 1 :])
    reducer.greet()
    reducer.start()

    def step(t, carry):
        reducer.step(t)
        return carry

    lax.fori_loop(0, reducer.steps, step, 0)


def chunk_view(group):
    turns, rows, d = group.shape
    return group.reshape(turns, rows // CHUNK, 2, 2, QUARTER, d)


def split_sums(result, counts):
    d = result.shape[-1]
    sums, first = [], 0
    for n in counts:
        sums.append(result[first : first + n].reshape(n * CHUNK, d))
        first += n
    return sums


def reduce_all(place, groups):
    d = groups[0].shape[-1]
    counts = [g.shape[1] // CHUNK for g in groups]
    row_bits = place.bits("row")
    result = pl.pallas_call(
        functools.partial(reduce_kernel, counts, row_bits),
        in_specs=[pl.BlockSpec(memory_space=pl.ANY)] * len(groups),
        out_specs=pl.BlockSpec(memory_space=pl.ANY),
        out_shape=jax.ShapeDtypeStruct((sum(counts), 2, 2, QUARTER, d), BF),
        scratch_shapes=Reducer.scratch(row_bits, d),
        compiler_params=pltpu.CompilerParams(
            collective_id=0, has_side_effects=True, vmem_limit_bytes=48 * 2**20
        ),
        cost_estimate=cost(0, 4 * sum(counts) * CHUNK * d),
        name="reduce_all",
    )(*[chunk_view(g) for g in groups])
    return split_sums(result, counts)


def xor(left, right, bits):
    total = 0
    for bit in bits:
        a, b = (left // bit) % 2, (right // bit) % 2
        total = total + bit * (a + b - 2 * a * b)
    return total


TILE = 256
HALF = 2 * CHUNK


def encoder_back_kernel(counts, row_bits, memories, *refs):
    given = len(counts)
    (q_seg, k_seg, dck, dcv, cross, mid, tokens, dec_gain_grads, gain0, gain1) = refs[:10]
    (w_in, w_out, slope, hidden, mid_low, q, k, v, mk, mv, mixed, logs, wo, enc_low, fetched, w_qkv) = refs[10:26]
    groups, refs = refs[26 : 26 + given], refs[26 + given :]
    out, ff_out_part, ff_in_part, squares_part, token_grad, gain_sums = refs[:6]
    (g, total, acc, low, g_low, pg, dq, dk, dv, dmk, dmv, bias, ks, vs, dks, dvs) = refs[6:22]
    (stage_a, stage_b, gain_acc, gain_in, copy_sem, gain_send, gain_recv) = refs[22:29]
    parts = [ff_out_part, ff_in_part, squares_part]
    all_counts = list(counts) + [part.shape[1] for part in parts]
    reducer = Reducer(list(groups) + parts, all_counts, row_bits, out, refs[29:])
    me = lax.axis_index("dp")
    t = pl.program_id(0)
    length = g.shape[0]
    count = k.shape[0]
    width = bias.shape[1]
    blocks = ff_out_part.shape[1]
    pairs = g.shape[1] // LANES
    A0 = blocks
    S0 = A0 + pairs
    P0 = S0 + 6
    END = P0 + 3
    tiles = [slice(b, b + TILE) for b in range(0, length, TILE)]

    def fetch(source, target, i):
        return pltpu.make_async_copy(source, target, copy_sem.at[i])

    def early():
        return [
            fetch(dck, dq, 0),
            fetch(dcv, dk, 1),
            fetch(cross.at[1], dv, 2),
            fetch(cross.at[2], pg, 3),
            fetch(mid, token_grad, 4),
        ]

    def late():
        return fetch(tokens, pg, 3)

    def shares():
        for turn in range(4):
            shard = xor(me, turn, (1, 2))
            for i in range(4):
                start = pl.multiple_of(shard * CHUNK + i * QUARTER, 16)
                stage_a[turn, i // 2, i % 2] = acc[pl.ds(start, QUARTER), :].astype(BF)

    def copy_ff_out():
        return fetch(stage_a, ff_out_part.at[:, t], 5)

    def copy_ff_in():
        return fetch(stage_b, ff_in_part.at[xor(me, t, (1, 2))], 6)

    def copy_squares():
        return fetch(stage_a, squares_part.at[:, t - S0], 5)

    @pl.when(t == 0)
    def _():
        for copy in early():
            copy.start()
        reducer.greet()
        reducer.start()
        fill_bias(q_seg, k_seg, bias, False, TILE)
        ks[count:, :] = jnp.zeros((width - count, LANES), BF)
        vs[count:, :] = jnp.zeros((width - count, LANES), BF)
        gain_acc[0] = dec_gain_grads[...]
        for copy in early():
            copy.wait()
        for here in tiles:
            value = nt(dq[here, :], dv[...]) + nt(dk[here, :], pg[...])
            g[here, :] = value
            g_low[here, :] = value.astype(BF)
            total[here, :] = jnp.zeros_like(value)

    @pl.when(t < A0)
    def _():
        for here in tiles:
            block = (nt(g_low[here, :], w_out[...]) * slope[here, :].astype(F32)).astype(BF)
            pg[here, :] = block
            total[here, :] += nt(block, w_in[...])
        for n in range(0, acc.shape[0], HALF):
            acc[n : n + HALF, :] = tn(g_low[:, n : n + HALF], hidden[...])
        shares()
        copy_ff_out().start()
        for n in range(0, pg.shape[1], HALF):
            value = tn(pg[:, n : n + HALF], mid_low[...])
            for i in range(8):
                stage_b[n // CHUNK + i // 4, (i // 2) % 2, i % 2] = value[
                    i * QUARTER : (i + 1) * QUARTER, :
                ].astype(BF)
        copy_ff_in().start()

    @pl.when(t == A0 - 1)
    def _():
        gain_sum = jnp.zeros((1, g.shape[1]), F32)
        for here in tiles:
            back, gain_part = rms_back(token_grad[here, :], gain1[...], total[here, :])
            gain_sum = gain_sum + gain_part
            value = g[here, :] + back
            g[here, :] = value
            low[here, :] = value.astype(BF)
        gain_acc[0, 1:2, :] = gain_sum

    @pl.when((t >= A0) & (t < S0))
    def _():
        pair = t - A0
        lanes = pl.ds(pl.multiple_of(pair * LANES, LANES), LANES)
        join_keys((k, v, mk, mv, ks, vs), count, memories, width)
        lane = lax.broadcasted_iota(jnp.int32, (TILE, LANES), 1)
        for number, here in enumerate(tiles):
            queries = q[here, :] * BF(HD**-0.5)
            grads = nt(low[here, :], wo[...]).astype(BF)
            product = grads.astype(F32) * mixed[here, lanes].astype(F32)
            kept = logs[here, :]
            sides = []
            for head in range(2):
                mine = (lane < HD) if head == 0 else (lane >= HD)
                own_q = jnp.where(mine, queries, BF(0))
                own_grad = jnp.where(mine, grads, BF(0))
                chosen = lane == 2 * pair + head
                log_sum = jnp.sum(jnp.where(chosen, kept, 0.0), axis=1, keepdims=True)
                center = jnp.sum(jnp.where(mine, product, 0.0), axis=1, keepdims=True)
                probs = jnp.exp(nt(own_q, ks[...]) + bias[here, :] - log_sum)
                score_grad = (probs * (nt(own_grad, vs[...]) - center)).astype(BF)
                sides.append(nn(score_grad, ks[...]))
                value_part = nn(own_grad.T, probs.astype(BF))
                key_part = nn(own_q.T, score_grad)
                if number == 0 and head == 0:
                    dvs[...] = value_part
                    dks[...] = key_part
                else:
                    dvs[...] += value_part
                    dks[...] += key_part
            dq[here, lanes] = (jnp.where(lane < HD, sides[0], sides[1]) * HD**-0.5).astype(BF)
        dk[:, lanes] = dks[:, :count].T.astype(BF)
        dv[:, lanes] = dvs[:, :count].T.astype(BF)
        dmk[:, lanes] = dks[:, count:].T[:memories].astype(BF)
        dmv[:, lanes] = dvs[:, count:].T[:memories].astype(BF)

    items = [(enc_low, dq), (enc_low, dk), (enc_low, dv), (mixed, low), (fetched, dmk), (fetched, dmv)]
    for j, (acts, grads) in enumerate(items):

        @pl.when(t == S0 + j)
        def _(acts=acts, grads=grads):
            for n in range(0, acc.shape[0], HALF):
                acc[n : n + HALF, :] = tn(grads[:, n : n + HALF], acts[...])
            shares()
            copy_squares().start()

    for j, grads in enumerate((dq, dk, dv)):

        @pl.when(t == P0 + j)
        def _(j=j, grads=grads):
            if j == 0:
                late().start()
            for here in tiles:
                value = nt(grads[here, :], w_qkv[...])
                total[here, :] = value if j == 0 else total[here, :] + value

    @pl.when(t == END - 1)
    def _():
        late().wait()
        gain_sum = jnp.zeros((1, g.shape[1]), F32)
        for here in tiles:
            back, gain_part = rms_back(pg[here, :].astype(F32), gain0[...], total[here, :])
            gain_sum = gain_sum + gain_part
            token_grad[here, :] = g[here, :] + back
        gain_acc[0, 0:1, :] = gain_sum

    reducer.step(t)

    @pl.when(t < A0)
    def _():
        copy_ff_out().wait()
        copy_ff_in().wait()

    @pl.when((t >= S0) & (t < P0))
    def _():
        copy_squares().wait()

    def gain_copy(i):
        return pltpu.make_async_remote_copy(
            src_ref=gain_acc.at[i],
            dst_ref=gain_in.at[i],
            send_sem=gain_send.at[i],
            recv_sem=gain_recv.at[i],
            device_id=reducer.peers[i],
            device_id_type=MESH_ID,
        )

    last = len(reducer.peers)
    for i in range(last + 1):

        @pl.when(t == END + i)
        def _(i=i):
            if i:
                gain_copy(i - 1).wait()
                value = gain_acc[i - 1] + gain_in[i - 1]
                if i < last:
                    gain_acc[i] = value
                else:
                    gain_sums[...] = value
            if i < last:
                gain_copy(i).start()


def encoder_back(
    place, groups, q_seg, k_seg, dck, dcv, cross, mid, tokens, dec_gain_grads, gains,
    w_in, w_out, slope, hidden, mid_low, qkv, memory, mixed, logs, wo, enc_low, fetched, w_qkv,
):
    t, d = tokens.shape
    ff = w_in.shape[1]
    blocks, pairs, memories = ff // d, d // LANES, fetched.shape[0]
    width = k_seg.shape[1]
    row_bits = place.bits("row")
    counts = [g.shape[1] // CHUNK for g in groups]
    new = [blocks, ff // (4 * CHUNK), 6]
    total = sum(counts) + sum(new)
    A0 = blocks
    P0 = A0 + pairs + 6
    steps = max(total + DELAY + len(row_bits) + 2, P0 + 6 + len(row_bits))

    def phase(first, size):
        return lambda s: jnp.minimum(jnp.maximum(s - first, 0), size - 1)

    f_at, a_at, p_at = phase(0, blocks), phase(A0, pairs), phase(P0, 3)
    anywhere = pl.BlockSpec(memory_space=pl.ANY)
    once = lambda shape: pl.BlockSpec(shape, lambda s: (0,) * len(shape), pipeline_mode=pl.Buffered(1))
    column = lambda i: pl.BlockSpec((None, t, LANES), lambda s: (i, 0, a_at(s)))
    in_specs = [
        once((t, 1)), once((1, width)), anywhere, anywhere, anywhere, anywhere, anywhere,
        once((8, d)), once((1, d)), once((1, d)),
        pl.BlockSpec((d, d), lambda s: (0, f_at(s))),
        pl.BlockSpec((d, d), lambda s: (f_at(s), 0)),
        pl.BlockSpec((t, d), lambda s: (0, f_at(s))),
        pl.BlockSpec((t, d), lambda s: (0, f_at(s))),
        once((t, d)),
        column(0), column(1), column(2),
        pl.BlockSpec((None, memories, LANES), lambda s: (0, 0, a_at(s))),
        pl.BlockSpec((None, memories, LANES), lambda s: (1, 0, a_at(s))),
        once((t, d)), once((t, LANES)),
        pl.BlockSpec((LANES, d), lambda s: (a_at(s), 0)),
        once((t, d)), once((memories, d)),
        pl.BlockSpec((None, d, d), lambda s: (p_at(s), 0, 0)),
    ] + [anywhere] * len(groups)
    chunk = (2, 2, QUARTER, d)
    part = lambda n: jax.ShapeDtypeStruct((4, n) + chunk, BF)
    out_shape = [
        jax.ShapeDtypeStruct((total,) + chunk, BF),
        part(new[0]), part(new[1]), part(new[2]),
        jax.ShapeDtypeStruct((t, d), F32),
        jax.ShapeDtypeStruct((8, d), F32),
    ]
    square = lambda kind: pltpu.VMEM((t, d), kind)
    exchanges = 2 + len(row_bits)
    scratch = (
        [square(F32), square(F32), pltpu.VMEM((d, d), F32)]
        + [square(BF)] * 6
        + [pltpu.VMEM((memories, d), BF)] * 2
        + [pltpu.VMEM((t, width), F32)]
        + [pltpu.VMEM((width, LANES), BF)] * 2
        + [pltpu.VMEM((LANES, width), F32)] * 2
        + [pltpu.VMEM((4,) + chunk, BF), pltpu.VMEM((4,) + chunk, BF)]
        + [pltpu.VMEM((exchanges, 8, d), F32)] * 2
        + [pltpu.SemaphoreType.DMA((7,))]
        + [pltpu.SemaphoreType.DMA((exchanges,))] * 2
        + Reducer.scratch(row_bits, d)
    )
    result, _, _, _, token_grad, gain_sums = pl.pallas_call(
        functools.partial(encoder_back_kernel, counts, row_bits, memories),
        grid=(steps,),
        in_specs=in_specs,
        out_specs=[anywhere] * 4 + [once((t, d)), once((8, d))],
        out_shape=out_shape,
        scratch_shapes=scratch,
        compiler_params=pltpu.CompilerParams(
            collective_id=1, has_side_effects=True, vmem_limit_bytes=60 * 2**20
        ),
        cost_estimate=cost(2 * t * d * (4 * ff + 14 * d), 30 * total * CHUNK * d),
        name="encoder_back",
    )(
        q_seg, k_seg, dck, dcv, cross, mid, tokens, dec_gain_grads, gains[0], gains[1],
        w_in, w_out, slope, hidden, mid_low, qkv, qkv, qkv, memory, memory, mixed, logs, wo,
        enc_low, fetched, w_qkv, *[chunk_view(g) for g in groups],
    )
    return split_sums(result, counts + new), token_grad, gain_sums


def fold_outer(place, value):
    while value.shape[0] > 4:
        half = value.shape[0] // 2
        value = add(value[:half], place.swap(value[half:], "dp", half))
    return value


def gain_group(place, gains):
    shards = place.sizes["dp"]
    count, d = gains.shape
    parts = gains.reshape(count, shards, -1)
    turned = jnp.stack(
        [lax.dynamic_index_in_dim(parts, place.dp ^ turn, 1, False) for turn in range(shards)]
    )
    return jnp.pad(turned.astype(BF), ((0, 0), (0, CHUNK - count), (0, d - parts.shape[2])))


def weights_of(value, count, size):
    value = value[: count * size].reshape(count, size, -1)
    return jnp.swapaxes(value, 1, 2).astype(F32)


def encoder_back_apart(
    place, groups, q_seg, k_seg, dck, dcv, cross, mid, tokens, dec_gain_grads, gains,
    w_in, w_out, slope, hidden, mid_low, qkv, memory, mixed, logs, wo, enc_low, fetched, w_qkv,
):
    pre_grad, grad_low, new, low, mid_gain_grad = ffn_back(
        (dck, dcv), cross, w_in, w_out, slope, mid, gains[1]
    )
    dq, dk, dv, dmk, dmv = attend_back(
        (qkv, 0), (qkv, 1), (qkv, 2), mixed, logs, low, wo, q_seg, k_seg, memory
    )
    parts = [
        ff_out_grads(place, hidden, grad_low),
        ff_in_grads(place, mid_low, pre_grad),
        square_grads(place, [(enc_low, [dq, dk, dv]), (mixed, [low]), (fetched, [dmk, dmv])]),
    ]
    token_grad, _, enc_gain_grad = proj_back(tokens, gains[0], new, w_qkv, [dq, dk, dv])
    gain_part = gain_group(
        place, jnp.concatenate([enc_gain_grad, mid_gain_grad] + dec_gain_grads)
    )
    parts = [fold_outer(place, part) for part in groups + parts + [gain_part]]
    sums = reduce_all(place, parts)
    size = tokens.shape[1] // place.sizes["dp"]
    return sums, token_grad, sums[-1][:5, :size].astype(F32)


def fetch_memory(place, table, ids):
    rows = table.shape[0]
    others = range(1, place.sizes["dp"])
    wanted = [ids] + [place.swap(ids, "dp", turn) for turn in others]
    local = jnp.concatenate(wanted) - place.dp * rows
    chosen = (local[:, None] == jnp.arange(rows)[None, :]).astype(BF)
    picked = nn(chosen, table).astype(BF).reshape(len(wanted), ids.shape[0], -1)
    result = picked[0]
    for turn in others:
        result = result + place.swap(picked[turn], "dp", turn)
    return result


def on_device(
    sizes,
    enc_input,
    dec_input,
    memory_table,
    memory_ids,
    enc_segments,
    dec_segments,
    enc_qkv,
    enc_attn_out,
    mem_proj,
    enc_gains,
    enc_ff_in,
    enc_ff_out,
    dec_qkv,
    dec_self_out,
    dec_cross,
    dec_cross_out,
    dec_gains,
    dec_ff_in,
    dec_ff_out,
    out_grad,
):
    place = Place(sizes)
    tokens, answers = enc_input[0], dec_input[0]
    fetched = fetch_memory(place, memory_table, memory_ids.reshape(-1))
    memories = fetched.shape[0]
    enc_gain = enc_gains.astype(F32)[:, None]
    dec_gain = dec_gains.astype(F32)[:, None]

    enc_at, dec_at = enc_segments[0], dec_segments[0]
    enc_q_seg, dec_q_seg = enc_at[:, None], dec_at[:, None]
    owner = jnp.arange(memories, dtype=jnp.int32) // TOPK
    padding = jnp.full((-memories % LANES,), -1, jnp.int32)
    all_k_seg = jnp.concatenate([enc_at, owner, padding])[None]
    enc_k_seg, dec_k_seg = enc_at[None], dec_at[None]

    self_low, self_proj = project(answers, dec_gain[0], dec_qkv, 0, 3)
    self_q, self_k, self_v = [(self_proj, j) for j in range(3)]
    self_mixed, self_logs = attend(self_q, self_k, self_v, dec_q_seg, dec_k_seg, causal=True)
    first, cross_low, cross_q = project(
        answers, dec_gain[1], dec_cross, 0, 1, self_mixed, dec_self_out
    )
    cross_q = (cross_q, 0)

    enc_low, enc_proj = project(tokens, enc_gain[0], enc_qkv, 0, 3)
    enc_q, enc_k, enc_v = [(enc_proj, j) for j in range(3)]
    memory = project_plain(fetched, mem_proj, 0, 2)
    enc_mixed, enc_logs = attend(enc_q, enc_k, enc_v, enc_q_seg, all_k_seg, memory)
    middle, mid_low, enc_hidden, enc_slope, encoded = ffn_forward(
        tokens, enc_mixed, enc_attn_out, enc_gain[1], enc_ff_in, enc_ff_out
    )
    pairs = project_plain(encoded, dec_cross, 1, 2)
    cross_k, cross_v = (pairs, 0), (pairs, 1)
    cross_mixed, cross_logs = attend(cross_q, cross_k, cross_v, dec_q_seg, enc_k_seg)
    second, ffn_low, dec_hidden, dec_slope, final = ffn_forward(
        first, cross_mixed, dec_cross_out, dec_gain[2], dec_ff_in, dec_ff_out
    )

    grad = out_grad[0]
    dec_ff_out_part = ff_out_grads(place, dec_hidden, grad)
    pre_grad, _, new, low, ffn_gain_grad = ffn_back(
        grad, None, dec_ff_in, dec_ff_out, dec_slope, second, dec_gain[2]
    )
    dec_ff_in_part = ff_in_grads(place, ffn_low, pre_grad)
    dcq, dck, dcv = attend_back(
        cross_q, cross_k, cross_v, cross_mixed, cross_logs, low, dec_cross_out,
        dec_q_seg, enc_k_seg,
    )
    cross_part = square_grads(
        place, [(cross_mixed, [low]), (cross_low, [dcq]), (encoded, [dck, dcv])]
    )

    new, low, cross_gain_grad = proj_back(first, dec_gain[1], new, dec_cross, [dcq])
    dsq, dsk, dsv = attend_back(
        self_q, self_k, self_v, self_mixed, self_logs, low, dec_self_out,
        dec_q_seg, dec_k_seg, causal=True,
    )
    self_part = square_grads(place, [(self_low, [dsq, dsk, dsv]), (self_mixed, [low])])
    answer_grad, _, self_gain_grad = proj_back(answers, dec_gain[0], new, dec_qkv, [dsq, dsk, dsv])

    dec_gain_grads = [self_gain_grad, cross_gain_grad, ffn_gain_grad]
    dec_parts = [dec_ff_out_part, dec_ff_in_part, cross_part, self_part]
    if sizes["dp"] == 4:
        blank = jnp.zeros((1, tokens.shape[1]), F32)
        sums, token_grad, gain_sums = encoder_back(
            place, dec_parts, enc_q_seg, all_k_seg, dck, dcv, dec_cross, middle, tokens,
            jnp.concatenate([blank, blank] + dec_gain_grads + [blank] * 3), enc_gain,
            enc_ff_in, enc_ff_out, enc_slope, enc_hidden, mid_low, enc_proj, memory, enc_mixed,
            enc_logs, enc_attn_out, enc_low, fetched, enc_qkv,
        )
        share = tokens.shape[1] // 4
        gains = lax.dynamic_slice_in_dim(gain_sums[:5], place.dp * share, share, 1)
    else:
        sums, token_grad, gains = encoder_back_apart(
            place, dec_parts, enc_q_seg, all_k_seg, dck, dcv, dec_cross, middle, tokens,
            dec_gain_grads, enc_gain, enc_ff_in, enc_ff_out, enc_slope, enc_hidden, mid_low,
            enc_proj, memory, enc_mixed, enc_logs, enc_attn_out, enc_low, fetched, enc_qkv,
        )
    size = tokens.shape[1] // sizes["dp"]
    blocks = enc_ff_in.shape[1] // tokens.shape[1]
    ff_size = enc_ff_in.shape[1] // sizes["dp"]
    enc_squares = weights_of(sums[6], 6, size)
    self_squares = weights_of(sums[3], 4, size)
    cross_squares = weights_of(sums[2], 4, size)
    return (
        final[None],
        token_grad[None],
        answer_grad[None],
        enc_squares[0:3],
        enc_squares[3],
        enc_squares[4:6],
        gains[0:2],
        weights_of(sums[5], 1, ff_size)[0],
        weights_of(sums[4], blocks, size).reshape(-1, size),
        self_squares[0:3],
        self_squares[3],
        cross_squares[1:4],
        cross_squares[0],
        gains[2:4],
        weights_of(sums[1], 1, ff_size)[0],
        weights_of(sums[0], blocks, size).reshape(-1, size),
        gains[4],
    )


def solution(mesh):
    rows = P(("row", "dp"), None, None)
    in_specs = (
        (rows, rows, P("dp", None), rows, P(("row", "dp"), None), P(("row", "dp"), None))
        + (P(),) * 13
        + (rows,)
    )
    cube, flat = P(None, None, "dp"), P(None, "dp")
    out_specs = (
        (rows, rows, rows)
        + (cube, flat, cube, flat, flat, flat)
        + (cube, flat, cube, flat, flat, flat, flat)
        + (P("dp"),)
    )
    return jax.shard_map(
        functools.partial(on_device, dict(mesh.shape)),
        mesh=mesh,
        in_specs=in_specs,
        out_specs=out_specs,
        check_vma=False,
    )
```

```python
import functools

import jax
import jax.numpy as jnp
from jax import lax
from jax.experimental import pallas as pl
from jax.experimental.pallas import tpu as pltpu
from jax.sharding import PartitionSpec as P

HD = 64
TOPK = 10
LANES = 128
MASKED = -1e30
BF = jnp.bfloat16
F32 = jnp.float32


def nn(left, right):
    return lax.dot_general(left, right, (((1,), (0,)), ((), ())), preferred_element_type=F32)


def nt(left, right):
    return lax.dot_general(left, right, (((1,), (1,)), ((), ())), preferred_element_type=F32)


def tn(left, right):
    return lax.dot_general(left, right, (((0,), (0,)), ((), ())), preferred_element_type=F32)


def full(shape):
    return pl.BlockSpec(shape, lambda *_: (0,) * len(shape))


def params(mib=16):
    return pltpu.CompilerParams(vmem_limit_bytes=mib * 2**20)


def cost(flops, nbytes, exps=0):
    return pl.CostEstimate(flops=int(flops), bytes_accessed=int(nbytes), transcendentals=int(exps))


def rms_scale(x):
    return lax.rsqrt(jnp.mean(x * x, axis=-1, keepdims=True) + 1e-06)


def rms_back(x, gain, dy):
    scale = rms_scale(x)
    gain_grad = jnp.sum(dy * x * scale, axis=0, keepdims=True)
    inner = dy * gain
    mixed = jnp.mean(inner * x, axis=-1, keepdims=True)
    return scale * (inner - x * (scale * scale) * mixed), gain_grad


def proj_kernel(residual, x, gain, *refs):
    if residual:
        mixed, wo, w, mid, low, out = refs
    else:
        w, low, out = refs

    @pl.when(pl.program_id(0) == 0)
    def _():
        value = x[...].astype(F32)
        if residual:
            value = value + nn(mixed[...], wo[...])
            mid[...] = value
        low[...] = (value * rms_scale(value) * gain[...]).astype(BF)

    out[...] = nn(low[...], w[...]).astype(BF)


def project(x, gain, w, first, count, mixed=None, wo=None):
    t, d = x.shape
    residual = mixed is not None
    args = [x, gain]
    specs = [full((t, d)), full((1, d))]
    outs = [jax.ShapeDtypeStruct((t, d), BF), jax.ShapeDtypeStruct((count, t, d), BF)]
    out_specs = [full((t, d)), pl.BlockSpec((None, t, d), lambda j: (j, 0, 0))]
    if residual:
        args += [mixed, wo]
        specs += [full((t, d)), full((d, d))]
        outs = [jax.ShapeDtypeStruct((t, d), F32)] + outs
        out_specs = [full((t, d))] + out_specs
    args.append(w)
    specs.append(pl.BlockSpec((None, d, d), lambda j: (first + j, 0, 0)))
    return pl.pallas_call(
        functools.partial(proj_kernel, residual),
        grid=(count,),
        in_specs=specs,
        out_specs=out_specs,
        out_shape=outs,
        compiler_params=params(),
        cost_estimate=cost(2 * t * d * d * (count + residual), 2 * d * (t + d) * (count + 2)),
        name="project",
    )(*args)


def pairs_kernel(x, w, out):
    out[...] = nn(x[...], w[...]).astype(BF)


def project_plain(x, w, first, count):
    t, d = x.shape
    return pl.pallas_call(
        pairs_kernel,
        grid=(count,),
        in_specs=[full((t, d)), pl.BlockSpec((None, d, d), lambda j: (first + j, 0, 0))],
        out_specs=pl.BlockSpec((None, t, d), lambda j: (j, 0, 0)),
        out_shape=jax.ShapeDtypeStruct((count, t, d), BF),
        compiler_params=params(),
        cost_estimate=cost(2 * t * d * d * count, 2 * d * (t + d) * count),
        name="project_plain",
    )(x, w)


def proj_back_kernel(count, x, gain, grad, w, *refs):
    parts = refs[:count]
    new, low, gain_grad, total = refs[count:]
    step = pl.program_id(0)
    for j in range(count):

        @pl.when(step == j)
        def _(j=j):
            value = nt(parts[j][...], w[...])
            total[...] = value if j == 0 else total[...] + value

    @pl.when(step == count - 1)
    def _():
        back, gain_grad[...] = rms_back(x[...].astype(F32), gain[...], total[...])
        value = grad[...] + back
        new[...] = value
        low[...] = value.astype(BF)


def proj_back(x, gain, grad, w, parts):
    t, d = x.shape
    count = len(parts)
    return pl.pallas_call(
        functools.partial(proj_back_kernel, count),
        grid=(count,),
        in_specs=[full((t, d)), full((1, d)), full((t, d))]
        + [pl.BlockSpec((None, d, d), lambda j: (j, 0, 0))]
        + [full((t, d))] * count,
        out_specs=[full((t, d)), full((t, d)), full((1, d))],
        out_shape=[
            jax.ShapeDtypeStruct((t, d), F32),
            jax.ShapeDtypeStruct((t, d), BF),
            jax.ShapeDtypeStruct((1, d), F32),
        ],
        scratch_shapes=[pltpu.VMEM((t, d), F32)],
        compiler_params=params(),
        cost_estimate=cost(2 * t * d * d * count, 2 * d * (t + d) * count + 12 * t * d),
        name="proj_back",
    )(x, gain, grad, w, *parts)


GELU_A = 0.7978845608028654
GELU_B = 0.044715


def gelu_parts(pre):
    square = pre * pre
    half = 0.5 + 0.5 * jnp.tanh(pre * (GELU_A + (GELU_A * GELU_B) * square))
    act = pre * half
    slope = half + (act * (1.0 - half)) * (2 * GELU_A + (6 * GELU_A * GELU_B) * square)
    return act.astype(BF), slope.astype(BF)


def tiles_of(length):
    size = min(length, 256)
    return [slice(begin, begin + size) for begin in range(0, length, size)]


def ffn_kernel(res, mixed, wo, gain, w_in, w_out, mid, low, hidden, slope, out, total):
    step = pl.program_id(0)
    tiles = tiles_of(res.shape[0])

    @pl.when(step == 0)
    def _():
        for here in tiles:
            value = res[here, :].astype(F32) + nn(mixed[here, :], wo[...])
            mid[here, :] = value
            low[here, :] = (value * rms_scale(value) * gain[...]).astype(BF)
            total[here, :] = value

    for here in tiles:
        act, slope[here, :] = gelu_parts(nn(low[here, :], w_in[...]))
        hidden[here, :] = act
        total[here, :] += nn(act, w_out[...])

    @pl.when(step == pl.num_programs(0) - 1)
    def _():
        for here in tiles:
            out[here, :] = total[here, :].astype(BF)


def ffn_forward(res, mixed, wo, gain, w_in, w_out, block=768):
    t, d = res.shape
    ff = w_in.shape[1]
    return pl.pallas_call(
        ffn_kernel,
        grid=(ff // block,),
        in_specs=[
            full((t, d)),
            full((t, d)),
            full((d, d)),
            full((1, d)),
            pl.BlockSpec((d, block), lambda j: (0, j)),
            pl.BlockSpec((block, d), lambda j: (j, 0)),
        ],
        out_specs=[
            full((t, d)),
            full((t, d)),
            pl.BlockSpec((t, block), lambda j: (0, j)),
            pl.BlockSpec((t, block), lambda j: (0, j)),
            full((t, d)),
        ],
        out_shape=[
            jax.ShapeDtypeStruct((t, d), F32),
            jax.ShapeDtypeStruct((t, d), BF),
            jax.ShapeDtypeStruct((t, ff), BF),
            jax.ShapeDtypeStruct((t, ff), BF),
            jax.ShapeDtypeStruct((t, d), BF),
        ],
        scratch_shapes=[pltpu.VMEM((t, d), F32)],
        compiler_params=params(28),
        cost_estimate=cost(2 * t * d * (2 * ff + d), 4 * d * ff + 4 * t * ff + 12 * t * d, t * ff),
        name="ffn_forward",
    )(res, mixed, wo, gain, w_in, w_out)


def ffn_back_kernel(sourced, *refs):
    if sourced:
        dk, dv, wk, wv, w_in, w_out, slope, mid, gain, pre_grad, g_low, new, low, gain_grad, g, total = refs
    else:
        grad, w_in, w_out, slope, mid, gain, pre_grad, g_low, new, low, gain_grad, g, total = refs
    step = pl.program_id(0)

    @pl.when(step == 0)
    def _():
        if sourced:
            value = nt(dk[...], wk[...]) + nt(dv[...], wv[...])
        else:
            value = grad[...].astype(F32)
        g[...] = value
        g_low[...] = value.astype(BF)
        total[...] = jnp.zeros_like(total)

    block = (nt(g_low[...], w_out[...]) * slope[...].astype(F32)).astype(BF)
    pre_grad[...] = block
    total[...] += nt(block, w_in[...])

    @pl.when(step == pl.num_programs(0) - 1)
    def _():
        back, gain_grad[...] = rms_back(mid[...], gain[...], total[...])
        value = g[...] + back
        new[...] = value
        low[...] = value.astype(BF)


def ffn_back(grads, weights, w_in, w_out, slope, mid, gain, block=512):
    t, d = mid.shape
    ff = w_in.shape[1]
    sourced = weights is not None
    if sourced:
        args = [grads[0], grads[1], weights, weights]
        specs = [
            full((t, d)),
            full((t, d)),
            pl.BlockSpec((None, d, d), lambda j: (1, 0, 0)),
            pl.BlockSpec((None, d, d), lambda j: (2, 0, 0)),
        ]
    else:
        args = [grads]
        specs = [full((t, d))]
    return pl.pallas_call(
        functools.partial(ffn_back_kernel, sourced),
        grid=(ff // block,),
        in_specs=specs
        + [
            pl.BlockSpec((d, block), lambda j: (0, j)),
            pl.BlockSpec((block, d), lambda j: (j, 0)),
            pl.BlockSpec((t, block), lambda j: (0, j)),
            full((t, d)),
            full((1, d)),
        ],
        out_specs=[
            pl.BlockSpec((t, block), lambda j: (0, j)),
            full((t, d)),
            full((t, d)),
            full((t, d)),
            full((1, d)),
        ],
        out_shape=[
            jax.ShapeDtypeStruct((t, ff), BF),
            jax.ShapeDtypeStruct((t, d), BF),
            jax.ShapeDtypeStruct((t, d), F32),
            jax.ShapeDtypeStruct((t, d), BF),
            jax.ShapeDtypeStruct((1, d), F32),
        ],
        scratch_shapes=[pltpu.VMEM((t, d), F32), pltpu.VMEM((t, d), F32)],
        compiler_params=params(32),
        cost_estimate=cost(4 * t * d * ff, 4 * d * ff + 4 * t * ff + 16 * t * d),
        name="ffn_back",
    )(*args, w_in, w_out, slope, mid, gain)


def fill_bias(q_seg, k_seg, bias, causal, rows):
    length, width = bias.shape
    for begin in range(0, length, rows):
        allowed = q_seg[begin : begin + rows, :] == k_seg[...]
        if causal:
            at = lax.broadcasted_iota(jnp.int32, (rows, width), 0) + begin
            key = lax.broadcasted_iota(jnp.int32, (rows, width), 1)
            allowed = allowed & (key <= at)
        bias[begin : begin + rows, :] = jnp.where(allowed, 0.0, MASKED)


def join_keys(refs, count, extra, width):
    keys, values, mem_keys, mem_values, all_keys, all_values = refs
    for source, more, target in ((keys, mem_keys, all_keys), (values, mem_values, all_values)):
        target[:count, :] = source[...]
        target[count : count + extra, :] = more[...]


def attend_kernel(extra, causal, rows, *refs):
    if extra:
        q_seg, k_seg, q, k, v, mk, mv, out, logs, bias, ks, vs = refs
    else:
        q_seg, k_seg, q, k, v, out, logs, bias = refs
    length, width = bias.shape
    count = k.shape[0]
    step = pl.program_id(0)

    @pl.when(step == 0)
    def _():
        fill_bias(q_seg, k_seg, bias, causal, rows)
        logs[...] = jnp.zeros_like(logs)
        if extra:
            ks[count:, :] = jnp.zeros((width - count, LANES), BF)
            vs[count:, :] = jnp.zeros((width - count, LANES), BF)

    if extra:
        join_keys((k, v, mk, mv, ks, vs), count, extra, width)
        k, v = ks, vs
    lane = lax.broadcasted_iota(jnp.int32, (rows, LANES), 1)
    for begin in range(0, length, rows):
        here = slice(begin, begin + rows)
        queries = q[here, :] * BF(HD**-0.5)
        sides = []
        kept = logs[here, :]
        for head in range(2):
            mine = (lane < HD) if head == 0 else (lane >= HD)
            scores = nt(jnp.where(mine, queries, BF(0)), k[...]) + bias[here, :]
            top = jnp.max(scores, axis=1, keepdims=True)
            exponent = jnp.exp(scores - top)
            sums = jnp.sum(exponent, axis=1, keepdims=True)
            sides.append(nn(exponent.astype(BF), v[...]) * (1.0 / sums))
            kept = jnp.where(lane == 2 * step + head, top + jnp.log(sums), kept)
        logs[here, :] = kept
        out[here, :] = jnp.where(lane < HD, sides[0], sides[1]).astype(BF)


def part_of(stack, index):
    rows = stack.shape[1]
    return pl.BlockSpec((None, rows, LANES), lambda p: (index, 0, p))


def attend(q, k, v, q_seg, k_seg, memory=None, causal=False, rows=256):
    t, d = q[0].shape[1:]
    count = k[0].shape[1]
    width = k_seg.shape[1]
    args = [q_seg, k_seg, q[0], k[0], v[0]]
    specs = [full(q_seg.shape), full(k_seg.shape), part_of(*q), part_of(*k), part_of(*v)]
    scratch = [pltpu.VMEM((t, width), F32)]
    extra = 0
    if memory is not None:
        extra = memory.shape[1]
        args += [memory, memory]
        specs += [part_of(memory, 0), part_of(memory, 1)]
        scratch += [pltpu.VMEM((width, LANES), BF)] * 2
    return pl.pallas_call(
        functools.partial(attend_kernel, extra, causal, rows),
        grid=(d // LANES,),
        in_specs=specs,
        out_specs=[pl.BlockSpec((t, LANES), lambda p: (0, p)), full((t, LANES))],
        out_shape=[jax.ShapeDtypeStruct((t, d), BF), jax.ShapeDtypeStruct((t, LANES), F32)],
        scratch_shapes=scratch,
        compiler_params=params(),
        cost_estimate=cost(16 * t * width * d, 8 * d * (t + count), t * width * d // HD),
        name="attend",
    )(*args)


def attend_back_kernel(extra, causal, rows, *refs):
    if extra:
        q_seg, k_seg, q, k, v, out, logs, grad, wo, mk, mv = refs[:11]
        dq, dk, dv, dmk, dmv, bias, dks, dvs, ks, vs = refs[11:]
    else:
        q_seg, k_seg, q, k, v, out, logs, grad, wo, dq, dk, dv, bias, dks, dvs = refs
    length, width = bias.shape
    count = k.shape[0]
    step = pl.program_id(0)

    @pl.when(step == 0)
    def _():
        fill_bias(q_seg, k_seg, bias, causal, rows)
        if extra:
            ks[count:, :] = jnp.zeros((width - count, LANES), BF)
            vs[count:, :] = jnp.zeros((width - count, LANES), BF)

    if extra:
        join_keys((k, v, mk, mv, ks, vs), count, extra, width)
        k, v = ks, vs
    lane = lax.broadcasted_iota(jnp.int32, (rows, LANES), 1)
    for begin in range(0, length, rows):
        here = slice(begin, begin + rows)
        queries = q[here, :] * BF(HD**-0.5)
        mixed = nt(grad[here, :], wo[...]).astype(BF)
        product = mixed.astype(F32) * out[here, :].astype(F32)
        kept = logs[here, :]
        sides = []
        for head in range(2):
            mine = (lane < HD) if head == 0 else (lane >= HD)
            own_q = jnp.where(mine, queries, BF(0))
            own_grad = jnp.where(mine, mixed, BF(0))
            log_sum = jnp.sum(jnp.where(lane == 2 * step + head, kept, 0.0), axis=1, keepdims=True)
            center = jnp.sum(jnp.where(mine, product, 0.0), axis=1, keepdims=True)
            probs = jnp.exp(nt(own_q, k[...]) + bias[here, :] - log_sum)
            score_grad = (probs * (nt(own_grad, v[...]) - center)).astype(BF)
            sides.append(nn(score_grad, k[...]))
            value_part = nn(own_grad.T, probs.astype(BF))
            key_part = nn(own_q.T, score_grad)
            if begin == 0 and head == 0:
                dvs[...] = value_part
                dks[...] = key_part
            else:
                dvs[...] += value_part
                dks[...] += key_part
        dq[here, :] = (jnp.where(lane < HD, sides[0], sides[1]) * HD**-0.5).astype(BF)
    dk[...] = dks[:, :count].T.astype(BF)
    dv[...] = dvs[:, :count].T.astype(BF)
    if extra:
        dmk[...] = dks[:, count:].T[:extra].astype(BF)
        dmv[...] = dvs[:, count:].T[:extra].astype(BF)


def attend_back(q, k, v, out, logs, grad, wo, q_seg, k_seg, memory=None, causal=False, rows=256):
    t, d = q[0].shape[1:]
    count = k[0].shape[1]
    width = k_seg.shape[1]
    column = lambda n: pl.BlockSpec((n, LANES), lambda p: (0, p))
    args = [q_seg, k_seg, q[0], k[0], v[0], out, logs, grad, wo]
    specs = [full(q_seg.shape), full(k_seg.shape), part_of(*q), part_of(*k), part_of(*v)]
    specs += [column(t), full((t, LANES)), full((t, d)), pl.BlockSpec((LANES, d), lambda p: (p, 0))]
    scratch = [pltpu.VMEM((t, width), F32)] + [pltpu.VMEM((LANES, width), F32)] * 2
    lengths = [t, count, count]
    extra = 0
    if memory is not None:
        extra = memory.shape[1]
        args += [memory, memory]
        specs += [part_of(memory, 0), part_of(memory, 1)]
        scratch += [pltpu.VMEM((width, LANES), BF)] * 2
        lengths += [extra, extra]
    return pl.pallas_call(
        functools.partial(attend_back_kernel, extra, causal, rows),
        grid=(d // LANES,),
        in_specs=specs,
        out_specs=[column(n) for n in lengths],
        out_shape=[jax.ShapeDtypeStruct((n, d), BF) for n in lengths],
        scratch_shapes=scratch,
        compiler_params=params(),
        cost_estimate=cost(32 * t * width * d, 12 * d * (t + count), t * width * d // HD),
        name="attend_back",
    )(*args)


def share_rows(index, acc, out, shards, size):
    for turn in range(shards):
        shard = index[0] ^ turn
        start = pl.multiple_of(shard * size, 16)
        out[turn] = acc[pl.ds(start, size), :].astype(BF)


def squares_kernel(items, shards, index, *refs):
    out, acc = refs[-2:]
    size = acc.shape[0] // shards
    for j, (a, g) in enumerate(items):

        @pl.when(pl.program_id(0) == j)
        def _(a=a, g=g):
            acc[...] = tn(refs[g][...], refs[a][...])
            share_rows(index, acc, out, shards, size)


def pad_rows(rows):
    return -(-rows // CHUNK) * CHUNK


def square_grads(place, products):
    arrays, items = [], []

    def at(array):
        for i, other in enumerate(arrays):
            if other is array:
                return i
        arrays.append(array)
        return len(arrays) - 1

    for acts, grads in products:
        for grad in grads:
            items.append((at(acts), at(grad)))
    shards = place.sizes["dp"]
    d = products[0][0].shape[1]
    size = d // shards
    work = sum(2 * arrays[a].shape[0] * d * d for a, _ in items)
    return pl.pallas_call(
        functools.partial(squares_kernel, items, shards),
        grid=(len(items),),
        in_specs=[pl.BlockSpec(memory_space=pltpu.SMEM)] + [full(x.shape) for x in arrays],
        out_specs=pl.BlockSpec((shards, size, d), lambda j: (0, j, 0)),
        out_shape=jax.ShapeDtypeStruct((shards, pad_rows(len(items) * size), d), BF),
        scratch_shapes=[pltpu.VMEM((d, d), F32)],
        compiler_params=params(),
        cost_estimate=cost(work, sum(2 * x.size for x in arrays) + 2 * len(items) * d * d),
        name="square_grads",
    )(place.index, *arrays)


def out_kernel(shards, index, acts, grad, out, acc):
    acc[...] = tn(grad[...], acts[...])
    share_rows(index, acc, out, shards, acc.shape[0] // shards)


def ff_out_grads(place, acts, grad):
    shards = place.sizes["dp"]
    t, d = grad.shape
    blocks = acts.shape[1] // d
    size = d // shards
    return pl.pallas_call(
        functools.partial(out_kernel, shards),
        grid=(blocks,),
        in_specs=[
            pl.BlockSpec(memory_space=pltpu.SMEM),
            pl.BlockSpec((t, d), lambda j: (0, j)),
            full((t, d)),
        ],
        out_specs=pl.BlockSpec((shards, size, d), lambda j: (0, j, 0)),
        out_shape=jax.ShapeDtypeStruct((shards, blocks * size, d), BF),
        scratch_shapes=[pltpu.VMEM((d, d), F32)],
        compiler_params=params(),
        cost_estimate=cost(2 * t * d * d * blocks, 2 * (t + d) * d * (blocks + 1)),
        name="ff_out_grads",
    )(place.index, acts, grad)


def in_kernel(per_block, index, grad, acts, out):
    acc = tn(grad[...], acts[...]).astype(BF)
    size = acc.shape[0] // per_block
    for i in range(per_block):
        shard = pl.program_id(0) * per_block + i
        out[index[0] ^ shard] = acc[i * size : (i + 1) * size]


def ff_in_grads(place, acts, grad):
    shards = place.sizes["dp"]
    t, d = acts.shape
    ff = grad.shape[1]
    blocks = ff // d
    size = ff // shards
    return pl.pallas_call(
        functools.partial(in_kernel, d // size),
        grid=(blocks,),
        in_specs=[
            pl.BlockSpec(memory_space=pltpu.SMEM),
            pl.BlockSpec((t, d), lambda j: (0, j)),
            full((t, d)),
        ],
        out_specs=full((shards, size, d)),
        out_shape=jax.ShapeDtypeStruct((shards, size, d), BF),
        compiler_params=params(),
        cost_estimate=cost(2 * t * d * ff, 2 * (t + d) * d * (blocks + 1)),
        name="ff_in_grads",
    )(place.index, grad, acts)


def ffn_back_weights_kernel(
    index, grad, w_in, w_out, slope, hidden, low_in, mid, gain,
    new, low, gain_grad, out_part, in_part, total, acc,
):
    step = pl.program_id(0)

    @pl.when(step == 0)
    def _():
        total[...] = jnp.zeros_like(total)

    acc[...] = tn(grad[...], hidden[...])
    share_rows(index, acc, out_part, out_part.shape[0], out_part.shape[1])
    block = (nt(grad[...], w_out[...]) * slope[...].astype(F32)).astype(BF)
    total[...] += nt(block, w_in[...])
    in_part[index[0] ^ step] = tn(low_in[...], block).astype(BF)

    @pl.when(step == pl.num_programs(0) - 1)
    def _():
        back, gain_grad[...] = rms_back(mid[...], gain[...], total[...])
        value = grad[...].astype(F32) + back
        new[...] = value
        low[...] = value.astype(BF)


def ffn_back_weights(place, grad, w_in, w_out, slope, hidden, low_in, mid, gain):
    t, d = mid.shape
    blocks = w_in.shape[1] // d
    shards = place.sizes["dp"]
    size = d // shards
    return pl.pallas_call(
        ffn_back_weights_kernel,
        grid=(blocks,),
        in_specs=[
            pl.BlockSpec(memory_space=pltpu.SMEM),
            full((t, d)),
            pl.BlockSpec((d, d), lambda j: (0, j)),
            pl.BlockSpec((d, d), lambda j: (j, 0)),
            pl.BlockSpec((t, d), lambda j: (0, j)),
            pl.BlockSpec((t, d), lambda j: (0, j)),
            full((t, d)),
            full((t, d)),
            full((1, d)),
        ],
        out_specs=[
            full((t, d)),
            full((t, d)),
            full((1, d)),
            pl.BlockSpec((shards, size, d), lambda j: (0, j, 0)),
            full((shards, d, d)),
        ],
        out_shape=[
            jax.ShapeDtypeStruct((t, d), F32),
            jax.ShapeDtypeStruct((t, d), BF),
            jax.ShapeDtypeStruct((1, d), F32),
            jax.ShapeDtypeStruct((shards, blocks * size, d), BF),
            jax.ShapeDtypeStruct((shards, d, d), BF),
        ],
        scratch_shapes=[pltpu.VMEM((t, d), F32), pltpu.VMEM((d, d), F32)],
        compiler_params=params(32),
        cost_estimate=cost(8 * t * d * d * blocks, 8 * d * d * blocks + 24 * t * d),
        name="ffn_back_weights",
    )(place.index, grad, w_in, w_out, slope, hidden, low_in, mid, gain)


def flip(index, bit):
    return index + bit - 2 * bit * ((index // bit) % 2)


class Place:
    def __init__(self, sizes):
        self.sizes = sizes
        self.dp = lax.axis_index("dp")
        self.row = lax.axis_index("row")
        self.index = self.dp.astype(jnp.int32)[None]

    def swap(self, value, axis, turn):
        return lax.ppermute(value, axis, [(i, i ^ turn) for i in range(self.sizes[axis])])

    def bits(self, axis):
        return [1 << i for i in range(self.sizes[axis].bit_length() - 1)]


QUARTER = 48
CHUNK = 4 * QUARTER
AHEAD = 3
DELAY = 4
FAR_RING = DELAY + 2
Y_RING = DELAY + 4
RING = 5
MESH_ID = pl.DeviceIdType.MESH


def add(left, right):
    return (left.astype(F32) + right.astype(F32)).astype(BF)


class Reducer:
    def __init__(self, groups, counts, row_bits, out, refs):
        self.groups, self.counts, self.out = groups, counts, out
        self.total = sum(counts)
        others = len(row_bits) - 2
        (self.own, self.core_in, self.far, self.near, self.y_in, self.x_in, self.z_in, self.kept) = refs[:8]
        self.w_in = refs[8 : 8 + others]
        sems = list(refs[8 + others :])
        self.load_sem, self.kept_sem, self.core_send, self.core_recv = sems[:4]
        self.core_free, self.send, self.recv, self.free = sems[4], sems[5::3], sems[6::3], sems[7::3]
        row, dp = lax.axis_index("row"), lax.axis_index("dp")
        self.x, self.z = row % 2, (row // 2) % 2
        self.core_peer = (row, flip(dp, 1))
        self.y_peer = (row, flip(dp, 2))
        self.row_peers = [(flip(row, bit), dp) for bit in row_bits]
        self.x_peer, self.z_peer = self.row_peers[:2]
        self.peers = [self.core_peer, self.y_peer] + self.row_peers
        self.stages = [self.y_stage, self.x_stage, self.z_stage]
        self.stages += [functools.partial(self.w_stage, i) for i in range(others)]
        self.stages += [self.back_z_stage, self.back_x_stage]
        self.steps = self.total + DELAY + len(self.stages) - 1

    @staticmethod
    def scratch(row_bits, d):
        others = len(row_bits) - 2
        chunk = (2, 2, QUARTER, d)
        shapes = [
            (AHEAD, 2) + chunk,
            (AHEAD, 2) + chunk,
            (FAR_RING,) + chunk,
            (FAR_RING,) + chunk,
            (Y_RING,) + chunk,
            (RING,) + chunk[1:],
            (RING,) + chunk[2:],
            (RING,) + chunk[2:],
        ] + [(RING,) + chunk[2:]] * others
        dma = pltpu.SemaphoreType.DMA
        regular = pltpu.SemaphoreType.REGULAR
        rings = [Y_RING, RING, RING] + [RING] * others + [RING, RING]
        sems = [dma((AHEAD, 2)), dma((RING,)), dma((AHEAD, 2)), dma((AHEAD, 2)), regular]
        for ring in rings:
            sems += [dma((ring,)), dma((ring,)), regular]
        return [pltpu.VMEM(shape, BF) for shape in shapes] + sems

    def greet(self):
        barrier = pltpu.get_barrier_semaphore()
        for peer in self.peers:
            pl.semaphore_signal(barrier, inc=1, device_id=peer, device_id_type=MESH_ID)
        pl.semaphore_wait(barrier, len(self.peers))

    def start(self):
        for c in range(min(AHEAD, self.total)):
            self.begin(c)

    def step(self, t):
        @pl.when(t < self.total)
        def _():
            self.core_stage(t)

        for i, stage in enumerate(self.stages):
            c = t - DELAY - i

            @pl.when((c >= 0) & (c < self.total))
            def _(c=c, stage=stage):
                stage(c)

        @pl.when(t + AHEAD < self.total)
        def _():
            pl.semaphore_wait(self.core_free, 1)
            self.begin(t + AHEAD)

    def remote(self, stage, ring, c, source, target, peer):
        return pltpu.make_async_remote_copy(
            src_ref=source,
            dst_ref=target,
            send_sem=self.send[stage].at[c % ring],
            recv_sem=self.recv[stage].at[c % ring],
            device_id=peer,
            device_id_type=MESH_ID,
        )

    def give(self, stage, ring, c, peer):
        @pl.when(c + ring < self.total)
        def _():
            pl.semaphore_signal(
                self.free[stage], inc=1, device_id=peer, device_id_type=MESH_ID
            )

    def take(self, stage, ring, c):
        @pl.when(c >= ring)
        def _():
            pl.semaphore_wait(self.free[stage], 1)

    def core_copy(self, c, side, source):
        return pltpu.make_async_remote_copy(
            src_ref=source,
            dst_ref=self.core_in.at[c % AHEAD, side],
            send_sem=self.core_send.at[c % AHEAD, side],
            recv_sem=self.core_recv.at[c % AHEAD, side],
            device_id=self.core_peer,
            device_id_type=MESH_ID,
        )

    def load(self, c, side, source):
        return pltpu.make_async_copy(
            source, self.own.at[c % AHEAD, side], self.load_sem.at[c % AHEAD, side]
        )

    def begin(self, c):
        first = 0
        for group, count in zip(self.groups, self.counts):

            @pl.when((c >= first) & (c < first + count))
            def _(group=group, first=first):
                at = c - first
                for side in range(2):
                    self.core_copy(c, side, group.at[2 * side + 1, at]).start()
                for side in range(2):
                    self.load(c, side, group.at[2 * side, at]).start()

            first += count

    def y_copy(self, c):
        return self.remote(0, Y_RING, c, self.far.at[c % FAR_RING], self.y_in.at[c % Y_RING], self.y_peer)

    def x_copy(self, c):
        source = self.y_in.at[c % Y_RING, 1 - self.x]
        return self.remote(1, RING, c, source, self.x_in.at[c % RING], self.x_peer)

    def z_copy(self, c):
        source = self.x_in.at[c % RING, 1 - self.z]
        return self.remote(2, RING, c, source, self.z_in.at[c % RING], self.z_peer)

    def w_copy(self, i, c):
        source = self.z_in if i == 0 else self.w_in[i - 1]
        return self.remote(
            3 + i, RING, c, source.at[c % RING], self.w_in[i].at[c % RING], self.row_peers[2 + i]
        )

    def back_z_copy(self, c, place):
        at = self.out.at[c, self.x, place]
        return self.remote(3 + len(self.w_in), RING, c, self.kept.at[c % RING], at, self.z_peer)

    def kept_copy(self, c):
        at = self.out.at[c, self.x, self.z]
        return pltpu.make_async_copy(self.kept.at[c % RING], at, self.kept_sem.at[c % RING])

    def back_x_copy(self, c, place):
        at = self.out.at[c, place]
        return self.remote(4 + len(self.w_in), RING, c, at, at, self.x_peer)

    def core_stage(self, c):
        slot, at = c % AHEAD, c % FAR_RING
        for side in range(2):
            self.load(c, side, self.own.at[slot, side]).wait()
            self.core_copy(c, side, self.own.at[slot, side]).wait()
        self.far[at] = add(self.own[slot, 1], self.core_in[slot, 1])
        self.take(0, Y_RING, c)
        self.y_copy(c).start()
        self.near[at] = add(self.own[slot, 0], self.core_in[slot, 0])

        @pl.when(c + AHEAD < self.total)
        def _():
            pl.semaphore_signal(
                self.core_free, inc=1, device_id=self.core_peer, device_id_type=MESH_ID
            )

    def y_stage(self, c):
        self.y_copy(c).wait()
        slot = c % Y_RING
        self.y_in[slot] = add(self.y_in[slot], self.near[c % FAR_RING])
        self.take(1, RING, c)
        self.x_copy(c).start()

    def x_stage(self, c):
        self.x_copy(c).wait()
        slot = c % RING
        self.x_in[slot] = add(self.x_in[slot], self.y_in[c % Y_RING, self.x])
        self.give(0, Y_RING, c, self.y_peer)
        self.take(2, RING, c)
        self.z_copy(c).start()

    def z_stage(self, c):
        self.z_copy(c).wait()
        slot = c % RING
        self.z_in[slot] = add(self.z_in[slot], self.x_in[slot, self.z])
        self.give(1, RING, c, self.x_peer)
        self.take(3, RING, c)
        self.w_copy(0, c).start()

    def w_stage(self, i, c):
        self.w_copy(i, c).wait()
        slot = c % RING
        source = self.z_in if i == 0 else self.w_in[i - 1]
        value = add(self.w_in[i][slot], source[slot])
        giver = self.z_peer if i == 0 else self.row_peers[1 + i]
        self.give(2 + i, RING, c, giver)
        if i + 1 < len(self.w_in):
            self.w_in[i][slot] = value
            self.take(4 + i, RING, c)
            self.w_copy(i + 1, c).start()
        else:
            self.kept[slot] = value
            self.give(3 + i, RING, c, self.row_peers[2 + i])
            self.kept_copy(c).start()
            self.back_z_copy(c, self.z).start()

    def back_z_stage(self, c):
        self.kept_copy(c).wait()
        self.back_z_copy(c, self.z).wait_send()
        self.back_z_copy(c, 1 - self.z).wait_recv()
        self.back_x_copy(c, self.x).start()

    def back_x_stage(self, c):
        self.back_x_copy(c, self.x).wait_send()
        self.back_x_copy(c, 1 - self.x).wait_recv()


def reduce_kernel(counts, row_bits, *refs):
    count = len(counts)
    reducer = Reducer(refs[:count], counts, row_bits, refs[count], refs[count + 1 :])
    reducer.greet()
    reducer.start()

    def step(t, carry):
        reducer.step(t)
        return carry

    lax.fori_loop(0, reducer.steps, step, 0)


def chunk_view(group):
    turns, rows, d = group.shape
    return group.reshape(turns, rows // CHUNK, 2, 2, QUARTER, d)


def split_sums(result, counts):
    d = result.shape[-1]
    sums, first = [], 0
    for n in counts:
        sums.append(result[first : first + n].reshape(n * CHUNK, d))
        first += n
    return sums


def reduce_all(place, groups):
    d = groups[0].shape[-1]
    counts = [g.shape[1] // CHUNK for g in groups]
    row_bits = place.bits("row")
    result = pl.pallas_call(
        functools.partial(reduce_kernel, counts, row_bits),
        in_specs=[pl.BlockSpec(memory_space=pl.ANY)] * len(groups),
        out_specs=pl.BlockSpec(memory_space=pl.ANY),
        out_shape=jax.ShapeDtypeStruct((sum(counts), 2, 2, QUARTER, d), BF),
        scratch_shapes=Reducer.scratch(row_bits, d),
        compiler_params=pltpu.CompilerParams(
            collective_id=0, has_side_effects=True, vmem_limit_bytes=48 * 2**20
        ),
        cost_estimate=cost(0, 4 * sum(counts) * CHUNK * d),
        name="reduce_all",
    )(*[chunk_view(g) for g in groups])
    return split_sums(result, counts)


def xor(left, right, bits):
    total = 0
    for bit in bits:
        a, b = (left // bit) % 2, (right // bit) % 2
        total = total + bit * (a + b - 2 * a * b)
    return total


TILE = 256
HALF = 2 * CHUNK


def encoder_back_kernel(counts, row_bits, memories, *refs):
    given = len(counts)
    (q_seg, k_seg, dck, dcv, cross, mid, tokens, dec_gain_grads, gain0, gain1) = refs[:10]
    (w_in, w_out, slope, hidden, mid_low, q, k, v, mk, mv, mixed, logs, wo, enc_low, fetched, w_qkv) = refs[10:26]
    groups, refs = refs[26 : 26 + given], refs[26 + given :]
    out, ff_out_part, ff_in_part, squares_part, token_grad, gain_sums = refs[:6]
    (g, total, acc, low, g_low, pg, dq, dk, dv, dmk, dmv, bias, ks, vs, dks, dvs) = refs[6:22]
    (stage_a, stage_b, gain_acc, gain_in, copy_sem, gain_send, gain_recv) = refs[22:29]
    parts = [ff_out_part, ff_in_part, squares_part]
    all_counts = list(counts) + [part.shape[1] for part in parts]
    reducer = Reducer(list(groups) + parts, all_counts, row_bits, out, refs[29:])
    me = lax.axis_index("dp")
    t = pl.program_id(0)
    length = g.shape[0]
    count = k.shape[0]
    width = bias.shape[1]
    blocks = ff_out_part.shape[1]
    pairs = g.shape[1] // LANES
    A0 = blocks
    S0 = A0 + pairs
    P0 = S0 + 6
    END = P0 + 3
    tiles = [slice(b, b + TILE) for b in range(0, length, TILE)]

    def fetch(source, target, i):
        return pltpu.make_async_copy(source, target, copy_sem.at[i])

    def early():
        return [
            fetch(dck, dq, 0),
            fetch(dcv, dk, 1),
            fetch(cross.at[1], dv, 2),
            fetch(cross.at[2], pg, 3),
            fetch(mid, token_grad, 4),
        ]

    def late():
        return fetch(tokens, pg, 3)

    def shares():
        for turn in range(4):
            shard = xor(me, turn, (1, 2))
            for i in range(4):
                start = pl.multiple_of(shard * CHUNK + i * QUARTER, 16)
                stage_a[turn, i // 2, i % 2] = acc[pl.ds(start, QUARTER), :].astype(BF)

    def copy_ff_out():
        return fetch(stage_a, ff_out_part.at[:, t], 5)

    def copy_ff_in():
        return fetch(stage_b, ff_in_part.at[xor(me, t, (1, 2))], 6)

    def copy_squares():
        return fetch(stage_a, squares_part.at[:, t - S0], 5)

    @pl.when(t == 0)
    def _():
        for copy in early():
            copy.start()
        reducer.greet()
        reducer.start()
        fill_bias(q_seg, k_seg, bias, False, TILE)
        ks[count:, :] = jnp.zeros((width - count, LANES), BF)
        vs[count:, :] = jnp.zeros((width - count, LANES), BF)
        gain_acc[0] = dec_gain_grads[...]
        for copy in early():
            copy.wait()
        for here in tiles:
            value = nt(dq[here, :], dv[...]) + nt(dk[here, :], pg[...])
            g[here, :] = value
            g_low[here, :] = value.astype(BF)
            total[here, :] = jnp.zeros_like(value)

    @pl.when(t < A0)
    def _():
        for here in tiles:
            block = (nt(g_low[here, :], w_out[...]) * slope[here, :].astype(F32)).astype(BF)
            pg[here, :] = block
            total[here, :] += nt(block, w_in[...])
        for n in range(0, acc.shape[0], HALF):
            acc[n : n + HALF, :] = tn(g_low[:, n : n + HALF], hidden[...])
        shares()
        copy_ff_out().start()
        for n in range(0, mid_low.shape[1], HALF):
            value = tn(mid_low[:, n : n + HALF], pg[...])
            for i in range(8):
                stage_b[n // CHUNK + i // 4, (i // 2) % 2, i % 2] = value[
                    i * QUARTER : (i + 1) * QUARTER, :
                ].astype(BF)
        copy_ff_in().start()

    @pl.when(t == A0 - 1)
    def _():
        gain_sum = jnp.zeros((1, g.shape[1]), F32)
        for here in tiles:
            back, gain_part = rms_back(token_grad[here, :], gain1[...], total[here, :])
            gain_sum = gain_sum + gain_part
            value = g[here, :] + back
            g[here, :] = value
            low[here, :] = value.astype(BF)
        gain_acc[0, 1:2, :] = gain_sum

    @pl.when((t >= A0) & (t < S0))
    def _():
        pair = t - A0
        lanes = pl.ds(pl.multiple_of(pair * LANES, LANES), LANES)
        join_keys((k, v, mk, mv, ks, vs), count, memories, width)
        lane = lax.broadcasted_iota(jnp.int32, (TILE, LANES), 1)
        for number, here in enumerate(tiles):
            queries = q[here, :] * BF(HD**-0.5)
            grads = nt(low[here, :], wo[...]).astype(BF)
            product = grads.astype(F32) * mixed[here, lanes].astype(F32)
            kept = logs[here, :]
            sides = []
            for head in range(2):
                mine = (lane < HD) if head == 0 else (lane >= HD)
                own_q = jnp.where(mine, queries, BF(0))
                own_grad = jnp.where(mine, grads, BF(0))
                chosen = lane == 2 * pair + head
                log_sum = jnp.sum(jnp.where(chosen, kept, 0.0), axis=1, keepdims=True)
                center = jnp.sum(jnp.where(mine, product, 0.0), axis=1, keepdims=True)
                probs = jnp.exp(nt(own_q, ks[...]) + bias[here, :] - log_sum)
                score_grad = (probs * (nt(own_grad, vs[...]) - center)).astype(BF)
                sides.append(nn(score_grad, ks[...]))
                value_part = nn(own_grad.T, probs.astype(BF))
                key_part = nn(own_q.T, score_grad)
                if number == 0 and head == 0:
                    dvs[...] = value_part
                    dks[...] = key_part
                else:
                    dvs[...] += value_part
                    dks[...] += key_part
            dq[here, lanes] = (jnp.where(lane < HD, sides[0], sides[1]) * HD**-0.5).astype(BF)
        dk[:, lanes] = dks[:, :count].T.astype(BF)
        dv[:, lanes] = dvs[:, :count].T.astype(BF)
        dmk[:, lanes] = dks[:, count:].T[:memories].astype(BF)
        dmv[:, lanes] = dvs[:, count:].T[:memories].astype(BF)

    items = [(enc_low, dq), (enc_low, dk), (enc_low, dv), (mixed, low), (fetched, dmk), (fetched, dmv)]
    for j, (acts, grads) in enumerate(items):

        @pl.when(t == S0 + j)
        def _(acts=acts, grads=grads):
            for n in range(0, acc.shape[0], HALF):
                acc[n : n + HALF, :] = tn(grads[:, n : n + HALF], acts[...])
            shares()
            copy_squares().start()

    for j, grads in enumerate((dq, dk, dv)):

        @pl.when(t == P0 + j)
        def _(j=j, grads=grads):
            if j == 0:
                late().start()
            for here in tiles:
                value = nt(grads[here, :], w_qkv[...])
                total[here, :] = value if j == 0 else total[here, :] + value

    @pl.when(t == END - 1)
    def _():
        late().wait()
        gain_sum = jnp.zeros((1, g.shape[1]), F32)
        for here in tiles:
            back, gain_part = rms_back(pg[here, :].astype(F32), gain0[...], total[here, :])
            gain_sum = gain_sum + gain_part
            token_grad[here, :] = g[here, :] + back
        gain_acc[0, 0:1, :] = gain_sum

    reducer.step(t)

    @pl.when(t < A0)
    def _():
        copy_ff_out().wait()
        copy_ff_in().wait()

    @pl.when((t >= S0) & (t < P0))
    def _():
        copy_squares().wait()

    def gain_copy(i):
        return pltpu.make_async_remote_copy(
            src_ref=gain_acc.at[i],
            dst_ref=gain_in.at[i],
            send_sem=gain_send.at[i],
            recv_sem=gain_recv.at[i],
            device_id=reducer.peers[i],
            device_id_type=MESH_ID,
        )

    last = len(reducer.peers)
    for i in range(last + 1):

        @pl.when(t == END + i)
        def _(i=i):
            if i:
                gain_copy(i - 1).wait()
                value = gain_acc[i - 1] + gain_in[i - 1]
                if i < last:
                    gain_acc[i] = value
                else:
                    gain_sums[...] = value
            if i < last:
                gain_copy(i).start()


def encoder_back(
    place, groups, q_seg, k_seg, dck, dcv, cross, mid, tokens, dec_gain_grads, gains,
    w_in, w_out, slope, hidden, mid_low, qkv, memory, mixed, logs, wo, enc_low, fetched, w_qkv,
):
    t, d = tokens.shape
    ff = w_in.shape[1]
    blocks, pairs, memories = ff // d, d // LANES, fetched.shape[0]
    width = k_seg.shape[1]
    row_bits = place.bits("row")
    counts = [g.shape[1] // CHUNK for g in groups]
    new = [blocks, ff // (4 * CHUNK), 6]
    total = sum(counts) + sum(new)
    A0 = blocks
    P0 = A0 + pairs + 6
    steps = max(total + DELAY + len(row_bits) + 2, P0 + 6 + len(row_bits))

    def phase(first, size):
        return lambda s: jnp.minimum(jnp.maximum(s - first, 0), size - 1)

    f_at, a_at, p_at = phase(0, blocks), phase(A0, pairs), phase(P0, 3)
    anywhere = pl.BlockSpec(memory_space=pl.ANY)
    once = lambda shape: pl.BlockSpec(shape, lambda s: (0,) * len(shape), pipeline_mode=pl.Buffered(1))
    column = lambda i: pl.BlockSpec((None, t, LANES), lambda s: (i, 0, a_at(s)))
    in_specs = [
        once((t, 1)), once((1, width)), anywhere, anywhere, anywhere, anywhere, anywhere,
        once((8, d)), once((1, d)), once((1, d)),
        pl.BlockSpec((d, d), lambda s: (0, f_at(s))),
        pl.BlockSpec((d, d), lambda s: (f_at(s), 0)),
        pl.BlockSpec((t, d), lambda s: (0, f_at(s))),
        pl.BlockSpec((t, d), lambda s: (0, f_at(s))),
        once((t, d)),
        column(0), column(1), column(2),
        pl.BlockSpec((None, memories, LANES), lambda s: (0, 0, a_at(s))),
        pl.BlockSpec((None, memories, LANES), lambda s: (1, 0, a_at(s))),
        once((t, d)), once((t, LANES)),
        pl.BlockSpec((LANES, d), lambda s: (a_at(s), 0)),
        once((t, d)), once((memories, d)),
        pl.BlockSpec((None, d, d), lambda s: (p_at(s), 0, 0)),
    ] + [anywhere] * len(groups)
    chunk = (2, 2, QUARTER, d)
    part = lambda n: jax.ShapeDtypeStruct((4, n) + chunk, BF)
    out_shape = [
        jax.ShapeDtypeStruct((total,) + chunk, BF),
        part(new[0]), part(new[1]), part(new[2]),
        jax.ShapeDtypeStruct((t, d), F32),
        jax.ShapeDtypeStruct((8, d), F32),
    ]
    square = lambda kind: pltpu.VMEM((t, d), kind)
    exchanges = 2 + len(row_bits)
    scratch = (
        [square(F32), square(F32), pltpu.VMEM((d, d), F32)]
        + [square(BF)] * 6
        + [pltpu.VMEM((memories, d), BF)] * 2
        + [pltpu.VMEM((t, width), F32)]
        + [pltpu.VMEM((width, LANES), BF)] * 2
        + [pltpu.VMEM((LANES, width), F32)] * 2
        + [pltpu.VMEM((4,) + chunk, BF), pltpu.VMEM((4,) + chunk, BF)]
        + [pltpu.VMEM((exchanges, 8, d), F32)] * 2
        + [pltpu.SemaphoreType.DMA((7,))]
        + [pltpu.SemaphoreType.DMA((exchanges,))] * 2
        + Reducer.scratch(row_bits, d)
    )
    result, _, _, _, token_grad, gain_sums = pl.pallas_call(
        functools.partial(encoder_back_kernel, counts, row_bits, memories),
        grid=(steps,),
        in_specs=in_specs,
        out_specs=[anywhere] * 4 + [once((t, d)), once((8, d))],
        out_shape=out_shape,
        scratch_shapes=scratch,
        compiler_params=pltpu.CompilerParams(
            collective_id=1, has_side_effects=True, vmem_limit_bytes=60 * 2**20
        ),
        cost_estimate=cost(2 * t * d * (4 * ff + 14 * d), 30 * total * CHUNK * d),
        name="encoder_back",
    )(
        q_seg, k_seg, dck, dcv, cross, mid, tokens, dec_gain_grads, gains[0], gains[1],
        w_in, w_out, slope, hidden, mid_low, qkv, qkv, qkv, memory, memory, mixed, logs, wo,
        enc_low, fetched, w_qkv, *[chunk_view(g) for g in groups],
    )
    return result, token_grad, gain_sums


def fold_outer(place, value):
    while value.shape[0] > 4:
        half = value.shape[0] // 2
        value = add(value[:half], place.swap(value[half:], "dp", half))
    return value


def gain_group(place, gains):
    shards = place.sizes["dp"]
    count, d = gains.shape
    parts = gains.reshape(count, shards, -1)
    turned = jnp.stack(
        [lax.dynamic_index_in_dim(parts, place.dp ^ turn, 1, False) for turn in range(shards)]
    )
    return jnp.pad(turned.astype(BF), ((0, 0), (0, CHUNK - count), (0, d - parts.shape[2])))


def weights_of(value, count, size):
    value = value[: count * size].reshape(count, size, -1)
    return jnp.swapaxes(value, 1, 2).astype(F32)


def finish_kernel(places, index, sums, gain_sums, *refs):
    outs, gain_outs = refs[: len(places)], refs[len(places) : len(places) + 3]
    narrow, wide, load_sem, store_sem = refs[len(places) + 3 :]
    spots = [(out, at, i) for out, (count, at) in zip(outs, places) for i in range(count)]
    total = len(spots)

    def load(c):
        return pltpu.make_async_copy(sums.at[c], narrow.at[c], load_sem.at[c])

    def store(c):
        out, at, i = spots[c]
        return pltpu.make_async_copy(
            wide.at[c % 4], out.at[at(i)], store_sem.at[c % 4]
        )

    for c in range(total):
        load(c).start()
    size = gain_outs[2].shape[1]
    for shard in range(gain_sums.shape[1] // size):

        @pl.when(index[0] == shard)
        def _(shard=shard):
            lanes = slice(shard * size, (shard + 1) * size)
            gain_outs[0][...] = gain_sums[0:2, lanes]
            gain_outs[1][...] = gain_sums[2:4, lanes]
            gain_outs[2][...] = gain_sums[4:5, lanes]

    for c in range(total):
        load(c).wait()
        if c >= 4:
            store(c - 4).wait()
        wide[c % 4] = narrow[c].astype(F32)
        store(c).start()
    for c in range(total - 4, total):
        store(c).wait()


def finish_sums(place, sums, gain_sums, blocks):
    d = gain_sums.shape[1]
    total = sums.shape[0]
    one = lambda i: ()
    lead = lambda i: (i,)
    rows = lambda i: (pl.ds(i * CHUNK, CHUNK), slice(None))
    lanes = lambda i: (slice(None), pl.ds(i * d, d))
    flat, tall, wide = (CHUNK, d), (blocks * CHUNK, d), (CHUNK, blocks * d)
    kinds = [
        (wide, blocks, lanes),
        (tall, blocks, rows),
        (flat, 1, one),
        ((3,) + flat, 3, lead),
        ((3,) + flat, 3, lead),
        (flat, 1, one),
        (wide, blocks, lanes),
        (tall, blocks, rows),
        ((3,) + flat, 3, lead),
        (flat, 1, one),
        ((2,) + flat, 2, lead),
    ]
    anywhere = pl.BlockSpec(memory_space=pl.ANY)
    gain_shapes = [(2, CHUNK), (2, CHUNK), (1, CHUNK)]
    return pl.pallas_call(
        functools.partial(finish_kernel, [(count, at) for _, count, at in kinds]),
        in_specs=[
            pl.BlockSpec(memory_space=pltpu.SMEM),
            pl.BlockSpec(memory_space=pltpu.HBM),
            full((8, d)),
        ],
        out_specs=[anywhere] * len(kinds) + [full(shape) for shape in gain_shapes],
        out_shape=[jax.ShapeDtypeStruct(shape, F32) for shape, _, _ in kinds]
        + [jax.ShapeDtypeStruct(shape, F32) for shape in gain_shapes],
        scratch_shapes=[
            pltpu.VMEM((total, CHUNK, d), BF),
            pltpu.VMEM((4, CHUNK, d), F32),
            pltpu.SemaphoreType.DMA((total,)),
            pltpu.SemaphoreType.DMA((4,)),
        ],
        compiler_params=params(24),
        cost_estimate=cost(0, 6 * total * CHUNK * d),
        name="finish_sums",
    )(place.index, sums, gain_sums)


def encoder_back_apart(
    place, groups, q_seg, k_seg, dck, dcv, cross, mid, tokens, dec_gain_grads, gains,
    w_in, w_out, slope, hidden, mid_low, qkv, memory, mixed, logs, wo, enc_low, fetched, w_qkv,
):
    pre_grad, grad_low, new, low, mid_gain_grad = ffn_back(
        (dck, dcv), cross, w_in, w_out, slope, mid, gains[1]
    )
    dq, dk, dv, dmk, dmv = attend_back(
        (qkv, 0), (qkv, 1), (qkv, 2), mixed, logs, low, wo, q_seg, k_seg, memory
    )
    parts = [
        ff_out_grads(place, hidden, grad_low),
        ff_in_grads(place, mid_low, pre_grad),
        square_grads(place, [(enc_low, [dq, dk, dv]), (mixed, [low]), (fetched, [dmk, dmv])]),
    ]
    token_grad, _, enc_gain_grad = proj_back(tokens, gains[0], new, w_qkv, [dq, dk, dv])
    gain_part = gain_group(
        place, jnp.concatenate([enc_gain_grad, mid_gain_grad] + dec_gain_grads)
    )
    parts = [fold_outer(place, part) for part in groups + parts + [gain_part]]
    sums = reduce_all(place, parts)
    size = tokens.shape[1] // place.sizes["dp"]
    return sums, token_grad, sums[-1][:5, :size].astype(F32)


def fetch_memory(place, table, ids):
    rows = table.shape[0]
    others = range(1, place.sizes["dp"])
    wanted = [ids] + [place.swap(ids, "dp", turn) for turn in others]
    local = jnp.concatenate(wanted) - place.dp * rows
    chosen = (local[:, None] == jnp.arange(rows)[None, :]).astype(BF)
    picked = nn(chosen, table).astype(BF).reshape(len(wanted), ids.shape[0], -1)
    result = picked[0]
    for turn in others:
        result = result + place.swap(picked[turn], "dp", turn)
    return result


def on_device(
    sizes,
    enc_input,
    dec_input,
    memory_table,
    memory_ids,
    enc_segments,
    dec_segments,
    enc_qkv,
    enc_attn_out,
    mem_proj,
    enc_gains,
    enc_ff_in,
    enc_ff_out,
    dec_qkv,
    dec_self_out,
    dec_cross,
    dec_cross_out,
    dec_gains,
    dec_ff_in,
    dec_ff_out,
    out_grad,
):
    place = Place(sizes)
    direct = sizes["dp"] == 4
    tokens, answers = enc_input[0], dec_input[0]
    fetched = fetch_memory(place, memory_table, memory_ids.reshape(-1))
    memories = fetched.shape[0]
    enc_gain = enc_gains.astype(F32)[:, None]
    dec_gain = dec_gains.astype(F32)[:, None]

    enc_at, dec_at = enc_segments[0], dec_segments[0]
    enc_q_seg, dec_q_seg = enc_at[:, None], dec_at[:, None]
    owner = jnp.arange(memories, dtype=jnp.int32) // TOPK
    padding = jnp.full((-memories % LANES,), -1, jnp.int32)
    all_k_seg = jnp.concatenate([enc_at, owner, padding])[None]
    enc_k_seg, dec_k_seg = enc_at[None], dec_at[None]

    self_low, self_proj = project(answers, dec_gain[0], dec_qkv, 0, 3)
    self_q, self_k, self_v = [(self_proj, j) for j in range(3)]
    self_mixed, self_logs = attend(self_q, self_k, self_v, dec_q_seg, dec_k_seg, causal=True)
    first, cross_low, cross_q = project(
        answers, dec_gain[1], dec_cross, 0, 1, self_mixed, dec_self_out
    )
    cross_q = (cross_q, 0)

    enc_low, enc_proj = project(tokens, enc_gain[0], enc_qkv, 0, 3)
    enc_q, enc_k, enc_v = [(enc_proj, j) for j in range(3)]
    memory = project_plain(fetched, mem_proj, 0, 2)
    enc_mixed, enc_logs = attend(enc_q, enc_k, enc_v, enc_q_seg, all_k_seg, memory)
    middle, mid_low, enc_hidden, enc_slope, encoded = ffn_forward(
        tokens, enc_mixed, enc_attn_out, enc_gain[1], enc_ff_in, enc_ff_out
    )
    pairs = project_plain(encoded, dec_cross, 1, 2)
    cross_k, cross_v = (pairs, 0), (pairs, 1)
    cross_mixed, cross_logs = attend(cross_q, cross_k, cross_v, dec_q_seg, enc_k_seg)
    second, ffn_low, dec_hidden, dec_slope, final = ffn_forward(
        first, cross_mixed, dec_cross_out, dec_gain[2], dec_ff_in, dec_ff_out
    )

    grad = out_grad[0]
    if direct:
        new, low, ffn_gain_grad, dec_ff_out_part, dec_ff_in_part = ffn_back_weights(
            place, grad, dec_ff_in, dec_ff_out, dec_slope, dec_hidden, ffn_low, second, dec_gain[2]
        )
    else:
        dec_ff_out_part = ff_out_grads(place, dec_hidden, grad)
        pre_grad, _, new, low, ffn_gain_grad = ffn_back(
            grad, None, dec_ff_in, dec_ff_out, dec_slope, second, dec_gain[2]
        )
        dec_ff_in_part = ff_in_grads(place, ffn_low, pre_grad)
    dcq, dck, dcv = attend_back(
        cross_q, cross_k, cross_v, cross_mixed, cross_logs, low, dec_cross_out,
        dec_q_seg, enc_k_seg,
    )
    cross_part = square_grads(
        place, [(cross_mixed, [low]), (cross_low, [dcq]), (encoded, [dck, dcv])]
    )

    new, low, cross_gain_grad = proj_back(first, dec_gain[1], new, dec_cross, [dcq])
    dsq, dsk, dsv = attend_back(
        self_q, self_k, self_v, self_mixed, self_logs, low, dec_self_out,
        dec_q_seg, dec_k_seg, causal=True,
    )
    self_part = square_grads(place, [(self_low, [dsq, dsk, dsv]), (self_mixed, [low])])
    answer_grad, _, self_gain_grad = proj_back(answers, dec_gain[0], new, dec_qkv, [dsq, dsk, dsv])

    dec_gain_grads = [self_gain_grad, cross_gain_grad, ffn_gain_grad]
    dec_parts = [dec_ff_out_part, dec_ff_in_part, cross_part, self_part]
    if direct:
        blank = jnp.zeros((1, tokens.shape[1]), F32)
        result, token_grad, gain_sums = encoder_back(
            place, dec_parts, enc_q_seg, all_k_seg, dck, dcv, dec_cross, middle, tokens,
            jnp.concatenate([blank, blank] + dec_gain_grads + [blank] * 3), enc_gain,
            enc_ff_in, enc_ff_out, enc_slope, enc_hidden, mid_low, enc_proj, memory, enc_mixed,
            enc_logs, enc_attn_out, enc_low, fetched, enc_qkv,
        )
        d = tokens.shape[1]
        (
            dec_out_grad, dec_in_grad, cross_out_grad, cross_grad, self_grad, self_out_grad,
            out_ff_grad, in_ff_grad, qkv_grad, attn_out_grad, mem_grad, enc_gain, dec_gain, ffn_gain,
        ) = finish_sums(place, result.reshape(-1, CHUNK, d), gain_sums, enc_ff_in.shape[1] // d)
        turn = lambda value: jnp.swapaxes(value, -1, -2)
        return (
            final[None],
            token_grad[None],
            answer_grad[None],
            turn(qkv_grad),
            turn(attn_out_grad),
            turn(mem_grad),
            enc_gain,
            in_ff_grad,
            turn(out_ff_grad),
            turn(self_grad),
            turn(self_out_grad),
            turn(cross_grad),
            turn(cross_out_grad),
            dec_gain,
            dec_in_grad,
            turn(dec_out_grad),
            ffn_gain[0],
        )
    sums, token_grad, gains = encoder_back_apart(
        place, dec_parts, enc_q_seg, all_k_seg, dck, dcv, dec_cross, middle, tokens,
        dec_gain_grads, enc_gain, enc_ff_in, enc_ff_out, enc_slope, enc_hidden, mid_low,
        enc_proj, memory, enc_mixed, enc_logs, enc_attn_out, enc_low, fetched, enc_qkv,
    )
    size = tokens.shape[1] // sizes["dp"]
    blocks = enc_ff_in.shape[1] // tokens.shape[1]
    ff_size = enc_ff_in.shape[1] // sizes["dp"]
    enc_squares = weights_of(sums[6], 6, size)
    self_squares = weights_of(sums[3], 4, size)
    cross_squares = weights_of(sums[2], 4, size)
    return (
        final[None],
        token_grad[None],
        answer_grad[None],
        enc_squares[0:3],
        enc_squares[3],
        enc_squares[4:6],
        gains[0:2],
        weights_of(sums[5], 1, ff_size)[0],
        weights_of(sums[4], blocks, size).reshape(-1, size),
        self_squares[0:3],
        self_squares[3],
        cross_squares[1:4],
        cross_squares[0],
        gains[2:4],
        weights_of(sums[1], 1, ff_size)[0],
        weights_of(sums[0], blocks, size).reshape(-1, size),
        gains[4],
    )


def solution(mesh):
    rows = P(("row", "dp"), None, None)
    in_specs = (
        (rows, rows, P("dp", None), rows, P(("row", "dp"), None), P(("row", "dp"), None))
        + (P(),) * 13
        + (rows,)
    )
    cube, flat = P(None, None, "dp"), P(None, "dp")
    out_specs = (
        (rows, rows, rows)
        + (cube, flat, cube, flat, flat, flat)
        + (cube, flat, cube, flat, flat, flat, flat)
        + (P("dp"),)
    )
    return jax.shard_map(
        functools.partial(on_device, dict(mesh.shape)),
        mesh=mesh,
        in_specs=in_specs,
        out_specs=out_specs,
        check_vma=False,
    )
```

```python
import functools

import jax
import jax.numpy as jnp
from jax import lax
from jax.experimental import pallas as pl
from jax.experimental.pallas import tpu as pltpu
from jax.sharding import PartitionSpec as P

HD = 64
TOPK = 10
LANES = 128
MASKED = -1e30
BF = jnp.bfloat16
F32 = jnp.float32


def nn(left, right):
    return lax.dot_general(left, right, (((1,), (0,)), ((), ())), preferred_element_type=F32)


def nt(left, right):
    return lax.dot_general(left, right, (((1,), (1,)), ((), ())), preferred_element_type=F32)


def tn(left, right):
    return lax.dot_general(left, right, (((0,), (0,)), ((), ())), preferred_element_type=F32)


def full(shape):
    return pl.BlockSpec(shape, lambda *_: (0,) * len(shape))


def params(mib=16):
    return pltpu.CompilerParams(vmem_limit_bytes=mib * 2**20)


def cost(flops, nbytes, exps=0):
    return pl.CostEstimate(flops=int(flops), bytes_accessed=int(nbytes), transcendentals=int(exps))


def rms_scale(x):
    return lax.rsqrt(jnp.mean(x * x, axis=-1, keepdims=True) + 1e-06)


def rms_back(x, gain, dy):
    scale = rms_scale(x)
    gain_grad = jnp.sum(dy * x * scale, axis=0, keepdims=True)
    inner = dy * gain
    mixed = jnp.mean(inner * x, axis=-1, keepdims=True)
    return scale * (inner - x * (scale * scale) * mixed), gain_grad


def proj_kernel(residual, x, gain, *refs):
    if residual:
        mixed, wo, w, mid, low, out = refs
    else:
        w, low, out = refs

    @pl.when(pl.program_id(0) == 0)
    def _():
        value = x[...].astype(F32)
        if residual:
            value = value + nn(mixed[...], wo[...])
            mid[...] = value
        low[...] = (value * rms_scale(value) * gain[...]).astype(BF)

    out[...] = nn(low[...], w[...]).astype(BF)


def project(x, gain, w, first, count, mixed=None, wo=None):
    t, d = x.shape
    residual = mixed is not None
    args = [x, gain]
    specs = [full((t, d)), full((1, d))]
    outs = [jax.ShapeDtypeStruct((t, d), BF), jax.ShapeDtypeStruct((count, t, d), BF)]
    out_specs = [full((t, d)), pl.BlockSpec((None, t, d), lambda j: (j, 0, 0))]
    if residual:
        args += [mixed, wo]
        specs += [full((t, d)), full((d, d))]
        outs = [jax.ShapeDtypeStruct((t, d), F32)] + outs
        out_specs = [full((t, d))] + out_specs
    args.append(w)
    specs.append(pl.BlockSpec((None, d, d), lambda j: (first + j, 0, 0)))
    return pl.pallas_call(
        functools.partial(proj_kernel, residual),
        grid=(count,),
        in_specs=specs,
        out_specs=out_specs,
        out_shape=outs,
        compiler_params=params(),
        cost_estimate=cost(2 * t * d * d * (count + residual), 2 * d * (t + d) * (count + 2)),
        name="project",
    )(*args)


def pairs_kernel(x, w, out):
    out[...] = nn(x[...], w[...]).astype(BF)


def project_plain(x, w, first, count):
    t, d = x.shape
    return pl.pallas_call(
        pairs_kernel,
        grid=(count,),
        in_specs=[full((t, d)), pl.BlockSpec((None, d, d), lambda j: (first + j, 0, 0))],
        out_specs=pl.BlockSpec((None, t, d), lambda j: (j, 0, 0)),
        out_shape=jax.ShapeDtypeStruct((count, t, d), BF),
        compiler_params=params(),
        cost_estimate=cost(2 * t * d * d * count, 2 * d * (t + d) * count),
        name="project_plain",
    )(x, w)


def proj_back_kernel(count, x, gain, grad, w, *refs):
    parts = refs[:count]
    new, low, gain_grad, total = refs[count:]
    step = pl.program_id(0)
    for j in range(count):

        @pl.when(step == j)
        def _(j=j):
            value = nt(parts[j][...], w[...])
            total[...] = value if j == 0 else total[...] + value

    @pl.when(step == count - 1)
    def _():
        back, gain_grad[...] = rms_back(x[...].astype(F32), gain[...], total[...])
        value = grad[...] + back
        new[...] = value
        low[...] = value.astype(BF)


def proj_back(x, gain, grad, w, parts):
    t, d = x.shape
    count = len(parts)
    return pl.pallas_call(
        functools.partial(proj_back_kernel, count),
        grid=(count,),
        in_specs=[full((t, d)), full((1, d)), full((t, d))]
        + [pl.BlockSpec((None, d, d), lambda j: (j, 0, 0))]
        + [full((t, d))] * count,
        out_specs=[full((t, d)), full((t, d)), full((1, d))],
        out_shape=[
            jax.ShapeDtypeStruct((t, d), F32),
            jax.ShapeDtypeStruct((t, d), BF),
            jax.ShapeDtypeStruct((1, d), F32),
        ],
        scratch_shapes=[pltpu.VMEM((t, d), F32)],
        compiler_params=params(),
        cost_estimate=cost(2 * t * d * d * count, 2 * d * (t + d) * count + 12 * t * d),
        name="proj_back",
    )(x, gain, grad, w, *parts)


GELU_A = 0.7978845608028654
GELU_B = 0.044715


def gelu_parts(pre):
    square = pre * pre
    half = 0.5 + 0.5 * jnp.tanh(pre * (GELU_A + (GELU_A * GELU_B) * square))
    act = pre * half
    slope = half + (act * (1.0 - half)) * (2 * GELU_A + (6 * GELU_A * GELU_B) * square)
    return act.astype(BF), slope.astype(BF)


def tiles_of(length):
    size = min(length, 256)
    return [slice(begin, begin + size) for begin in range(0, length, size)]


def ffn_kernel(res, mixed, wo, gain, w_in, w_out, mid, low, hidden, slope, out, total):
    step = pl.program_id(0)
    tiles = tiles_of(res.shape[0])

    @pl.when(step == 0)
    def _():
        for here in tiles:
            value = res[here, :].astype(F32) + nn(mixed[here, :], wo[...])
            mid[here, :] = value
            low[here, :] = (value * rms_scale(value) * gain[...]).astype(BF)
            total[here, :] = value

    coming = nn(low[tiles[0], :], w_in[...])
    for number, here in enumerate(tiles):
        pre = coming
        if number + 1 < len(tiles):
            coming = nn(low[tiles[number + 1], :], w_in[...])
        act, slope[here, :] = gelu_parts(pre)
        hidden[here, :] = act
        total[here, :] += nn(act, w_out[...])

    @pl.when(step == pl.num_programs(0) - 1)
    def _():
        for here in tiles:
            out[here, :] = total[here, :].astype(BF)


def ffn_forward(res, mixed, wo, gain, w_in, w_out, far=False, block=768):
    t, d = res.shape
    ff = w_in.shape[1]
    kept = pltpu.HBM if far else jax.ShapeDtypeStruct
    return pl.pallas_call(
        ffn_kernel,
        grid=(ff // block,),
        in_specs=[
            full((t, d)),
            full((t, d)),
            full((d, d)),
            full((1, d)),
            pl.BlockSpec((d, block), lambda j: (0, j)),
            pl.BlockSpec((block, d), lambda j: (j, 0)),
        ],
        out_specs=[
            full((t, d)),
            full((t, d)),
            pl.BlockSpec((t, block), lambda j: (0, j)),
            pl.BlockSpec((t, block), lambda j: (0, j)),
            full((t, d)),
        ],
        out_shape=[
            jax.ShapeDtypeStruct((t, d), F32),
            jax.ShapeDtypeStruct((t, d), BF),
            kept((t, ff), BF),
            kept((t, ff), BF),
            jax.ShapeDtypeStruct((t, d), BF),
        ],
        scratch_shapes=[pltpu.VMEM((t, d), F32)],
        compiler_params=params(28),
        cost_estimate=cost(2 * t * d * (2 * ff + d), 4 * d * ff + 4 * t * ff + 12 * t * d, t * ff),
        name="ffn_forward",
    )(res, mixed, wo, gain, w_in, w_out)


def ffn_back_kernel(sourced, *refs):
    if sourced:
        dk, dv, wk, wv, w_in, w_out, slope, mid, gain, pre_grad, g_low, new, low, gain_grad, g, total = refs
    else:
        grad, w_in, w_out, slope, mid, gain, pre_grad, g_low, new, low, gain_grad, g, total = refs
    step = pl.program_id(0)

    @pl.when(step == 0)
    def _():
        if sourced:
            value = nt(dk[...], wk[...]) + nt(dv[...], wv[...])
        else:
            value = grad[...].astype(F32)
        g[...] = value
        g_low[...] = value.astype(BF)
        total[...] = jnp.zeros_like(total)

    block = (nt(g_low[...], w_out[...]) * slope[...].astype(F32)).astype(BF)
    pre_grad[...] = block
    total[...] += nt(block, w_in[...])

    @pl.when(step == pl.num_programs(0) - 1)
    def _():
        back, gain_grad[...] = rms_back(mid[...], gain[...], total[...])
        value = g[...] + back
        new[...] = value
        low[...] = value.astype(BF)


def ffn_back(grads, weights, w_in, w_out, slope, mid, gain, block=512):
    t, d = mid.shape
    ff = w_in.shape[1]
    sourced = weights is not None
    if sourced:
        args = [grads[0], grads[1], weights, weights]
        specs = [
            full((t, d)),
            full((t, d)),
            pl.BlockSpec((None, d, d), lambda j: (1, 0, 0)),
            pl.BlockSpec((None, d, d), lambda j: (2, 0, 0)),
        ]
    else:
        args = [grads]
        specs = [full((t, d))]
    return pl.pallas_call(
        functools.partial(ffn_back_kernel, sourced),
        grid=(ff // block,),
        in_specs=specs
        + [
            pl.BlockSpec((d, block), lambda j: (0, j)),
            pl.BlockSpec((block, d), lambda j: (j, 0)),
            pl.BlockSpec((t, block), lambda j: (0, j)),
            full((t, d)),
            full((1, d)),
        ],
        out_specs=[
            pl.BlockSpec((t, block), lambda j: (0, j)),
            full((t, d)),
            full((t, d)),
            full((t, d)),
            full((1, d)),
        ],
        out_shape=[
            jax.ShapeDtypeStruct((t, ff), BF),
            jax.ShapeDtypeStruct((t, d), BF),
            jax.ShapeDtypeStruct((t, d), F32),
            jax.ShapeDtypeStruct((t, d), BF),
            jax.ShapeDtypeStruct((1, d), F32),
        ],
        scratch_shapes=[pltpu.VMEM((t, d), F32), pltpu.VMEM((t, d), F32)],
        compiler_params=params(32),
        cost_estimate=cost(4 * t * d * ff, 4 * d * ff + 4 * t * ff + 16 * t * d),
        name="ffn_back",
    )(*args, w_in, w_out, slope, mid, gain)


def fill_bias(q_seg, k_seg, bias, causal, rows):
    length, width = bias.shape
    for begin in range(0, length, rows):
        allowed = q_seg[begin : begin + rows, :] == k_seg[...]
        if causal:
            at = lax.broadcasted_iota(jnp.int32, (rows, width), 0) + begin
            key = lax.broadcasted_iota(jnp.int32, (rows, width), 1)
            allowed = allowed & (key <= at)
        bias[begin : begin + rows, :] = jnp.where(allowed, 0.0, MASKED)


def join_keys(refs, count, extra, width):
    keys, values, mem_keys, mem_values, all_keys, all_values = refs
    for source, more, target in ((keys, mem_keys, all_keys), (values, mem_values, all_values)):
        target[:count, :] = source[...]
        target[count : count + extra, :] = more[...]


def attend_kernel(extra, causal, rows, *refs):
    if extra:
        q_seg, k_seg, q, k, v, mk, mv, out, logs, bias, ks, vs = refs
    else:
        q_seg, k_seg, q, k, v, out, logs, bias = refs
    length, width = bias.shape
    count = k.shape[0]
    step = pl.program_id(0)

    @pl.when(step == 0)
    def _():
        fill_bias(q_seg, k_seg, bias, causal, rows)
        logs[...] = jnp.zeros_like(logs)
        if extra:
            ks[count:, :] = jnp.zeros((width - count, LANES), BF)
            vs[count:, :] = jnp.zeros((width - count, LANES), BF)

    if extra:
        join_keys((k, v, mk, mv, ks, vs), count, extra, width)
        k, v = ks, vs
    lane = lax.broadcasted_iota(jnp.int32, (rows, LANES), 1)

    def scores_of(begin, head):
        here = slice(begin, begin + rows)
        mine = (lane < HD) if head == 0 else (lane >= HD)
        queries = jnp.where(mine, q[here, :] * BF(HD**-0.5), BF(0))
        return nt(queries, k[...]) + bias[here, :]

    work = [(begin, head) for begin in range(0, length, rows) for head in range(2)]
    coming = scores_of(*work[0])
    for number, (begin, head) in enumerate(work):
        scores = coming
        if number + 1 < len(work):
            coming = scores_of(*work[number + 1])
        top = jnp.max(scores, axis=1, keepdims=True)
        exponent = jnp.exp(scores - top)
        sums = jnp.sum(exponent, axis=1, keepdims=True)
        side = nn(exponent.astype(BF), v[...]) * (1.0 / sums)
        here = slice(begin, begin + rows)
        kept = logs[here, :] if head == 0 else kept
        kept = jnp.where(lane == 2 * step + head, top + jnp.log(sums), kept)
        if head == 0:
            first = side
        else:
            logs[here, :] = kept
            out[here, :] = jnp.where(lane < HD, first, side).astype(BF)


def part_of(stack, index):
    rows = stack.shape[1]
    return pl.BlockSpec((None, rows, LANES), lambda p: (index, 0, p))


def attend(q, k, v, q_seg, k_seg, memory=None, causal=False, rows=256):
    t, d = q[0].shape[1:]
    count = k[0].shape[1]
    width = k_seg.shape[1]
    args = [q_seg, k_seg, q[0], k[0], v[0]]
    specs = [full(q_seg.shape), full(k_seg.shape), part_of(*q), part_of(*k), part_of(*v)]
    scratch = [pltpu.VMEM((t, width), F32)]
    extra = 0
    if memory is not None:
        extra = memory.shape[1]
        args += [memory, memory]
        specs += [part_of(memory, 0), part_of(memory, 1)]
        scratch += [pltpu.VMEM((width, LANES), BF)] * 2
    return pl.pallas_call(
        functools.partial(attend_kernel, extra, causal, rows),
        grid=(d // LANES,),
        in_specs=specs,
        out_specs=[pl.BlockSpec((t, LANES), lambda p: (0, p)), full((t, LANES))],
        out_shape=[jax.ShapeDtypeStruct((t, d), BF), jax.ShapeDtypeStruct((t, LANES), F32)],
        scratch_shapes=scratch,
        compiler_params=params(),
        cost_estimate=cost(16 * t * width * d, 8 * d * (t + count), t * width * d // HD),
        name="attend",
    )(*args)


def attend_back_kernel(extra, causal, rows, *refs):
    if extra:
        q_seg, k_seg, q, k, v, out, logs, grad, wo, mk, mv = refs[:11]
        dq, dk, dv, dmk, dmv, bias, dks, dvs, ks, vs = refs[11:]
    else:
        q_seg, k_seg, q, k, v, out, logs, grad, wo, dq, dk, dv, bias, dks, dvs = refs
    length, width = bias.shape
    count = k.shape[0]
    step = pl.program_id(0)

    @pl.when(step == 0)
    def _():
        fill_bias(q_seg, k_seg, bias, causal, rows)
        if extra:
            ks[count:, :] = jnp.zeros((width - count, LANES), BF)
            vs[count:, :] = jnp.zeros((width - count, LANES), BF)

    if extra:
        join_keys((k, v, mk, mv, ks, vs), count, extra, width)
        k, v = ks, vs
    lane = lax.broadcasted_iota(jnp.int32, (rows, LANES), 1)
    for begin in range(0, length, rows):
        here = slice(begin, begin + rows)
        queries = q[here, :] * BF(HD**-0.5)
        mixed = nt(grad[here, :], wo[...]).astype(BF)
        product = mixed.astype(F32) * out[here, :].astype(F32)
        kept = logs[here, :]
        sides = []
        for head in range(2):
            mine = (lane < HD) if head == 0 else (lane >= HD)
            own_q = jnp.where(mine, queries, BF(0))
            own_grad = jnp.where(mine, mixed, BF(0))
            log_sum = jnp.sum(jnp.where(lane == 2 * step + head, kept, 0.0), axis=1, keepdims=True)
            center = jnp.sum(jnp.where(mine, product, 0.0), axis=1, keepdims=True)
            probs = jnp.exp(nt(own_q, k[...]) + bias[here, :] - log_sum)
            score_grad = (probs * (nt(own_grad, v[...]) - center)).astype(BF)
            sides.append(nn(score_grad, k[...]))
            value_part = nn(own_grad.T, probs.astype(BF))
            key_part = nn(own_q.T, score_grad)
            if begin == 0 and head == 0:
                dvs[...] = value_part
                dks[...] = key_part
            else:
                dvs[...] += value_part
                dks[...] += key_part
        dq[here, :] = (jnp.where(lane < HD, sides[0], sides[1]) * HD**-0.5).astype(BF)
    dk[...] = dks[:, :count].T.astype(BF)
    dv[...] = dvs[:, :count].T.astype(BF)
    if extra:
        dmk[...] = dks[:, count:].T[:extra].astype(BF)
        dmv[...] = dvs[:, count:].T[:extra].astype(BF)


def attend_back(q, k, v, out, logs, grad, wo, q_seg, k_seg, memory=None, causal=False, rows=256):
    t, d = q[0].shape[1:]
    count = k[0].shape[1]
    width = k_seg.shape[1]
    column = lambda n: pl.BlockSpec((n, LANES), lambda p: (0, p))
    args = [q_seg, k_seg, q[0], k[0], v[0], out, logs, grad, wo]
    specs = [full(q_seg.shape), full(k_seg.shape), part_of(*q), part_of(*k), part_of(*v)]
    specs += [column(t), full((t, LANES)), full((t, d)), pl.BlockSpec((LANES, d), lambda p: (p, 0))]
    scratch = [pltpu.VMEM((t, width), F32)] + [pltpu.VMEM((LANES, width), F32)] * 2
    lengths = [t, count, count]
    extra = 0
    if memory is not None:
        extra = memory.shape[1]
        args += [memory, memory]
        specs += [part_of(memory, 0), part_of(memory, 1)]
        scratch += [pltpu.VMEM((width, LANES), BF)] * 2
        lengths += [extra, extra]
    return pl.pallas_call(
        functools.partial(attend_back_kernel, extra, causal, rows),
        grid=(d // LANES,),
        in_specs=specs,
        out_specs=[column(n) for n in lengths],
        out_shape=[jax.ShapeDtypeStruct((n, d), BF) for n in lengths],
        scratch_shapes=scratch,
        compiler_params=params(),
        cost_estimate=cost(32 * t * width * d, 12 * d * (t + count), t * width * d // HD),
        name="attend_back",
    )(*args)


def share_rows(index, acc, out, shards, size):
    for turn in range(shards):
        shard = index[0] ^ turn
        start = pl.multiple_of(shard * size, 16)
        out[turn] = acc[pl.ds(start, size), :].astype(BF)


def squares_kernel(items, shards, index, *refs):
    out, acc = refs[-2:]
    size = acc.shape[0] // shards
    for j, (a, g) in enumerate(items):

        @pl.when(pl.program_id(0) == j)
        def _(a=a, g=g):
            acc[...] = tn(refs[g][...], refs[a][...])
            share_rows(index, acc, out, shards, size)


def pad_rows(rows):
    return -(-rows // CHUNK) * CHUNK


def square_grads(place, products):
    arrays, items = [], []

    def at(array):
        for i, other in enumerate(arrays):
            if other is array:
                return i
        arrays.append(array)
        return len(arrays) - 1

    for acts, grads in products:
        for grad in grads:
            items.append((at(acts), at(grad)))
    shards = place.sizes["dp"]
    d = products[0][0].shape[1]
    size = d // shards
    work = sum(2 * arrays[a].shape[0] * d * d for a, _ in items)
    return pl.pallas_call(
        functools.partial(squares_kernel, items, shards),
        grid=(len(items),),
        in_specs=[pl.BlockSpec(memory_space=pltpu.SMEM)] + [full(x.shape) for x in arrays],
        out_specs=pl.BlockSpec((shards, size, d), lambda j: (0, j, 0)),
        out_shape=jax.ShapeDtypeStruct((shards, pad_rows(len(items) * size), d), BF),
        scratch_shapes=[pltpu.VMEM((d, d), F32)],
        compiler_params=params(),
        cost_estimate=cost(work, sum(2 * x.size for x in arrays) + 2 * len(items) * d * d),
        name="square_grads",
    )(place.index, *arrays)


def out_kernel(shards, index, acts, grad, out, acc):
    acc[...] = tn(grad[...], acts[...])
    share_rows(index, acc, out, shards, acc.shape[0] // shards)


def ff_out_grads(place, acts, grad):
    shards = place.sizes["dp"]
    t, d = grad.shape
    blocks = acts.shape[1] // d
    size = d // shards
    return pl.pallas_call(
        functools.partial(out_kernel, shards),
        grid=(blocks,),
        in_specs=[
            pl.BlockSpec(memory_space=pltpu.SMEM),
            pl.BlockSpec((t, d), lambda j: (0, j)),
            full((t, d)),
        ],
        out_specs=pl.BlockSpec((shards, size, d), lambda j: (0, j, 0)),
        out_shape=jax.ShapeDtypeStruct((shards, blocks * size, d), BF),
        scratch_shapes=[pltpu.VMEM((d, d), F32)],
        compiler_params=params(),
        cost_estimate=cost(2 * t * d * d * blocks, 2 * (t + d) * d * (blocks + 1)),
        name="ff_out_grads",
    )(place.index, acts, grad)


def in_kernel(per_block, index, grad, acts, out):
    acc = tn(grad[...], acts[...]).astype(BF)
    size = acc.shape[0] // per_block
    for i in range(per_block):
        shard = pl.program_id(0) * per_block + i
        out[index[0] ^ shard] = acc[i * size : (i + 1) * size]


def ff_in_grads(place, acts, grad):
    shards = place.sizes["dp"]
    t, d = acts.shape
    ff = grad.shape[1]
    blocks = ff // d
    size = ff // shards
    return pl.pallas_call(
        functools.partial(in_kernel, d // size),
        grid=(blocks,),
        in_specs=[
            pl.BlockSpec(memory_space=pltpu.SMEM),
            pl.BlockSpec((t, d), lambda j: (0, j)),
            full((t, d)),
        ],
        out_specs=full((shards, size, d)),
        out_shape=jax.ShapeDtypeStruct((shards, size, d), BF),
        compiler_params=params(),
        cost_estimate=cost(2 * t * d * ff, 2 * (t + d) * d * (blocks + 1)),
        name="ff_in_grads",
    )(place.index, grad, acts)


def ffn_back_weights_kernel(
    index, grad, w_in, w_out, slope, hidden, low_in, mid, gain,
    new, low, gain_grad, out_part, in_part, total, acc,
):
    step = pl.program_id(0)

    @pl.when(step == 0)
    def _():
        total[...] = jnp.zeros_like(total)

    acc[...] = tn(grad[...], hidden[...])
    share_rows(index, acc, out_part, out_part.shape[0], out_part.shape[1])
    block = (nt(grad[...], w_out[...]) * slope[...].astype(F32)).astype(BF)
    total[...] += nt(block, w_in[...])
    in_part[index[0] ^ step] = tn(low_in[...], block).astype(BF)

    @pl.when(step == pl.num_programs(0) - 1)
    def _():
        back, gain_grad[...] = rms_back(mid[...], gain[...], total[...])
        value = grad[...].astype(F32) + back
        new[...] = value
        low[...] = value.astype(BF)


def ffn_back_weights(place, grad, w_in, w_out, slope, hidden, low_in, mid, gain):
    t, d = mid.shape
    blocks = w_in.shape[1] // d
    shards = place.sizes["dp"]
    size = d // shards
    return pl.pallas_call(
        ffn_back_weights_kernel,
        grid=(blocks,),
        in_specs=[
            pl.BlockSpec(memory_space=pltpu.SMEM),
            full((t, d)),
            pl.BlockSpec((d, d), lambda j: (0, j)),
            pl.BlockSpec((d, d), lambda j: (j, 0)),
            pl.BlockSpec((t, d), lambda j: (0, j)),
            pl.BlockSpec((t, d), lambda j: (0, j)),
            full((t, d)),
            full((t, d)),
            full((1, d)),
        ],
        out_specs=[
            full((t, d)),
            full((t, d)),
            full((1, d)),
            pl.BlockSpec((shards, size, d), lambda j: (0, j, 0)),
            full((shards, d, d)),
        ],
        out_shape=[
            jax.ShapeDtypeStruct((t, d), F32),
            jax.ShapeDtypeStruct((t, d), BF),
            jax.ShapeDtypeStruct((1, d), F32),
            pltpu.HBM((shards, blocks * size, d), BF),
            pltpu.HBM((shards, d, d), BF),
        ],
        scratch_shapes=[pltpu.VMEM((t, d), F32), pltpu.VMEM((d, d), F32)],
        compiler_params=params(32),
        cost_estimate=cost(8 * t * d * d * blocks, 8 * d * d * blocks + 24 * t * d),
        name="ffn_back_weights",
    )(place.index, grad, w_in, w_out, slope, hidden, low_in, mid, gain)


def flip(index, bit):
    return index + bit - 2 * bit * ((index // bit) % 2)


class Place:
    def __init__(self, sizes):
        self.sizes = sizes
        self.dp = lax.axis_index("dp")
        self.row = lax.axis_index("row")
        self.index = self.dp.astype(jnp.int32)[None]

    def swap(self, value, axis, turn):
        return lax.ppermute(value, axis, [(i, i ^ turn) for i in range(self.sizes[axis])])

    def bits(self, axis):
        return [1 << i for i in range(self.sizes[axis].bit_length() - 1)]


QUARTER = 48
CHUNK = 4 * QUARTER
AHEAD = 3
DELAY = 4
FAR_RING = DELAY + 2
Y_RING = DELAY + 4
RING = 5
MESH_ID = pl.DeviceIdType.MESH


def add(left, right):
    return (left.astype(F32) + right.astype(F32)).astype(BF)


class Step:
    def __init__(self, value, low=None, high=None):
        self.value = value
        self.low = value if low is None else low
        self.high = value if high is None else high

    def __add__(self, other):
        return Step(self.value + other, self.low + other, self.high + other)


def within(step, low, high):
    if low <= step.low and step.high < high:
        return lambda function: function()
    if step.high < low or step.low >= high:
        return lambda function: None
    return pl.when((step.value >= low) & (step.value < high))


class Reducer:
    def __init__(self, groups, counts, row_bits, out, refs):
        self.groups, self.counts, self.out = groups, counts, out
        self.total = sum(counts)
        others = len(row_bits) - 2
        (self.own, self.core_in, self.far, self.near, self.y_in, self.x_in, self.z_in, self.kept) = refs[:8]
        self.w_in = refs[8 : 8 + others]
        sems = list(refs[8 + others :])
        self.load_sem, self.kept_sem, self.core_send, self.core_recv = sems[:4]
        self.core_free, self.send_sem, self.recv, self.free = sems[4], sems[5::3], sems[6::3], sems[7::3]
        row, dp = lax.axis_index("row"), lax.axis_index("dp")
        self.x, self.z = row % 2, (row // 2) % 2
        self.core_peer = (row, flip(dp, 1))
        self.y_peer = (row, flip(dp, 2))
        self.row_peers = [(flip(row, bit), dp) for bit in row_bits]
        self.x_peer, self.z_peer = self.row_peers[:2]
        self.peers = [self.core_peer, self.y_peer] + self.row_peers
        self.stages = [self.y_stage, self.x_stage, self.z_stage]
        self.stages += [functools.partial(self.w_stage, i) for i in range(others)]
        self.stages += [self.back_z_stage, self.back_x_stage]
        self.steps = self.total + DELAY + len(self.stages) - 1

    @staticmethod
    def scratch(row_bits, d):
        others = len(row_bits) - 2
        chunk = (2, 2, QUARTER, d)
        shapes = [
            (AHEAD, 2) + chunk,
            (AHEAD, 2) + chunk,
            (FAR_RING,) + chunk,
            (FAR_RING,) + chunk,
            (Y_RING,) + chunk,
            (RING,) + chunk[1:],
            (RING,) + chunk[2:],
            (RING,) + chunk[2:],
        ] + [(RING,) + chunk[2:]] * others
        dma = pltpu.SemaphoreType.DMA
        regular = pltpu.SemaphoreType.REGULAR
        rings = [Y_RING, RING, RING] + [RING] * others + [RING, RING]
        sems = [dma((AHEAD, 2)), dma((RING,)), dma((AHEAD, 2)), dma((AHEAD, 2)), regular]
        for ring in rings:
            sems += [dma((ring,)), dma((ring,)), regular]
        return [pltpu.VMEM(shape, BF) for shape in shapes] + sems

    def greet(self):
        barrier = pltpu.get_barrier_semaphore()
        for peer in self.peers:
            pl.semaphore_signal(barrier, inc=1, device_id=peer, device_id_type=MESH_ID)
        pl.semaphore_wait(barrier, len(self.peers))

    def start(self):
        for c in range(min(AHEAD, self.total)):
            self.begin(Step(c))

    def send(self, t):
        @within(t, 0, self.total)
        def _():
            self.core_stage(t)

    def step(self, t):
        for i, stage in enumerate(self.stages):
            c = t + (-DELAY - i)

            @within(c, 0, self.total)
            def _(c=c, stage=stage):
                stage(c)

    def load_next(self, t):
        @within(t, 0, self.total - AHEAD)
        def _():
            pl.semaphore_wait(self.core_free, 1)
            self.begin(t + AHEAD)

    def remote(self, stage, ring, c, source, target, peer):
        return pltpu.make_async_remote_copy(
            src_ref=source,
            dst_ref=target,
            send_sem=self.send_sem[stage].at[c.value % ring],
            recv_sem=self.recv[stage].at[c.value % ring],
            device_id=peer,
            device_id_type=MESH_ID,
        )

    def give(self, stage, ring, c, peer):
        @within(c, 0, self.total - ring)
        def _():
            pl.semaphore_signal(
                self.free[stage], inc=1, device_id=peer, device_id_type=MESH_ID
            )

    def take(self, stage, ring, c):
        @within(c, ring, self.total)
        def _():
            pl.semaphore_wait(self.free[stage], 1)

    def core_copy(self, c, side, source):
        return pltpu.make_async_remote_copy(
            src_ref=source,
            dst_ref=self.core_in.at[c.value % AHEAD, side],
            send_sem=self.core_send.at[c.value % AHEAD, side],
            recv_sem=self.core_recv.at[c.value % AHEAD, side],
            device_id=self.core_peer,
            device_id_type=MESH_ID,
        )

    def load(self, c, side, source):
        return pltpu.make_async_copy(
            source, self.own.at[c.value % AHEAD, side], self.load_sem.at[c.value % AHEAD, side]
        )

    def begin(self, c):
        first = 0
        for group, count in zip(self.groups, self.counts):

            @within(c, first, first + count)
            def _(group=group, first=first):
                at = c.value - first
                for side in range(2):
                    self.core_copy(c, side, group.at[2 * side + 1, at]).start()
                for side in range(2):
                    self.load(c, side, group.at[2 * side, at]).start()

            first += count

    def y_copy(self, c):
        return self.remote(0, Y_RING, c, self.far.at[c.value % FAR_RING], self.y_in.at[c.value % Y_RING], self.y_peer)

    def x_copy(self, c):
        source = self.y_in.at[c.value % Y_RING, 1 - self.x]
        return self.remote(1, RING, c, source, self.x_in.at[c.value % RING], self.x_peer)

    def z_copy(self, c):
        source = self.x_in.at[c.value % RING, 1 - self.z]
        return self.remote(2, RING, c, source, self.z_in.at[c.value % RING], self.z_peer)

    def w_copy(self, i, c):
        source = self.z_in if i == 0 else self.w_in[i - 1]
        return self.remote(
            3 + i, RING, c, source.at[c.value % RING], self.w_in[i].at[c.value % RING], self.row_peers[2 + i]
        )

    def back_z_copy(self, c, place):
        at = self.out.at[c.value, self.x, place]
        return self.remote(3 + len(self.w_in), RING, c, self.kept.at[c.value % RING], at, self.z_peer)

    def kept_copy(self, c):
        at = self.out.at[c.value, self.x, self.z]
        return pltpu.make_async_copy(self.kept.at[c.value % RING], at, self.kept_sem.at[c.value % RING])

    def back_x_copy(self, c, place):
        at = self.out.at[c.value, place]
        return self.remote(4 + len(self.w_in), RING, c, at, at, self.x_peer)

    def core_stage(self, c):
        slot, at = c.value % AHEAD, c.value % FAR_RING
        for side in range(2):
            self.load(c, side, self.own.at[slot, side]).wait()
            self.core_copy(c, side, self.own.at[slot, side]).wait()
        self.far[at] = add(self.own[slot, 1], self.core_in[slot, 1])
        self.take(0, Y_RING, c)
        self.y_copy(c).start()
        self.near[at] = add(self.own[slot, 0], self.core_in[slot, 0])

        @within(c, 0, self.total - AHEAD)
        def _():
            pl.semaphore_signal(
                self.core_free, inc=1, device_id=self.core_peer, device_id_type=MESH_ID
            )

    def y_stage(self, c):
        self.y_copy(c).wait()
        slot = c.value % Y_RING
        self.y_in[slot] = add(self.y_in[slot], self.near[c.value % FAR_RING])
        self.take(1, RING, c)
        self.x_copy(c).start()

    def x_stage(self, c):
        self.x_copy(c).wait()
        slot = c.value % RING
        self.x_in[slot] = add(self.x_in[slot], self.y_in[c.value % Y_RING, self.x])
        self.give(0, Y_RING, c, self.y_peer)
        self.take(2, RING, c)
        self.z_copy(c).start()

    def z_stage(self, c):
        self.z_copy(c).wait()
        slot = c.value % RING
        self.z_in[slot] = add(self.z_in[slot], self.x_in[slot, self.z])
        self.give(1, RING, c, self.x_peer)
        self.take(3, RING, c)
        self.w_copy(0, c).start()

    def w_stage(self, i, c):
        self.w_copy(i, c).wait()
        slot = c.value % RING
        source = self.z_in if i == 0 else self.w_in[i - 1]
        value = add(self.w_in[i][slot], source[slot])
        giver = self.z_peer if i == 0 else self.row_peers[1 + i]
        self.give(2 + i, RING, c, giver)
        if i + 1 < len(self.w_in):
            self.w_in[i][slot] = value
            self.take(4 + i, RING, c)
            self.w_copy(i + 1, c).start()
        else:
            self.kept[slot] = value
            self.give(3 + i, RING, c, self.row_peers[2 + i])
            self.kept_copy(c).start()
            self.back_z_copy(c, self.z).start()

    def back_z_stage(self, c):
        self.kept_copy(c).wait()
        self.back_z_copy(c, self.z).wait_send()
        self.back_z_copy(c, 1 - self.z).wait_recv()
        self.back_x_copy(c, self.x).start()

    def back_x_stage(self, c):
        self.back_x_copy(c, self.x).wait_send()
        self.back_x_copy(c, 1 - self.x).wait_recv()


def reduce_kernel(counts, row_bits, *refs):
    count = len(counts)
    reducer = Reducer(refs[:count], counts, row_bits, refs[count], refs[count + 1 :])
    reducer.greet()
    reducer.start()

    def step(t, carry):
        t = Step(t, 0, reducer.steps - 1)
        reducer.send(t)
        reducer.step(t)
        reducer.load_next(t)
        return carry

    lax.fori_loop(0, reducer.steps, step, 0)


def chunk_view(group):
    turns, rows, d = group.shape
    return group.reshape(turns, rows // CHUNK, 2, 2, QUARTER, d)


def split_sums(result, counts):
    d = result.shape[-1]
    sums, first = [], 0
    for n in counts:
        sums.append(result[first : first + n].reshape(n * CHUNK, d))
        first += n
    return sums


def reduce_all(place, groups):
    d = groups[0].shape[-1]
    counts = [g.shape[1] // CHUNK for g in groups]
    row_bits = place.bits("row")
    result = pl.pallas_call(
        functools.partial(reduce_kernel, counts, row_bits),
        in_specs=[pl.BlockSpec(memory_space=pl.ANY)] * len(groups),
        out_specs=pl.BlockSpec(memory_space=pl.ANY),
        out_shape=jax.ShapeDtypeStruct((sum(counts), 2, 2, QUARTER, d), BF),
        scratch_shapes=Reducer.scratch(row_bits, d),
        compiler_params=pltpu.CompilerParams(
            collective_id=0, has_side_effects=True, vmem_limit_bytes=48 * 2**20
        ),
        cost_estimate=cost(0, 4 * sum(counts) * CHUNK * d),
        name="reduce_all",
    )(*[chunk_view(g) for g in groups])
    return split_sums(result, counts)


def xor(left, right, bits):
    total = 0
    for bit in bits:
        a, b = (left // bit) % 2, (right // bit) % 2
        total = total + bit * (a + b - 2 * a * b)
    return total


HALF = 2 * CHUNK


def pair_back(pair, width, q, k, v, grad, wo, mixed, logs, bias, dks, dvs, put):
    length = logs.shape[0]
    for number, here in enumerate(tiles_of(length)):
        lane = lax.broadcasted_iota(jnp.int32, (here.stop - here.start, LANES), 1)
        queries = q(here) * BF(HD**-0.5)
        grads = nt(grad[here, :], wo).astype(BF)
        product = grads.astype(F32) * mixed(here).astype(F32)
        kept = logs[here, :]
        sides = []
        for head in range(2):
            mine = (lane < HD) if head == 0 else (lane >= HD)
            own_q = jnp.where(mine, queries, BF(0))
            own_grad = jnp.where(mine, grads, BF(0))
            chosen = lane == 2 * pair + head
            log_sum = jnp.sum(jnp.where(chosen, kept, 0.0), axis=1, keepdims=True)
            center = jnp.sum(jnp.where(mine, product, 0.0), axis=1, keepdims=True)
            probs = jnp.exp(nt(own_q, k) + bias[here, :width] - log_sum)
            score_grad = (probs * (nt(own_grad, v) - center)).astype(BF)
            sides.append(nn(score_grad, k))
            value_part = nn(own_grad.T, probs.astype(BF))
            key_part = nn(own_q.T, score_grad)
            if number == 0 and head == 0:
                dvs[:, :width] = value_part
                dks[:, :width] = key_part
            else:
                dvs[:, :width] += value_part
                dks[:, :width] += key_part
        put(here, (jnp.where(lane < HD, sides[0], sides[1]) * HD**-0.5).astype(BF))


NEAR = (
    "dec_q_seg", "enc_k_seg", "dec_k_seg", "enc_q_seg", "all_k_seg", "cross_q", "cross_mixed",
    "cross_logs", "cross_low", "dec_low", "memory", "ffn_gain_grad", "enc_gain", "dec_gain",
)
LATER = (
    "mid_low", "enc_mixed", "enc_logs", "fetched", "self_proj", "self_mixed", "self_logs",
    "self_low", "dec_new", "first", "answers",
)
FAR = (
    "encoded", "pairs", "cross", "cross_out", "mid", "tokens", "dec_qkv", "w_in", "w_out", "slope",
    "hidden", "enc_low", "w_qkv", "enc_proj", "attn_out", "self_out",
)


class Named:
    pass


def backward_kernel(counts, row_bits, memories, *refs):
    x, refs = Named(), list(refs)
    for name in NEAR + FAR:
        setattr(x, name, refs.pop(0))
    later_sources = [refs.pop(0) for _ in LATER]
    groups = [refs.pop(0) for _ in counts]
    out, cross_part, ff_out_part, ff_in_part, squares_part, self_part = refs[:6]
    token_grad, answer_grad, gain_sums = refs[6:9]
    (g, total, acc, low, g_low, pg, dq, dk, dv, dmk, dmv, bias, ks, vs, dks, dvs) = refs[9:25]
    (b0, b1, b2, b3, dcq, new2, low2, stage_a, stage_b) = refs[25:34]
    gain_acc, gain_in, copy_sem, later_sem, gain_send, gain_recv = refs[34:40]
    refs = refs[40:]
    later_targets = [refs.pop(0) for _ in LATER]
    for name, target in zip(LATER, later_targets):
        setattr(x, name, target)
    parts = [cross_part, ff_out_part, ff_in_part, squares_part, self_part]
    all_counts = list(counts) + [part.shape[1] for part in parts]
    reducer = Reducer(list(groups) + parts, all_counts, row_bits, out, refs)
    me = lax.axis_index("dp")
    d = g.shape[1]
    length, dec_length, count, width = g.shape[0], dcq.shape[0], b1.shape[0], bias.shape[1]
    blocks, pairs = ff_out_part.shape[1], d // LANES
    tiles = tiles_of(length)
    dsq, dsk, dsv = [g_low.at[i * dec_length : (i + 1) * dec_length] for i in range(3)]

    def fetch(source, target, i):
        return pltpu.make_async_copy(source, target, copy_sem.at[i])

    def lanes_of(pair):
        return pl.ds(pl.multiple_of(pair * LANES, LANES), LANES)

    later = [
        pltpu.make_async_copy(source, target, later_sem.at[i])
        for i, (source, target) in enumerate(zip(later_sources, later_targets))
    ]
    first_loads = [
        fetch(x.pairs.at[0], b1, 7),
        fetch(x.pairs.at[1], b2, 8),
        fetch(x.cross_out, b3, 9),
    ]
    encoded_load = fetch(x.encoded, b0, 6)
    early = [fetch(x.cross.at[1], dv, 0), fetch(x.cross.at[2], pg, 1), fetch(x.mid, token_grad, 2)]
    attend_loads = [
        fetch(x.enc_proj.at[0], b0, 6),
        fetch(x.enc_proj.at[1], b1, 7),
        fetch(x.enc_proj.at[2], b2, 8),
        fetch(x.attn_out, b3, 9),
    ]
    low_load = fetch(x.enc_low, b0, 6)
    qkv_loads = [fetch(x.w_qkv.at[i], target, 7 + i) for i, target in enumerate((b1, b2, b3))]
    tokens_load = fetch(x.tokens, pg, 10)
    cross_load = fetch(x.cross.at[0], b0, 6)
    self_out_load = fetch(x.self_out, low, 3)
    dec_qkv_loads = [fetch(x.dec_qkv.at[i], target, 11 + i) for i, target in enumerate((dq, dk, dv))]

    def ff_blocks(j):
        lanes = pl.ds(pl.multiple_of(j * d, d), d)
        return [
            fetch(x.w_in.at[:, lanes], b0, 6),
            fetch(x.w_out.at[lanes], b1, 7),
            fetch(x.slope.at[:, lanes], b2, 8),
            fetch(x.hidden.at[:, lanes], b3, 9),
        ]

    def start_all(copies):
        for copy in copies:
            copy.start()

    def wait_all(copies):
        for copy in copies:
            copy.wait()

    def product_to_acc(acts, grads):
        for n in range(0, d, HALF):
            acc[n : n + HALF, :] = tn(grads[:, n : n + HALF], acts[...])

    def shares(stage):
        for turn in range(4):
            shard = xor(me, turn, (1, 2))
            for i in range(4):
                start = pl.multiple_of(shard * CHUNK + i * QUARTER, 16)
                stage[turn, i // 2, i % 2] = acc[pl.ds(start, QUARTER), :].astype(BF)

    now = [0]

    def once(compute, copies=()):
        t = Step(now[0])
        now[0] += 1
        reducer.send(t)
        compute()
        start_all(copies)
        reducer.step(t)
        wait_all(copies)
        reducer.load_next(t)

    def loop(number, compute, copies=lambda i: ()):
        first = now[0]
        now[0] += number

        def body(i, carry):
            t = Step(first + i, first, first + number - 1)
            reducer.send(t)
            compute(i)
            reducer.step(t)
            wait_all(copies(i))
            reducer.load_next(t)
            return carry

        lax.fori_loop(0, number, body, 0)

    def squares(part, items, before=None, after=None):
        for n in range(0, len(items), 2):

            def compute(n=n):
                if n == 0 and before:
                    before()
                for stage, (acts, grads) in zip((stage_a, stage_b), items[n : n + 2]):
                    product_to_acc(acts, grads)
                    shares(stage)
                if n + 2 >= len(items) and after:
                    after()

            once(
                compute,
                [fetch(stage_a, part.at[:, n], 4), fetch(stage_b, part.at[:, n + 1], 5)],
            )

    start_all(first_loads)
    encoded_load.start()
    start_all(early)
    start_all(later)
    reducer.greet()
    reducer.start()
    ks[count:, :] = jnp.zeros((width - count, LANES), BF)
    vs[count:, :] = jnp.zeros((width - count, LANES), BF)
    gain_acc[0] = jnp.zeros_like(gain_acc[0])
    gain_acc[0, 4:5, :] = x.ffn_gain_grad[...]
    fill_bias(x.dec_q_seg, x.enc_k_seg, bias.at[:dec_length, :count], False, dec_length)
    wait_all(first_loads)

    def cross_attention(i):
        for side in range(2):
            pair = 2 * i + side
            lanes = lanes_of(pair)

            def put(here, value):
                dcq[here, lanes] = value

            pair_back(
                pair, count, lambda here: x.cross_q[0, here, lanes], b1[:, lanes], b2[:, lanes],
                x.dec_low, b3[lanes, :], lambda here: x.cross_mixed[here, lanes], x.cross_logs,
                bias, dks, dvs, put,
            )
            dq[:, lanes] = dks[:, :count].T.astype(BF)
            dk[:, lanes] = dvs[:, :count].T.astype(BF)

    loop(pairs // 2, cross_attention)
    squares(
        cross_part,
        [(x.cross_mixed, x.dec_low), (x.cross_low, dcq), (b0, dq), (b0, dk)],
        encoded_load.wait,
        lambda: start_all(ff_blocks(0)),
    )

    wait_all(early)
    wait_all(later)
    for here in tiles:
        value = nt(dq[here, :], dv[...]) + nt(dk[here, :], pg[...])
        g[here, :] = value
        g_low[here, :] = value.astype(BF)
        total[here, :] = jnp.zeros_like(value)

    def ff_copies(j):
        return [
            fetch(stage_a, ff_out_part.at[:, j], 4),
            fetch(stage_b, ff_in_part.at[xor(me, j, (1, 2))], 5),
        ]

    def feed_forward(j):
        wait_all(ff_blocks(j))
        for here in tiles:
            block = (nt(g_low[here, :], b1[...]) * b2[here, :].astype(F32)).astype(BF)
            pg[here, :] = block
            total[here, :] += nt(block, b0[...])
        product_to_acc(b3, g_low)
        shares(stage_a)
        for n in range(0, d, HALF):
            value = tn(x.mid_low[:, n : n + HALF], pg[...])
            for i in range(8):
                stage_b[n // CHUNK + i // 4, (i // 2) % 2, i % 2] = value[
                    i * QUARTER : (i + 1) * QUARTER, :
                ].astype(BF)
        start_all(ff_copies(j))

        @pl.when(j < blocks - 1)
        def _():
            start_all(ff_blocks(j + 1))

        @pl.when(j == blocks - 1)
        def _():
            start_all(attend_loads)

    loop(blocks, feed_forward, ff_copies)

    gain_sum = jnp.zeros((1, d), F32)
    for here in tiles:
        back, gain_part = rms_back(token_grad[here, :], x.enc_gain[1], total[here, :])
        gain_sum = gain_sum + gain_part
        value = g[here, :] + back
        g[here, :] = value
        low[here, :] = value.astype(BF)
    gain_acc[0, 1:2, :] = gain_sum
    tokens_load.start()

    fill_bias(x.enc_q_seg, x.all_k_seg, bias, False, tiles[0].stop)
    wait_all(attend_loads)

    def attention(pair):
        lanes = lanes_of(pair)
        ks[:count, :] = b1[:, lanes]
        vs[:count, :] = b2[:, lanes]
        ks[count : count + memories, :] = x.memory[0, :, lanes]
        vs[count : count + memories, :] = x.memory[1, :, lanes]

        def put(here, value):
            dq[here, lanes] = value

        pair_back(
            pair, width, lambda here: b0[here, lanes], ks[...], vs[...], low, b3[lanes, :],
            lambda here: x.enc_mixed[here, lanes], x.enc_logs, bias, dks, dvs, put,
        )
        dk[:, lanes] = dks[:, :count].T.astype(BF)
        dv[:, lanes] = dvs[:, :count].T.astype(BF)
        dmk[:, lanes] = dks[:, count:].T[:memories].astype(BF)
        dmv[:, lanes] = dvs[:, count:].T[:memories].astype(BF)

        @pl.when(pair == pairs - 1)
        def _():
            low_load.start()
            start_all(qkv_loads)

    loop(pairs, attention)

    def after_squares():
        cross_load.start()
        self_out_load.start()

    squares(
        squares_part,
        [(b0, dq), (b0, dk), (b0, dv), (x.enc_mixed, low), (x.fetched, dmk), (x.fetched, dmv)],
        low_load.wait,
        after_squares,
    )

    def token_gradient():
        wait_all(qkv_loads)
        tokens_load.wait()
        gain_sum = jnp.zeros((1, d), F32)
        for here in tiles:
            value = nt(dq[here, :], b1[...]) + nt(dk[here, :], b2[...]) + nt(dv[here, :], b3[...])
            back, gain_part = rms_back(pg[here, :].astype(F32), x.enc_gain[0], value)
            gain_sum = gain_sum + gain_part
            token_grad[here, :] = g[here, :] + back
        gain_acc[0, 0:1, :] = gain_sum
        start_all(dec_qkv_loads)

    once(token_gradient)

    def to_first():
        cross_load.wait()
        back, gain_acc[0, 3:4, :] = rms_back(x.first[...], x.dec_gain[1], nt(dcq[...], b0[...]))
        value = x.dec_new[...] + back
        new2[...] = value
        low2[...] = value.astype(BF)
        fill_bias(x.dec_q_seg, x.dec_k_seg, bias.at[:dec_length, :dec_length], True, dec_length)
        self_out_load.wait()

    once(to_first)

    def self_attention(i):
        for side in range(2):
            pair = 2 * i + side
            lanes = lanes_of(pair)

            def put(here, value):
                dsq[here, lanes] = value

            pair_back(
                pair, dec_length, lambda here: x.self_proj[0, here, lanes],
                x.self_proj[1, :, lanes], x.self_proj[2, :, lanes], low2, low[lanes, :],
                lambda here: x.self_mixed[here, lanes], x.self_logs, bias, dks, dvs, put,
            )
            dsk[:, lanes] = dks[:, :dec_length].T.astype(BF)
            dsv[:, lanes] = dvs[:, :dec_length].T.astype(BF)

    loop(pairs // 2, self_attention)
    squares(
        self_part,
        [(x.self_low, dsq), (x.self_low, dsk), (x.self_low, dsv), (x.self_mixed, low2)],
    )

    def answer_gradient():
        wait_all(dec_qkv_loads)
        value = nt(dsq[...], dq[...]) + nt(dsk[...], dk[...]) + nt(dsv[...], dv[...])
        back, gain_acc[0, 2:3, :] = rms_back(x.answers[...].astype(F32), x.dec_gain[0], value)
        answer_grad[...] = new2[...] + back

    once(answer_gradient)

    def gain_copy(i):
        return pltpu.make_async_remote_copy(
            src_ref=gain_acc.at[i],
            dst_ref=gain_in.at[i],
            send_sem=gain_send.at[i],
            recv_sem=gain_recv.at[i],
            device_id=reducer.peers[i],
            device_id_type=MESH_ID,
        )

    last = len(reducer.peers)

    def gain_step(i):
        if i:
            gain_copy(i - 1).wait()
            value = gain_acc[i - 1] + gain_in[i - 1]
            if i < last:
                gain_acc[i] = value
            else:
                gain_sums[...] = value
        if i < last:
            gain_copy(i).start()

    gain_step(0)
    for i in range(1, last + 1):
        once(lambda: None)
        gain_step(i)
    loop(reducer.steps - now[0], lambda i: None)


def backward(place, groups, x):
    t, d = x["tokens"].shape
    dec_t = x["answers"].shape[0]
    ff = x["w_in"].shape[1]
    blocks, memories = ff // d, x["fetched"].shape[0]
    width = x["all_k_seg"].shape[1]
    row_bits = place.bits("row")
    counts = [g.shape[1] // CHUNK for g in groups]
    new = [4, blocks, ff // (4 * CHUNK), 6, 4]
    total = sum(counts) + sum(new)
    exchanges = 2 + len(row_bits)
    anywhere = pl.BlockSpec(memory_space=pl.ANY)
    vmem = pl.BlockSpec(memory_space=pltpu.VMEM)
    operands = [(x[name], vmem) for name in NEAR]
    operands += [(x[name], anywhere) for name in FAR + LATER]
    operands += [(chunk_view(g), anywhere) for g in groups]
    chunk = (2, 2, QUARTER, d)
    out_shape = [jax.ShapeDtypeStruct((total,) + chunk, BF)]
    out_shape += [jax.ShapeDtypeStruct((4, n) + chunk, BF) for n in new]
    out_shape += [
        jax.ShapeDtypeStruct((t, d), F32),
        jax.ShapeDtypeStruct((dec_t, d), F32),
        jax.ShapeDtypeStruct((8, d), F32),
    ]
    square = lambda kind: pltpu.VMEM((t, d), kind)
    scratch = (
        [square(F32), square(F32), pltpu.VMEM((d, d), F32)]
        + [square(BF)] * 6
        + [pltpu.VMEM((memories, d), BF)] * 2
        + [pltpu.VMEM((t, width), F32)]
        + [pltpu.VMEM((width, LANES), BF)] * 2
        + [pltpu.VMEM((LANES, width), F32)] * 2
        + [square(BF)] * 4
        + [pltpu.VMEM((dec_t, d), BF), pltpu.VMEM((dec_t, d), F32), pltpu.VMEM((dec_t, d), BF)]
        + [pltpu.VMEM((4,) + chunk, BF), pltpu.VMEM((4,) + chunk, BF)]
        + [pltpu.VMEM((exchanges, 8, d), F32)] * 2
        + [pltpu.SemaphoreType.DMA((14,)), pltpu.SemaphoreType.DMA((len(LATER),))]
        + [pltpu.SemaphoreType.DMA((exchanges,))] * 2
        + [pltpu.VMEM(x[name].shape, x[name].dtype) for name in LATER]
        + Reducer.scratch(row_bits, d)
    )
    results = pl.pallas_call(
        functools.partial(backward_kernel, counts, row_bits, memories),
        in_specs=[spec for _, spec in operands],
        out_specs=[anywhere] * 6 + [vmem] * 3,
        out_shape=out_shape,
        scratch_shapes=scratch,
        compiler_params=pltpu.CompilerParams(
            collective_id=1, has_side_effects=True, vmem_limit_bytes=60 * 2**20
        ),
        cost_estimate=cost(2 * t * d * (4 * ff + 14 * d), 30 * total * CHUNK * d),
        name="backward",
    )(*[array for array, _ in operands])
    return results[0], results[6], results[7], results[8]


def finish_kernel(places, index, sums, gain_sums, *refs):
    outs, gain_outs = refs[: len(places)], refs[len(places) : len(places) + 3]
    wide, store_sem = refs[len(places) + 3 :]
    spots = [(out, at, i) for out, (count, at) in zip(outs, places) for i in range(count)]
    total = len(spots)

    def store(c):
        out, at, i = spots[c]
        return pltpu.make_async_copy(
            wide.at[c % 4], out.at[at(i)], store_sem.at[c % 4]
        )

    size = gain_outs[2].shape[1]
    for shard in range(gain_sums.shape[1] // size):

        @pl.when(index[0] == shard)
        def _(shard=shard):
            lanes = slice(shard * size, (shard + 1) * size)
            gain_outs[0][...] = gain_sums[0:2, lanes]
            gain_outs[1][...] = gain_sums[2:4, lanes]
            gain_outs[2][...] = gain_sums[4:5, lanes]

    for c in range(total):
        if c >= 4:
            store(c - 4).wait()
        wide[c % 4] = sums[c].astype(F32)
        store(c).start()
    for c in range(total - 4, total):
        store(c).wait()


def finish_sums(place, sums, gain_sums, blocks):
    d = gain_sums.shape[1]
    total = sums.shape[0]
    one = lambda i: ()
    lead = lambda i: (i,)
    rows = lambda i: (pl.ds(i * CHUNK, CHUNK), slice(None))
    lanes = lambda i: (slice(None), pl.ds(i * d, d))
    flat, tall, wide = (CHUNK, d), (blocks * CHUNK, d), (CHUNK, blocks * d)
    kinds = [
        (wide, blocks, lanes),
        (tall, blocks, rows),
        (flat, 1, one),
        ((3,) + flat, 3, lead),
        (wide, blocks, lanes),
        (tall, blocks, rows),
        ((3,) + flat, 3, lead),
        (flat, 1, one),
        ((2,) + flat, 2, lead),
        ((3,) + flat, 3, lead),
        (flat, 1, one),
    ]
    anywhere = pl.BlockSpec(memory_space=pl.ANY)
    gain_shapes = [(2, CHUNK), (2, CHUNK), (1, CHUNK)]
    return pl.pallas_call(
        functools.partial(finish_kernel, [(count, at) for _, count, at in kinds]),
        in_specs=[
            pl.BlockSpec(memory_space=pltpu.SMEM),
            full((total, CHUNK, d)),
            full((8, d)),
        ],
        out_specs=[anywhere] * len(kinds) + [full(shape) for shape in gain_shapes],
        out_shape=[jax.ShapeDtypeStruct(shape, F32) for shape, _, _ in kinds]
        + [jax.ShapeDtypeStruct(shape, F32) for shape in gain_shapes],
        scratch_shapes=[
            pltpu.VMEM((4, CHUNK, d), F32),
            pltpu.SemaphoreType.DMA((4,)),
        ],
        compiler_params=params(24),
        cost_estimate=cost(0, 6 * total * CHUNK * d),
        name="finish_sums",
    )(place.index, sums, gain_sums)


def fold_outer(place, value):
    while value.shape[0] > 4:
        half = value.shape[0] // 2
        value = add(value[:half], place.swap(value[half:], "dp", half))
    return value


def gain_group(place, gains):
    shards = place.sizes["dp"]
    count, d = gains.shape
    parts = gains.reshape(count, shards, -1)
    turned = jnp.stack(
        [lax.dynamic_index_in_dim(parts, place.dp ^ turn, 1, False) for turn in range(shards)]
    )
    return jnp.pad(turned.astype(BF), ((0, 0), (0, CHUNK - count), (0, d - parts.shape[2])))


def weights_of(value, count, size):
    value = value[: count * size].reshape(count, size, -1)
    return jnp.swapaxes(value, 1, 2).astype(F32)


def encoder_back(
    place, groups, q_seg, k_seg, dck, dcv, cross, mid, tokens, dec_gain_grads, gains,
    w_in, w_out, slope, hidden, mid_low, qkv, memory, mixed, logs, wo, enc_low, fetched, w_qkv,
):
    pre_grad, grad_low, new, low, mid_gain_grad = ffn_back(
        (dck, dcv), cross, w_in, w_out, slope, mid, gains[1]
    )
    dq, dk, dv, dmk, dmv = attend_back(
        (qkv, 0), (qkv, 1), (qkv, 2), mixed, logs, low, wo, q_seg, k_seg, memory
    )
    parts = [
        ff_out_grads(place, hidden, grad_low),
        ff_in_grads(place, mid_low, pre_grad),
        square_grads(place, [(enc_low, [dq, dk, dv]), (mixed, [low]), (fetched, [dmk, dmv])]),
    ]
    token_grad, _, enc_gain_grad = proj_back(tokens, gains[0], new, w_qkv, [dq, dk, dv])
    gain_part = gain_group(
        place, jnp.concatenate([enc_gain_grad, mid_gain_grad] + dec_gain_grads)
    )
    parts = [fold_outer(place, part) for part in groups + parts + [gain_part]]
    sums = reduce_all(place, parts)
    size = tokens.shape[1] // place.sizes["dp"]
    return sums, token_grad, sums[-1][:5, :size].astype(F32)


def fetch_memory(place, table, ids):
    rows = table.shape[0]
    others = range(1, place.sizes["dp"])
    wanted = [ids] + [place.swap(ids, "dp", turn) for turn in others]
    local = jnp.concatenate(wanted) - place.dp * rows
    chosen = (local[:, None] == jnp.arange(rows)[None, :]).astype(BF)
    picked = nn(chosen, table).astype(BF).reshape(len(wanted), ids.shape[0], -1)
    result = picked[0]
    for turn in others:
        result = result + place.swap(picked[turn], "dp", turn)
    return result


def on_device(
    sizes,
    enc_input,
    dec_input,
    memory_table,
    memory_ids,
    enc_segments,
    dec_segments,
    enc_qkv,
    enc_attn_out,
    mem_proj,
    enc_gains,
    enc_ff_in,
    enc_ff_out,
    dec_qkv,
    dec_self_out,
    dec_cross,
    dec_cross_out,
    dec_gains,
    dec_ff_in,
    dec_ff_out,
    out_grad,
):
    place = Place(sizes)
    direct = sizes["dp"] == 4
    tokens, answers = enc_input[0], dec_input[0]
    fetched = fetch_memory(place, memory_table, memory_ids.reshape(-1))
    memories = fetched.shape[0]
    enc_gain = enc_gains.astype(F32)[:, None]
    dec_gain = dec_gains.astype(F32)[:, None]

    enc_at, dec_at = enc_segments[0], dec_segments[0]
    enc_q_seg, dec_q_seg = enc_at[:, None], dec_at[:, None]
    owner = jnp.arange(memories, dtype=jnp.int32) // TOPK
    padding = jnp.full((-memories % LANES,), -1, jnp.int32)
    all_k_seg = jnp.concatenate([enc_at, owner, padding])[None]
    enc_k_seg, dec_k_seg = enc_at[None], dec_at[None]

    self_low, self_proj = project(answers, dec_gain[0], dec_qkv, 0, 3)
    self_q, self_k, self_v = [(self_proj, j) for j in range(3)]
    self_mixed, self_logs = attend(self_q, self_k, self_v, dec_q_seg, dec_k_seg, causal=True)
    first, cross_low, cross_q = project(
        answers, dec_gain[1], dec_cross, 0, 1, self_mixed, dec_self_out
    )
    cross_q = (cross_q, 0)

    enc_low, enc_proj = project(tokens, enc_gain[0], enc_qkv, 0, 3)
    enc_q, enc_k, enc_v = [(enc_proj, j) for j in range(3)]
    memory = project_plain(fetched, mem_proj, 0, 2)
    enc_mixed, enc_logs = attend(enc_q, enc_k, enc_v, enc_q_seg, all_k_seg, memory)
    middle, mid_low, enc_hidden, enc_slope, encoded = ffn_forward(
        tokens, enc_mixed, enc_attn_out, enc_gain[1], enc_ff_in, enc_ff_out, far=True
    )
    pairs = project_plain(encoded, dec_cross, 1, 2)
    cross_k, cross_v = (pairs, 0), (pairs, 1)
    cross_mixed, cross_logs = attend(cross_q, cross_k, cross_v, dec_q_seg, enc_k_seg)
    second, ffn_low, dec_hidden, dec_slope, final = ffn_forward(
        first, cross_mixed, dec_cross_out, dec_gain[2], dec_ff_in, dec_ff_out
    )

    grad = out_grad[0]
    if direct:
        new, low, ffn_gain_grad, dec_ff_out_part, dec_ff_in_part = ffn_back_weights(
            place, grad, dec_ff_in, dec_ff_out, dec_slope, dec_hidden, ffn_low, second, dec_gain[2]
        )
        d = tokens.shape[1]
        result, token_grad, answer_grad, gain_sums = backward(
            place,
            [dec_ff_out_part, dec_ff_in_part],
            dict(
                dec_q_seg=dec_q_seg, enc_k_seg=enc_k_seg, dec_k_seg=dec_k_seg,
                enc_q_seg=enc_q_seg, all_k_seg=all_k_seg, encoded=encoded, cross=dec_cross,
                mid=middle, tokens=tokens, dec_qkv=dec_qkv, w_in=enc_ff_in, w_out=enc_ff_out,
                slope=enc_slope, hidden=enc_hidden, enc_low=enc_low, w_qkv=enc_qkv,
                cross_q=cross_q[0], pairs=pairs, cross_mixed=cross_mixed, cross_out=dec_cross_out,
                self_proj=self_proj, self_mixed=self_mixed, self_out=dec_self_out,
                enc_proj=enc_proj, memory=memory, attn_out=enc_attn_out, cross_logs=cross_logs,
                cross_low=cross_low, self_logs=self_logs, self_low=self_low, dec_low=low,
                dec_new=new, first=first, answers=answers, mid_low=mid_low, enc_mixed=enc_mixed,
                enc_logs=enc_logs, fetched=fetched, ffn_gain_grad=ffn_gain_grad,
                enc_gain=enc_gain, dec_gain=dec_gain,
            ),
        )
        (
            dec_out_grad, dec_in_grad, cross_out_grad, cross_grad, out_ff_grad, in_ff_grad,
            qkv_grad, attn_out_grad, mem_grad, self_grad, self_out_grad,
            enc_gain_grad, dec_gain_grad, ffn_gain_grad,
        ) = finish_sums(place, result.reshape(-1, CHUNK, d), gain_sums, enc_ff_in.shape[1] // d)
        turn = lambda value: jnp.swapaxes(value, -1, -2)
        return (
            final[None],
            token_grad[None],
            answer_grad[None],
            turn(qkv_grad),
            turn(attn_out_grad),
            turn(mem_grad),
            enc_gain_grad,
            in_ff_grad,
            turn(out_ff_grad),
            turn(self_grad),
            turn(self_out_grad),
            turn(cross_grad),
            turn(cross_out_grad),
            dec_gain_grad,
            dec_in_grad,
            turn(dec_out_grad),
            ffn_gain_grad[0],
        )

    dec_ff_out_part = ff_out_grads(place, dec_hidden, grad)
    pre_grad, _, new, low, ffn_gain_grad = ffn_back(
        grad, None, dec_ff_in, dec_ff_out, dec_slope, second, dec_gain[2]
    )
    dec_ff_in_part = ff_in_grads(place, ffn_low, pre_grad)
    dcq, dck, dcv = attend_back(
        cross_q, cross_k, cross_v, cross_mixed, cross_logs, low, dec_cross_out,
        dec_q_seg, enc_k_seg,
    )
    cross_part = square_grads(
        place, [(cross_mixed, [low]), (cross_low, [dcq]), (encoded, [dck, dcv])]
    )
    new, low, cross_gain_grad = proj_back(first, dec_gain[1], new, dec_cross, [dcq])
    dsq, dsk, dsv = attend_back(
        self_q, self_k, self_v, self_mixed, self_logs, low, dec_self_out,
        dec_q_seg, dec_k_seg, causal=True,
    )
    self_part = square_grads(place, [(self_low, [dsq, dsk, dsv]), (self_mixed, [low])])
    answer_grad, _, self_gain_grad = proj_back(answers, dec_gain[0], new, dec_qkv, [dsq, dsk, dsv])
    dec_gain_grads = [self_gain_grad, cross_gain_grad, ffn_gain_grad]
    dec_parts = [dec_ff_out_part, dec_ff_in_part, cross_part, self_part]
    sums, token_grad, gains = encoder_back(
        place, dec_parts, enc_q_seg, all_k_seg, dck, dcv, dec_cross, middle, tokens,
        dec_gain_grads, enc_gain, enc_ff_in, enc_ff_out, enc_slope, enc_hidden, mid_low,
        enc_proj, memory, enc_mixed, enc_logs, enc_attn_out, enc_low, fetched, enc_qkv,
    )
    size = tokens.shape[1] // sizes["dp"]
    blocks = enc_ff_in.shape[1] // tokens.shape[1]
    ff_size = enc_ff_in.shape[1] // sizes["dp"]
    enc_squares = weights_of(sums[6], 6, size)
    self_squares = weights_of(sums[3], 4, size)
    cross_squares = weights_of(sums[2], 4, size)
    return (
        final[None],
        token_grad[None],
        answer_grad[None],
        enc_squares[0:3],
        enc_squares[3],
        enc_squares[4:6],
        gains[0:2],
        weights_of(sums[5], 1, ff_size)[0],
        weights_of(sums[4], blocks, size).reshape(-1, size),
        self_squares[0:3],
        self_squares[3],
        cross_squares[1:4],
        cross_squares[0],
        gains[2:4],
        weights_of(sums[1], 1, ff_size)[0],
        weights_of(sums[0], blocks, size).reshape(-1, size),
        gains[4],
    )


def solution(mesh):
    rows = P(("row", "dp"), None, None)
    in_specs = (
        (rows, rows, P("dp", None), rows, P(("row", "dp"), None), P(("row", "dp"), None))
        + (P(),) * 13
        + (rows,)
    )
    cube, flat = P(None, None, "dp"), P(None, "dp")
    out_specs = (
        (rows, rows, rows)
        + (cube, flat, cube, flat, flat, flat)
        + (cube, flat, cube, flat, flat, flat, flat)
        + (P("dp"),)
    )
    return jax.shard_map(
        functools.partial(on_device, dict(mesh.shape)),
        mesh=mesh,
        in_specs=in_specs,
        out_specs=out_specs,
        check_vma=False,
    )
```

```python
import functools

import jax
import jax.numpy as jnp
from jax import lax
from jax.experimental import pallas as pl
from jax.experimental.pallas import tpu as pltpu
from jax.sharding import PartitionSpec as P

HD = 64
TOPK = 10
LANES = 128
MASKED = -1e30
BF = jnp.bfloat16
F32 = jnp.float32


def nn(left, right):
    return lax.dot_general(left, right, (((1,), (0,)), ((), ())), preferred_element_type=F32)


def nt(left, right):
    return lax.dot_general(left, right, (((1,), (1,)), ((), ())), preferred_element_type=F32)


def tn(left, right):
    return lax.dot_general(left, right, (((0,), (0,)), ((), ())), preferred_element_type=F32)


def full(shape):
    return pl.BlockSpec(shape, lambda *_: (0,) * len(shape))


def params(mib=16):
    return pltpu.CompilerParams(vmem_limit_bytes=mib * 2**20)


def cost(flops, nbytes, exps=0):
    return pl.CostEstimate(flops=int(flops), bytes_accessed=int(nbytes), transcendentals=int(exps))


def rms_scale(x):
    return lax.rsqrt(jnp.mean(x * x, axis=-1, keepdims=True) + 1e-06)


def rms_back(x, gain, dy):
    scale = rms_scale(x)
    gain_grad = jnp.sum(dy * x * scale, axis=0, keepdims=True)
    inner = dy * gain
    mixed = jnp.mean(inner * x, axis=-1, keepdims=True)
    return scale * (inner - x * (scale * scale) * mixed), gain_grad


def proj_kernel(residual, index, x, gains, *refs):
    if residual:
        mixed, wo, w, mid, low, out = refs
    else:
        w, low, out = refs

    @pl.when(pl.program_id(0) == 0)
    def _():
        value = x[...].astype(F32)
        if residual:
            value = value + nn(mixed[...], wo[...])
            mid[...] = value
        low[...] = (value * rms_scale(value) * gains[index : index + 1, :]).astype(BF)

    out[...] = nn(low[...], w[...]).astype(BF)


def project(x, gain, w, first, count, mixed=None, wo=None):
    t, d = x.shape
    gains, index = gain
    residual = mixed is not None
    args = [x, gains]
    specs = [full((t, d)), full(gains.shape)]
    outs = [pltpu.HBM((t, d), BF), pltpu.HBM((count, t, d), BF)]
    out_specs = [full((t, d)), pl.BlockSpec((None, t, d), lambda j: (j, 0, 0))]
    if residual:
        args += [mixed, wo]
        specs += [full((t, d)), full((d, d))]
        outs = [jax.ShapeDtypeStruct((t, d), F32)] + outs
        out_specs = [full((t, d))] + out_specs
    args.append(w)
    specs.append(pl.BlockSpec((None, d, d), lambda j: (first + j, 0, 0)))
    return pl.pallas_call(
        functools.partial(proj_kernel, residual, index),
        grid=(count,),
        in_specs=specs,
        out_specs=out_specs,
        out_shape=outs,
        compiler_params=params(),
        cost_estimate=cost(2 * t * d * d * (count + residual), 2 * d * (t + d) * (count + 2)),
        name="project",
    )(*args)


def pairs_kernel(x, w, out):
    out[...] = nn(x[...], w[...]).astype(BF)


def project_plain(x, w, first, count):
    t, d = x.shape
    return pl.pallas_call(
        pairs_kernel,
        grid=(count,),
        in_specs=[full((t, d)), pl.BlockSpec((None, d, d), lambda j: (first + j, 0, 0))],
        out_specs=pl.BlockSpec((None, t, d), lambda j: (j, 0, 0)),
        out_shape=jax.ShapeDtypeStruct((count, t, d), BF),
        compiler_params=params(),
        cost_estimate=cost(2 * t * d * d * count, 2 * d * (t + d) * count),
        name="project_plain",
    )(x, w)


def proj_back_kernel(count, x, gain, grad, w, *refs):
    parts = refs[:count]
    new, low, gain_grad, total = refs[count:]
    step = pl.program_id(0)
    for j in range(count):

        @pl.when(step == j)
        def _(j=j):
            value = nt(parts[j][...], w[...])
            total[...] = value if j == 0 else total[...] + value

    @pl.when(step == count - 1)
    def _():
        back, gain_grad[...] = rms_back(x[...].astype(F32), gain[...], total[...])
        value = grad[...] + back
        new[...] = value
        low[...] = value.astype(BF)


def proj_back(x, gain, grad, w, parts):
    t, d = x.shape
    count = len(parts)
    return pl.pallas_call(
        functools.partial(proj_back_kernel, count),
        grid=(count,),
        in_specs=[full((t, d)), full((1, d)), full((t, d))]
        + [pl.BlockSpec((None, d, d), lambda j: (j, 0, 0))]
        + [full((t, d))] * count,
        out_specs=[full((t, d)), full((t, d)), full((1, d))],
        out_shape=[
            jax.ShapeDtypeStruct((t, d), F32),
            jax.ShapeDtypeStruct((t, d), BF),
            jax.ShapeDtypeStruct((1, d), F32),
        ],
        scratch_shapes=[pltpu.VMEM((t, d), F32)],
        compiler_params=params(),
        cost_estimate=cost(2 * t * d * d * count, 2 * d * (t + d) * count + 12 * t * d),
        name="proj_back",
    )(x, gain, grad, w, *parts)


GELU_A = 0.7978845608028654
GELU_B = 0.044715


def gelu_parts(pre):
    square = pre * pre
    half = 0.5 + 0.5 * jnp.tanh(pre * (GELU_A + (GELU_A * GELU_B) * square))
    act = pre * half
    slope = half + (act * (1.0 - half)) * (2 * GELU_A + (6 * GELU_A * GELU_B) * square)
    return act.astype(BF), slope.astype(BF)


def tiles_of(length):
    size = min(length, 256)
    return [slice(begin, begin + size) for begin in range(0, length, size)]


def ffn_kernel(index, res, mixed, wo, gains, w_in, w_out, mid, low, hidden, slope, out, total):
    step = pl.program_id(0)
    tiles = tiles_of(res.shape[0])

    @pl.when(step == 0)
    def _():
        for here in tiles:
            value = res[here, :].astype(F32) + nn(mixed[here, :], wo[...])
            mid[here, :] = value
            low[here, :] = (value * rms_scale(value) * gains[index : index + 1, :]).astype(BF)
            total[here, :] = value

    coming = nn(low[tiles[0], :], w_in[...])
    for number, here in enumerate(tiles):
        pre = coming
        if number + 1 < len(tiles):
            coming = nn(low[tiles[number + 1], :], w_in[...])
        act, slope[here, :] = gelu_parts(pre)
        hidden[here, :] = act
        total[here, :] += nn(act, w_out[...])

    @pl.when(step == pl.num_programs(0) - 1)
    def _():
        for here in tiles:
            out[here, :] = total[here, :].astype(BF)


def ffn_forward(res, mixed, wo, gain, w_in, w_out, far=False, block=768):
    t, d = res.shape
    gains, index = gain
    ff = w_in.shape[1]
    kept = pltpu.HBM if far else jax.ShapeDtypeStruct
    return pl.pallas_call(
        functools.partial(ffn_kernel, index),
        grid=(ff // block,),
        in_specs=[
            full((t, d)),
            full((t, d)),
            full((d, d)),
            full(gains.shape),
            pl.BlockSpec((d, block), lambda j: (0, j)),
            pl.BlockSpec((block, d), lambda j: (j, 0)),
        ],
        out_specs=[
            full((t, d)),
            full((t, d)),
            pl.BlockSpec((t, block), lambda j: (0, j)),
            pl.BlockSpec((t, block), lambda j: (0, j)),
            full((t, d)),
        ],
        out_shape=[
            kept((t, d), F32),
            kept((t, d), BF),
            kept((t, ff), BF),
            kept((t, ff), BF),
            jax.ShapeDtypeStruct((t, d), BF),
        ],
        scratch_shapes=[pltpu.VMEM((t, d), F32)],
        compiler_params=params(28),
        cost_estimate=cost(2 * t * d * (2 * ff + d), 4 * d * ff + 4 * t * ff + 12 * t * d, t * ff),
        name="ffn_forward",
    )(res, mixed, wo, gains, w_in, w_out)


def ffn_back_kernel(sourced, *refs):
    if sourced:
        dk, dv, wk, wv, w_in, w_out, slope, mid, gain, pre_grad, g_low, new, low, gain_grad, g, total = refs
    else:
        grad, w_in, w_out, slope, mid, gain, pre_grad, g_low, new, low, gain_grad, g, total = refs
    step = pl.program_id(0)

    @pl.when(step == 0)
    def _():
        if sourced:
            value = nt(dk[...], wk[...]) + nt(dv[...], wv[...])
        else:
            value = grad[...].astype(F32)
        g[...] = value
        g_low[...] = value.astype(BF)
        total[...] = jnp.zeros_like(total)

    block = (nt(g_low[...], w_out[...]) * slope[...].astype(F32)).astype(BF)
    pre_grad[...] = block
    total[...] += nt(block, w_in[...])

    @pl.when(step == pl.num_programs(0) - 1)
    def _():
        back, gain_grad[...] = rms_back(mid[...], gain[...], total[...])
        value = g[...] + back
        new[...] = value
        low[...] = value.astype(BF)


def ffn_back(grads, weights, w_in, w_out, slope, mid, gain, block=512):
    t, d = mid.shape
    ff = w_in.shape[1]
    sourced = weights is not None
    if sourced:
        args = [grads[0], grads[1], weights, weights]
        specs = [
            full((t, d)),
            full((t, d)),
            pl.BlockSpec((None, d, d), lambda j: (1, 0, 0)),
            pl.BlockSpec((None, d, d), lambda j: (2, 0, 0)),
        ]
    else:
        args = [grads]
        specs = [full((t, d))]
    return pl.pallas_call(
        functools.partial(ffn_back_kernel, sourced),
        grid=(ff // block,),
        in_specs=specs
        + [
            pl.BlockSpec((d, block), lambda j: (0, j)),
            pl.BlockSpec((block, d), lambda j: (j, 0)),
            pl.BlockSpec((t, block), lambda j: (0, j)),
            full((t, d)),
            full((1, d)),
        ],
        out_specs=[
            pl.BlockSpec((t, block), lambda j: (0, j)),
            full((t, d)),
            full((t, d)),
            full((t, d)),
            full((1, d)),
        ],
        out_shape=[
            jax.ShapeDtypeStruct((t, ff), BF),
            jax.ShapeDtypeStruct((t, d), BF),
            jax.ShapeDtypeStruct((t, d), F32),
            jax.ShapeDtypeStruct((t, d), BF),
            jax.ShapeDtypeStruct((1, d), F32),
        ],
        scratch_shapes=[pltpu.VMEM((t, d), F32), pltpu.VMEM((t, d), F32)],
        compiler_params=params(32),
        cost_estimate=cost(4 * t * d * ff, 4 * d * ff + 4 * t * ff + 16 * t * d),
        name="ffn_back",
    )(*args, w_in, w_out, slope, mid, gain)


def fill_bias(q_seg, k_seg, bias, causal, rows):
    length, width = bias.shape
    for begin in range(0, length, rows):
        allowed = q_seg[begin : begin + rows, :] == k_seg[...]
        if causal:
            at = lax.broadcasted_iota(jnp.int32, (rows, width), 0) + begin
            key = lax.broadcasted_iota(jnp.int32, (rows, width), 1)
            allowed = allowed & (key <= at)
        bias[begin : begin + rows, :] = jnp.where(allowed, 0.0, MASKED)


def join_keys(refs, count, extra, width):
    keys, values, mem_keys, mem_values, all_keys, all_values = refs
    for source, more, target in ((keys, mem_keys, all_keys), (values, mem_values, all_values)):
        target[:count, :] = source[...]
        target[count : count + extra, :] = more[...]


def attend_kernel(extra, causal, rows, *refs):
    if extra:
        q_seg, k_seg, q, k, v, mk, mv, out, logs, bias, ks, vs = refs
    else:
        q_seg, k_seg, q, k, v, out, logs, bias = refs
    length, width = bias.shape
    count = k.shape[0]
    step = pl.program_id(0)

    @pl.when(step == 0)
    def _():
        fill_bias(q_seg, k_seg, bias, causal, rows)
        logs[...] = jnp.zeros_like(logs)
        if extra:
            ks[count:, :] = jnp.zeros((width - count, LANES), BF)
            vs[count:, :] = jnp.zeros((width - count, LANES), BF)

    if extra:
        join_keys((k, v, mk, mv, ks, vs), count, extra, width)
        k, v = ks, vs
    lane = lax.broadcasted_iota(jnp.int32, (rows, LANES), 1)

    def scores_of(begin, head):
        here = slice(begin, begin + rows)
        mine = (lane < HD) if head == 0 else (lane >= HD)
        queries = jnp.where(mine, q[here, :] * BF(HD**-0.5), BF(0))
        return nt(queries, k[...]) + bias[here, :]

    work = [(begin, head) for begin in range(0, length, rows) for head in range(2)]
    coming = scores_of(*work[0])
    for number, (begin, head) in enumerate(work):
        scores = coming
        if number + 1 < len(work):
            coming = scores_of(*work[number + 1])
        top = jnp.max(scores, axis=1, keepdims=True)
        exponent = jnp.exp(scores - top)
        sums = jnp.sum(exponent, axis=1, keepdims=True)
        side = nn(exponent.astype(BF), v[...]) * (1.0 / sums)
        here = slice(begin, begin + rows)
        kept = logs[here, :] if head == 0 else kept
        kept = jnp.where(lane == 2 * step + head, top + jnp.log(sums), kept)
        if head == 0:
            first = side
        else:
            logs[here, :] = kept
            out[here, :] = jnp.where(lane < HD, first, side).astype(BF)


def part_of(stack, index):
    rows = stack.shape[1]
    return pl.BlockSpec((None, rows, LANES), lambda p: (index, 0, p))


def attend(q, k, v, q_seg, k_seg, memory=None, causal=False, rows=256):
    t, d = q[0].shape[1:]
    count = k[0].shape[1]
    width = k_seg.shape[1]
    args = [q_seg, k_seg, q[0], k[0], v[0]]
    specs = [full(q_seg.shape), full(k_seg.shape), part_of(*q), part_of(*k), part_of(*v)]
    scratch = [pltpu.VMEM((t, width), F32)]
    extra = 0
    if memory is not None:
        extra = memory.shape[1]
        args += [memory, memory]
        specs += [part_of(memory, 0), part_of(memory, 1)]
        scratch += [pltpu.VMEM((width, LANES), BF)] * 2
    return pl.pallas_call(
        functools.partial(attend_kernel, extra, causal, rows),
        grid=(d // LANES,),
        in_specs=specs,
        out_specs=[pl.BlockSpec((t, LANES), lambda p: (0, p)), full((t, LANES))],
        out_shape=[jax.ShapeDtypeStruct((t, d), BF), jax.ShapeDtypeStruct((t, LANES), F32)],
        scratch_shapes=scratch,
        compiler_params=params(),
        cost_estimate=cost(16 * t * width * d, 8 * d * (t + count), t * width * d // HD),
        name="attend",
    )(*args)


def attend_back_kernel(extra, causal, rows, *refs):
    if extra:
        q_seg, k_seg, q, k, v, out, logs, grad, wo, mk, mv = refs[:11]
        dq, dk, dv, dmk, dmv, bias, dks, dvs, ks, vs = refs[11:]
    else:
        q_seg, k_seg, q, k, v, out, logs, grad, wo, dq, dk, dv, bias, dks, dvs = refs
    length, width = bias.shape
    count = k.shape[0]
    step = pl.program_id(0)

    @pl.when(step == 0)
    def _():
        fill_bias(q_seg, k_seg, bias, causal, rows)
        if extra:
            ks[count:, :] = jnp.zeros((width - count, LANES), BF)
            vs[count:, :] = jnp.zeros((width - count, LANES), BF)

    if extra:
        join_keys((k, v, mk, mv, ks, vs), count, extra, width)
        k, v = ks, vs
    lane = lax.broadcasted_iota(jnp.int32, (rows, LANES), 1)
    for begin in range(0, length, rows):
        here = slice(begin, begin + rows)
        queries = q[here, :] * BF(HD**-0.5)
        mixed = nt(grad[here, :], wo[...]).astype(BF)
        product = mixed.astype(F32) * out[here, :].astype(F32)
        kept = logs[here, :]
        sides = []
        for head in range(2):
            mine = (lane < HD) if head == 0 else (lane >= HD)
            own_q = jnp.where(mine, queries, BF(0))
            own_grad = jnp.where(mine, mixed, BF(0))
            log_sum = jnp.sum(jnp.where(lane == 2 * step + head, kept, 0.0), axis=1, keepdims=True)
            center = jnp.sum(jnp.where(mine, product, 0.0), axis=1, keepdims=True)
            probs = jnp.exp(nt(own_q, k[...]) + bias[here, :] - log_sum)
            score_grad = (probs * (nt(own_grad, v[...]) - center)).astype(BF)
            sides.append(nn(score_grad, k[...]))
            value_part = nn(own_grad.T, probs.astype(BF))
            key_part = nn(own_q.T, score_grad)
            if begin == 0 and head == 0:
                dvs[...] = value_part
                dks[...] = key_part
            else:
                dvs[...] += value_part
                dks[...] += key_part
        dq[here, :] = (jnp.where(lane < HD, sides[0], sides[1]) * HD**-0.5).astype(BF)
    dk[...] = dks[:, :count].T.astype(BF)
    dv[...] = dvs[:, :count].T.astype(BF)
    if extra:
        dmk[...] = dks[:, count:].T[:extra].astype(BF)
        dmv[...] = dvs[:, count:].T[:extra].astype(BF)


def attend_back(q, k, v, out, logs, grad, wo, q_seg, k_seg, memory=None, causal=False, rows=256):
    t, d = q[0].shape[1:]
    count = k[0].shape[1]
    width = k_seg.shape[1]
    column = lambda n: pl.BlockSpec((n, LANES), lambda p: (0, p))
    args = [q_seg, k_seg, q[0], k[0], v[0], out, logs, grad, wo]
    specs = [full(q_seg.shape), full(k_seg.shape), part_of(*q), part_of(*k), part_of(*v)]
    specs += [column(t), full((t, LANES)), full((t, d)), pl.BlockSpec((LANES, d), lambda p: (p, 0))]
    scratch = [pltpu.VMEM((t, width), F32)] + [pltpu.VMEM((LANES, width), F32)] * 2
    lengths = [t, count, count]
    extra = 0
    if memory is not None:
        extra = memory.shape[1]
        args += [memory, memory]
        specs += [part_of(memory, 0), part_of(memory, 1)]
        scratch += [pltpu.VMEM((width, LANES), BF)] * 2
        lengths += [extra, extra]
    return pl.pallas_call(
        functools.partial(attend_back_kernel, extra, causal, rows),
        grid=(d // LANES,),
        in_specs=specs,
        out_specs=[column(n) for n in lengths],
        out_shape=[jax.ShapeDtypeStruct((n, d), BF) for n in lengths],
        scratch_shapes=scratch,
        compiler_params=params(),
        cost_estimate=cost(32 * t * width * d, 12 * d * (t + count), t * width * d // HD),
        name="attend_back",
    )(*args)


def share_rows(index, acc, out, shards, size):
    for turn in range(shards):
        shard = index[0] ^ turn
        start = pl.multiple_of(shard * size, 16)
        out[turn] = acc[pl.ds(start, size), :].astype(BF)


def squares_kernel(items, shards, index, *refs):
    out, acc = refs[-2:]
    size = acc.shape[0] // shards
    for j, (a, g) in enumerate(items):

        @pl.when(pl.program_id(0) == j)
        def _(a=a, g=g):
            acc[...] = tn(refs[g][...], refs[a][...])
            share_rows(index, acc, out, shards, size)


def pad_rows(rows):
    return -(-rows // CHUNK) * CHUNK


def square_grads(place, products):
    arrays, items = [], []

    def at(array):
        for i, other in enumerate(arrays):
            if other is array:
                return i
        arrays.append(array)
        return len(arrays) - 1

    for acts, grads in products:
        for grad in grads:
            items.append((at(acts), at(grad)))
    shards = place.sizes["dp"]
    d = products[0][0].shape[1]
    size = d // shards
    work = sum(2 * arrays[a].shape[0] * d * d for a, _ in items)
    return pl.pallas_call(
        functools.partial(squares_kernel, items, shards),
        grid=(len(items),),
        in_specs=[pl.BlockSpec(memory_space=pltpu.SMEM)] + [full(x.shape) for x in arrays],
        out_specs=pl.BlockSpec((shards, size, d), lambda j: (0, j, 0)),
        out_shape=jax.ShapeDtypeStruct((shards, pad_rows(len(items) * size), d), BF),
        scratch_shapes=[pltpu.VMEM((d, d), F32)],
        compiler_params=params(),
        cost_estimate=cost(work, sum(2 * x.size for x in arrays) + 2 * len(items) * d * d),
        name="square_grads",
    )(place.index, *arrays)


def out_kernel(shards, index, acts, grad, out, acc):
    acc[...] = tn(grad[...], acts[...])
    share_rows(index, acc, out, shards, acc.shape[0] // shards)


def ff_out_grads(place, acts, grad):
    shards = place.sizes["dp"]
    t, d = grad.shape
    blocks = acts.shape[1] // d
    size = d // shards
    return pl.pallas_call(
        functools.partial(out_kernel, shards),
        grid=(blocks,),
        in_specs=[
            pl.BlockSpec(memory_space=pltpu.SMEM),
            pl.BlockSpec((t, d), lambda j: (0, j)),
            full((t, d)),
        ],
        out_specs=pl.BlockSpec((shards, size, d), lambda j: (0, j, 0)),
        out_shape=jax.ShapeDtypeStruct((shards, blocks * size, d), BF),
        scratch_shapes=[pltpu.VMEM((d, d), F32)],
        compiler_params=params(),
        cost_estimate=cost(2 * t * d * d * blocks, 2 * (t + d) * d * (blocks + 1)),
        name="ff_out_grads",
    )(place.index, acts, grad)


def in_kernel(per_block, index, grad, acts, out):
    acc = tn(grad[...], acts[...]).astype(BF)
    size = acc.shape[0] // per_block
    for i in range(per_block):
        shard = pl.program_id(0) * per_block + i
        out[index[0] ^ shard] = acc[i * size : (i + 1) * size]


def ff_in_grads(place, acts, grad):
    shards = place.sizes["dp"]
    t, d = acts.shape
    ff = grad.shape[1]
    blocks = ff // d
    size = ff // shards
    return pl.pallas_call(
        functools.partial(in_kernel, d // size),
        grid=(blocks,),
        in_specs=[
            pl.BlockSpec(memory_space=pltpu.SMEM),
            pl.BlockSpec((t, d), lambda j: (0, j)),
            full((t, d)),
        ],
        out_specs=full((shards, size, d)),
        out_shape=jax.ShapeDtypeStruct((shards, size, d), BF),
        compiler_params=params(),
        cost_estimate=cost(2 * t * d * ff, 2 * (t + d) * d * (blocks + 1)),
        name="ff_in_grads",
    )(place.index, grad, acts)


def ffn_back_weights_kernel(
    row, index, grad, w_in, w_out, slope, hidden, low_in, mid, gains,
    new, low, gain_grad, out_part, in_part, total, acc,
):
    step = pl.program_id(0)

    @pl.when(step == 0)
    def _():
        total[...] = jnp.zeros_like(total)

    acc[...] = tn(grad[...], hidden[...])
    share_rows(index, acc, out_part, out_part.shape[0], out_part.shape[1])
    block = (nt(grad[...], w_out[...]) * slope[...].astype(F32)).astype(BF)
    total[...] += nt(block, w_in[...])
    in_part[index[0] ^ step] = tn(low_in[...], block).astype(BF)

    @pl.when(step == pl.num_programs(0) - 1)
    def _():
        back, gain_grad[...] = rms_back(
            mid[...], gains[row : row + 1, :], total[...]
        )
        value = grad[...].astype(F32) + back
        new[...] = value
        low[...] = value.astype(BF)


def ffn_back_weights(place, grad, w_in, w_out, slope, hidden, low_in, mid, gain):
    t, d = mid.shape
    gains, row = gain
    blocks = w_in.shape[1] // d
    shards = place.sizes["dp"]
    size = d // shards
    return pl.pallas_call(
        functools.partial(ffn_back_weights_kernel, row),
        grid=(blocks,),
        in_specs=[
            pl.BlockSpec(memory_space=pltpu.SMEM),
            full((t, d)),
            pl.BlockSpec((d, d), lambda j: (0, j)),
            pl.BlockSpec((d, d), lambda j: (j, 0)),
            pl.BlockSpec((t, d), lambda j: (0, j)),
            pl.BlockSpec((t, d), lambda j: (0, j)),
            full((t, d)),
            full((t, d)),
            full(gains.shape),
        ],
        out_specs=[
            full((t, d)),
            full((t, d)),
            full((1, d)),
            pl.BlockSpec((shards, size, d), lambda j: (0, j, 0)),
            full((shards, d, d)),
        ],
        out_shape=[
            jax.ShapeDtypeStruct((t, d), F32),
            jax.ShapeDtypeStruct((t, d), BF),
            jax.ShapeDtypeStruct((1, d), F32),
            pltpu.HBM((shards, blocks * size, d), BF),
            pltpu.HBM((shards, d, d), BF),
        ],
        scratch_shapes=[pltpu.VMEM((t, d), F32), pltpu.VMEM((d, d), F32)],
        compiler_params=params(32),
        cost_estimate=cost(8 * t * d * d * blocks, 8 * d * d * blocks + 24 * t * d),
        name="ffn_back_weights",
    )(place.index, grad, w_in, w_out, slope, hidden, low_in, mid, gains)


def flip(index, bit):
    return index + bit - 2 * bit * ((index // bit) % 2)


class Place:
    def __init__(self, sizes):
        self.sizes = sizes
        self.dp = lax.axis_index("dp")
        self.row = lax.axis_index("row")
        self.index = self.dp.astype(jnp.int32)[None]

    def swap(self, value, axis, turn):
        return lax.ppermute(value, axis, [(i, i ^ turn) for i in range(self.sizes[axis])])

    def bits(self, axis):
        return [1 << i for i in range(self.sizes[axis].bit_length() - 1)]


QUARTER = 48
CHUNK = 4 * QUARTER
AHEAD = 3
DELAY = 2
FAR_RING = DELAY + 2
Y_RING = DELAY + 4
RING = 5
MESH_ID = pl.DeviceIdType.MESH


def add(left, right):
    return (left.astype(F32) + right.astype(F32)).astype(BF)


class Step:
    def __init__(self, value, low=None, high=None):
        self.value = value
        self.low = value if low is None else low
        self.high = value if high is None else high

    def __add__(self, other):
        return Step(self.value + other, self.low + other, self.high + other)


def within(step, low, high):
    if low <= step.low and step.high < high:
        return lambda function: function()
    if step.high < low or step.low >= high:
        return lambda function: None
    return pl.when((step.value >= low) & (step.value < high))


class Reducer:
    def __init__(self, groups, counts, row_bits, out, refs):
        self.groups, self.counts, self.out = groups, counts, out
        self.total = sum(counts)
        others = len(row_bits) - 2
        (self.own, self.core_in, self.far, self.near, self.y_in, self.x_in, self.z_in, self.kept) = refs[:8]
        self.w_in = refs[8 : 8 + others]
        sems = list(refs[8 + others :])
        self.load_sem, self.kept_sem, self.core_send, self.core_recv = sems[:4]
        self.core_free, self.send_sem, self.recv, self.free = sems[4], sems[5::3], sems[6::3], sems[7::3]
        row, dp = lax.axis_index("row"), lax.axis_index("dp")
        self.x, self.z = row % 2, (row // 2) % 2
        self.core_peer = (row, flip(dp, 1))
        self.y_peer = (row, flip(dp, 2))
        self.row_peers = [(flip(row, bit), dp) for bit in row_bits]
        self.x_peer, self.z_peer = self.row_peers[:2]
        self.peers = [self.core_peer, self.y_peer] + self.row_peers
        self.stages = [self.y_stage, self.x_stage, self.z_stage]
        self.stages += [functools.partial(self.w_stage, i) for i in range(others)]
        self.stages += [self.back_z_stage, self.back_x_stage]
        self.steps = self.total + DELAY + len(self.stages) - 1

    @staticmethod
    def scratch(row_bits, d):
        others = len(row_bits) - 2
        chunk = (2, 2, QUARTER, d)
        shapes = [
            (AHEAD, 2) + chunk,
            (AHEAD, 2) + chunk,
            (FAR_RING,) + chunk,
            (FAR_RING,) + chunk,
            (Y_RING,) + chunk,
            (RING,) + chunk[1:],
            (RING,) + chunk[2:],
            (RING,) + chunk[2:],
        ] + [(RING,) + chunk[2:]] * others
        dma = pltpu.SemaphoreType.DMA
        regular = pltpu.SemaphoreType.REGULAR
        rings = [Y_RING, RING, RING] + [RING] * others + [RING, RING]
        sems = [dma((AHEAD, 2)), dma((RING,)), dma((AHEAD, 2)), dma((AHEAD, 2)), regular]
        for ring in rings:
            sems += [dma((ring,)), dma((ring,)), regular]
        return [pltpu.VMEM(shape, BF) for shape in shapes] + sems

    def greet(self):
        barrier = pltpu.get_barrier_semaphore()
        for peer in self.peers:
            pl.semaphore_signal(barrier, inc=1, device_id=peer, device_id_type=MESH_ID)
        pl.semaphore_wait(barrier, len(self.peers))

    def start(self):
        for c in range(min(AHEAD, self.total)):
            self.begin(Step(c))

    def send(self, t):
        @within(t, 0, self.total)
        def _():
            self.core_stage(t)

    def step(self, t):
        for i, stage in enumerate(self.stages):
            c = t + (-DELAY - i)

            @within(c, 0, self.total)
            def _(c=c, stage=stage):
                stage(c)

    def load_next(self, t):
        @within(t, 0, self.total - AHEAD)
        def _():
            pl.semaphore_wait(self.core_free, 1)
            self.begin(t + AHEAD)

    def remote(self, stage, ring, c, source, target, peer):
        return pltpu.make_async_remote_copy(
            src_ref=source,
            dst_ref=target,
            send_sem=self.send_sem[stage].at[c.value % ring],
            recv_sem=self.recv[stage].at[c.value % ring],
            device_id=peer,
            device_id_type=MESH_ID,
        )

    def give(self, stage, ring, c, peer):
        @within(c, 0, self.total - ring)
        def _():
            pl.semaphore_signal(
                self.free[stage], inc=1, device_id=peer, device_id_type=MESH_ID
            )

    def take(self, stage, ring, c):
        @within(c, ring, self.total)
        def _():
            pl.semaphore_wait(self.free[stage], 1)

    def core_copy(self, c, side, source):
        return pltpu.make_async_remote_copy(
            src_ref=source,
            dst_ref=self.core_in.at[c.value % AHEAD, side],
            send_sem=self.core_send.at[c.value % AHEAD, side],
            recv_sem=self.core_recv.at[c.value % AHEAD, side],
            device_id=self.core_peer,
            device_id_type=MESH_ID,
        )

    def load(self, c, side, source):
        return pltpu.make_async_copy(
            source, self.own.at[c.value % AHEAD, side], self.load_sem.at[c.value % AHEAD, side]
        )

    def begin(self, c):
        first = 0
        for group, count in zip(self.groups, self.counts):

            @within(c, first, first + count)
            def _(group=group, first=first):
                at = c.value - first
                for side in range(2):
                    self.core_copy(c, side, group.at[2 * side + 1, at]).start()
                for side in range(2):
                    self.load(c, side, group.at[2 * side, at]).start()

            first += count

    def y_copy(self, c):
        return self.remote(0, Y_RING, c, self.far.at[c.value % FAR_RING], self.y_in.at[c.value % Y_RING], self.y_peer)

    def x_copy(self, c):
        source = self.y_in.at[c.value % Y_RING, 1 - self.x]
        return self.remote(1, RING, c, source, self.x_in.at[c.value % RING], self.x_peer)

    def z_copy(self, c):
        source = self.x_in.at[c.value % RING, 1 - self.z]
        return self.remote(2, RING, c, source, self.z_in.at[c.value % RING], self.z_peer)

    def w_copy(self, i, c):
        source = self.z_in if i == 0 else self.w_in[i - 1]
        return self.remote(
            3 + i, RING, c, source.at[c.value % RING], self.w_in[i].at[c.value % RING], self.row_peers[2 + i]
        )

    def back_z_copy(self, c, place):
        at = self.out.at[c.value, self.x, place]
        return self.remote(3 + len(self.w_in), RING, c, self.kept.at[c.value % RING], at, self.z_peer)

    def kept_copy(self, c):
        at = self.out.at[c.value, self.x, self.z]
        return pltpu.make_async_copy(self.kept.at[c.value % RING], at, self.kept_sem.at[c.value % RING])

    def back_x_copy(self, c, place):
        at = self.out.at[c.value, place]
        return self.remote(4 + len(self.w_in), RING, c, at, at, self.x_peer)

    def core_stage(self, c):
        slot, at = c.value % AHEAD, c.value % FAR_RING
        for side in range(2):
            self.load(c, side, self.own.at[slot, side]).wait()
            self.core_copy(c, side, self.own.at[slot, side]).wait()
        self.far[at] = add(self.own[slot, 1], self.core_in[slot, 1])
        self.take(0, Y_RING, c)
        self.y_copy(c).start()
        self.near[at] = add(self.own[slot, 0], self.core_in[slot, 0])

        @within(c, 0, self.total - AHEAD)
        def _():
            pl.semaphore_signal(
                self.core_free, inc=1, device_id=self.core_peer, device_id_type=MESH_ID
            )

    def y_stage(self, c):
        self.y_copy(c).wait()
        slot = c.value % Y_RING
        self.y_in[slot] = add(self.y_in[slot], self.near[c.value % FAR_RING])
        self.take(1, RING, c)
        self.x_copy(c).start()

    def x_stage(self, c):
        self.x_copy(c).wait()
        slot = c.value % RING
        self.x_in[slot] = add(self.x_in[slot], self.y_in[c.value % Y_RING, self.x])
        self.give(0, Y_RING, c, self.y_peer)
        self.take(2, RING, c)
        self.z_copy(c).start()

    def z_stage(self, c):
        self.z_copy(c).wait()
        slot = c.value % RING
        self.z_in[slot] = add(self.z_in[slot], self.x_in[slot, self.z])
        self.give(1, RING, c, self.x_peer)
        self.take(3, RING, c)
        self.w_copy(0, c).start()

    def w_stage(self, i, c):
        self.w_copy(i, c).wait()
        slot = c.value % RING
        source = self.z_in if i == 0 else self.w_in[i - 1]
        value = add(self.w_in[i][slot], source[slot])
        giver = self.z_peer if i == 0 else self.row_peers[1 + i]
        self.give(2 + i, RING, c, giver)
        if i + 1 < len(self.w_in):
            self.w_in[i][slot] = value
            self.take(4 + i, RING, c)
            self.w_copy(i + 1, c).start()
        else:
            self.kept[slot] = value
            self.give(3 + i, RING, c, self.row_peers[2 + i])
            self.kept_copy(c).start()
            self.back_z_copy(c, self.z).start()

    def back_z_stage(self, c):
        self.kept_copy(c).wait()
        self.back_z_copy(c, self.z).wait_send()
        self.back_z_copy(c, 1 - self.z).wait_recv()
        self.back_x_copy(c, self.x).start()

    def back_x_stage(self, c):
        self.back_x_copy(c, self.x).wait_send()
        self.back_x_copy(c, 1 - self.x).wait_recv()


def reduce_kernel(counts, row_bits, *refs):
    count = len(counts)
    reducer = Reducer(refs[:count], counts, row_bits, refs[count], refs[count + 1 :])
    reducer.greet()
    reducer.start()

    def step(t, carry):
        t = Step(t, 0, reducer.steps - 1)
        reducer.send(t)
        reducer.step(t)
        reducer.load_next(t)
        return carry

    lax.fori_loop(0, reducer.steps, step, 0)


def chunk_view(group):
    turns, rows, d = group.shape
    return group.reshape(turns, rows // CHUNK, 2, 2, QUARTER, d)


def split_sums(result, counts):
    d = result.shape[-1]
    sums, first = [], 0
    for n in counts:
        sums.append(result[first : first + n].reshape(n * CHUNK, d))
        first += n
    return sums


def reduce_all(place, groups):
    d = groups[0].shape[-1]
    counts = [g.shape[1] // CHUNK for g in groups]
    row_bits = place.bits("row")
    result = pl.pallas_call(
        functools.partial(reduce_kernel, counts, row_bits),
        in_specs=[pl.BlockSpec(memory_space=pl.ANY)] * len(groups),
        out_specs=pl.BlockSpec(memory_space=pl.ANY),
        out_shape=jax.ShapeDtypeStruct((sum(counts), 2, 2, QUARTER, d), BF),
        scratch_shapes=Reducer.scratch(row_bits, d),
        compiler_params=pltpu.CompilerParams(
            collective_id=0, has_side_effects=True, vmem_limit_bytes=48 * 2**20
        ),
        cost_estimate=cost(0, 4 * sum(counts) * CHUNK * d),
        name="reduce_all",
    )(*[chunk_view(g) for g in groups])
    return split_sums(result, counts)


def xor(left, right, bits):
    total = 0
    for bit in bits:
        a, b = (left // bit) % 2, (right // bit) % 2
        total = total + bit * (a + b - 2 * a * b)
    return total


HALF = 2 * CHUNK


def pair_back(pair, width, q, k, v, grad, wo, mixed, logs, bias, dks, dvs, put):
    length = logs.shape[0]
    for number, here in enumerate(tiles_of(length)):
        lane = lax.broadcasted_iota(jnp.int32, (here.stop - here.start, LANES), 1)
        queries = q(here) * BF(HD**-0.5)
        grads = nt(grad[here, :], wo).astype(BF)
        product = grads.astype(F32) * mixed(here).astype(F32)
        kept = logs[here, :]
        sides = []
        for head in range(2):
            mine = (lane < HD) if head == 0 else (lane >= HD)
            own_q = jnp.where(mine, queries, BF(0))
            own_grad = jnp.where(mine, grads, BF(0))
            chosen = lane == 2 * pair + head
            log_sum = jnp.sum(jnp.where(chosen, kept, 0.0), axis=1, keepdims=True)
            center = jnp.sum(jnp.where(mine, product, 0.0), axis=1, keepdims=True)
            probs = jnp.exp(nt(own_q, k) + bias[here, :width] - log_sum)
            score_grad = (probs * (nt(own_grad, v) - center)).astype(BF)
            sides.append(nn(score_grad, k))
            value_part = nn(own_grad.T, probs.astype(BF))
            key_part = nn(own_q.T, score_grad)
            if number == 0 and head == 0:
                dvs[:, :width] = value_part
                dks[:, :width] = key_part
            else:
                dvs[:, :width] += value_part
                dks[:, :width] += key_part
        put(here, (jnp.where(lane < HD, sides[0], sides[1]) * HD**-0.5).astype(BF))


NEAR = (
    "dec_q_seg", "enc_k_seg", "dec_k_seg", "enc_q_seg", "all_k_seg", "cross_q", "cross_mixed",
    "cross_logs", "cross_low", "dec_low", "memory", "ffn_gain_grad", "gains",
)
LATER = (
    "mid_low", "enc_mixed", "enc_logs", "fetched", "self_proj", "self_mixed", "self_logs",
    "self_low", "dec_new", "first", "answers",
)
FAR = (
    "encoded", "pairs", "cross", "cross_out", "mid", "tokens", "dec_qkv", "w_in", "w_out", "slope",
    "hidden", "enc_low", "w_qkv", "enc_proj", "attn_out", "self_out",
)


class Named:
    pass


def backward_kernel(counts, row_bits, memories, *refs):
    x, refs = Named(), list(refs)
    for name in NEAR + FAR:
        setattr(x, name, refs.pop(0))
    later_sources = [refs.pop(0) for _ in LATER]
    groups = [refs.pop(0) for _ in counts]
    out, cross_part, ff_out_part, ff_in_part, squares_part, self_part = refs[:6]
    token_grad, answer_grad, gain_sums = refs[6:9]
    (g, total, acc, low, g_low, pg, dq, dk, dv, dmk, dmv, bias, ks, vs, dks, dvs) = refs[9:25]
    (b0, b1, b2, b3, dcq, new2, low2, stage_a, stage_b) = refs[25:34]
    gain_acc, gain_in, copy_sem, later_sem, gain_send, gain_recv = refs[34:40]
    refs = refs[40:]
    later_targets = [refs.pop(0) for _ in LATER]
    for name, target in zip(LATER, later_targets):
        setattr(x, name, target)
    parts = [cross_part, ff_out_part, ff_in_part, squares_part, self_part]
    all_counts = list(counts) + [part.shape[1] for part in parts]
    reducer = Reducer(list(groups) + parts, all_counts, row_bits, out, refs)
    me = lax.axis_index("dp")
    d = g.shape[1]
    length, dec_length, count, width = g.shape[0], dcq.shape[0], b1.shape[0], bias.shape[1]
    blocks, pairs = ff_out_part.shape[1], d // LANES
    tiles = tiles_of(length)
    dsq, dsk, dsv = [g_low.at[i * dec_length : (i + 1) * dec_length] for i in range(3)]

    def fetch(source, target, i):
        return pltpu.make_async_copy(source, target, copy_sem.at[i])

    def lanes_of(pair):
        return pl.ds(pl.multiple_of(pair * LANES, LANES), LANES)

    later = [
        pltpu.make_async_copy(source, target, later_sem.at[i])
        for i, (source, target) in enumerate(zip(later_sources, later_targets))
    ]
    first_loads = [
        fetch(x.pairs.at[0], b1, 7),
        fetch(x.pairs.at[1], b2, 8),
        fetch(x.cross_out, b3, 9),
    ]
    encoded_load = fetch(x.encoded, b0, 6)
    early = [fetch(x.cross.at[1], dv, 0), fetch(x.cross.at[2], pg, 1), fetch(x.mid, token_grad, 2)]
    attend_loads = [
        fetch(x.enc_proj.at[0], b0, 6),
        fetch(x.enc_proj.at[1], b1, 7),
        fetch(x.enc_proj.at[2], b2, 8),
        fetch(x.attn_out, b3, 9),
    ]
    low_load = fetch(x.enc_low, b0, 6)
    qkv_loads = [fetch(x.w_qkv.at[i], target, 7 + i) for i, target in enumerate((b1, b2, b3))]
    tokens_load = fetch(x.tokens, pg, 10)
    cross_load = fetch(x.cross.at[0], b0, 6)
    self_out_load = fetch(x.self_out, low, 3)
    dec_qkv_loads = [fetch(x.dec_qkv.at[i], target, 11 + i) for i, target in enumerate((dq, dk, dv))]

    def ff_blocks(j):
        lanes = pl.ds(pl.multiple_of(j * d, d), d)
        return [
            fetch(x.w_in.at[:, lanes], b0, 6),
            fetch(x.w_out.at[lanes], b1, 7),
            fetch(x.slope.at[:, lanes], b2, 8),
            fetch(x.hidden.at[:, lanes], b3, 9),
        ]

    def start_all(copies):
        for copy in copies:
            copy.start()

    def wait_all(copies):
        for copy in copies:
            copy.wait()

    def product_to_acc(acts, grads):
        for n in range(0, d, HALF):
            acc[n : n + HALF, :] = tn(grads[:, n : n + HALF], acts[...])

    def shares(stage):
        for turn in range(4):
            shard = xor(me, turn, (1, 2))
            for i in range(4):
                start = pl.multiple_of(shard * CHUNK + i * QUARTER, 16)
                stage[turn, i // 2, i % 2] = acc[pl.ds(start, QUARTER), :].astype(BF)

    now = [0]

    def once(compute, copies=()):
        t = Step(now[0])
        now[0] += 1
        reducer.send(t)
        compute()
        start_all(copies)
        reducer.step(t)
        wait_all(copies)
        reducer.load_next(t)

    def loop(number, compute, copies=lambda i: ()):
        first = now[0]
        now[0] += number

        def body(i, carry):
            t = Step(first + i, first, first + number - 1)
            reducer.send(t)
            compute(i)
            reducer.step(t)
            wait_all(copies(i))
            reducer.load_next(t)
            return carry

        lax.fori_loop(0, number, body, 0)

    def squares(part, items, before=None, after=None):
        for n in range(0, len(items), 2):

            def compute(n=n):
                if n == 0 and before:
                    before()
                for stage, (acts, grads) in zip((stage_a, stage_b), items[n : n + 2]):
                    product_to_acc(acts, grads)
                    shares(stage)
                if n + 2 >= len(items) and after:
                    after()

            once(
                compute,
                [fetch(stage_a, part.at[:, n], 4), fetch(stage_b, part.at[:, n + 1], 5)],
            )

    start_all(first_loads)
    encoded_load.start()
    start_all(early)
    start_all(later)
    reducer.greet()
    reducer.start()
    ks[count:, :] = jnp.zeros((width - count, LANES), BF)
    vs[count:, :] = jnp.zeros((width - count, LANES), BF)
    gain_acc[0] = jnp.zeros_like(gain_acc[0])
    gain_acc[0, 4:5, :] = x.ffn_gain_grad[...]
    fill_bias(x.dec_q_seg, x.enc_k_seg, bias.at[:dec_length, :count], False, dec_length)
    wait_all(first_loads)

    def cross_attention(i):
        for side in range(2):
            pair = 2 * i + side
            lanes = lanes_of(pair)

            def put(here, value):
                dcq[here, lanes] = value

            pair_back(
                pair, count, lambda here: x.cross_q[0, here, lanes], b1[:, lanes], b2[:, lanes],
                x.dec_low, b3[lanes, :], lambda here: x.cross_mixed[here, lanes], x.cross_logs,
                bias, dks, dvs, put,
            )
            dq[:, lanes] = dks[:, :count].T.astype(BF)
            dk[:, lanes] = dvs[:, :count].T.astype(BF)

    loop(pairs // 2, cross_attention)
    squares(
        cross_part,
        [(x.cross_mixed, x.dec_low), (x.cross_low, dcq), (b0, dq), (b0, dk)],
        encoded_load.wait,
        lambda: start_all(ff_blocks(0)),
    )

    wait_all(early)
    wait_all(later)
    for here in tiles:
        value = nt(dq[here, :], dv[...]) + nt(dk[here, :], pg[...])
        g[here, :] = value
        g_low[here, :] = value.astype(BF)
        total[here, :] = jnp.zeros_like(value)

    def ff_copies(j):
        return [
            fetch(stage_a, ff_out_part.at[:, j], 4),
            fetch(stage_b, ff_in_part.at[xor(me, j, (1, 2))], 5),
        ]

    def feed_forward(j):
        wait_all(ff_blocks(j))
        for here in tiles:
            block = (nt(g_low[here, :], b1[...]) * b2[here, :].astype(F32)).astype(BF)
            pg[here, :] = block
            total[here, :] += nt(block, b0[...])
        product_to_acc(b3, g_low)
        shares(stage_a)
        for n in range(0, d, HALF):
            value = tn(x.mid_low[:, n : n + HALF], pg[...])
            for i in range(8):
                stage_b[n // CHUNK + i // 4, (i // 2) % 2, i % 2] = value[
                    i * QUARTER : (i + 1) * QUARTER, :
                ].astype(BF)
        start_all(ff_copies(j))

        @pl.when(j < blocks - 1)
        def _():
            start_all(ff_blocks(j + 1))

        @pl.when(j == blocks - 1)
        def _():
            start_all(attend_loads)

    loop(blocks, feed_forward, ff_copies)

    gain_sum = jnp.zeros((1, d), F32)
    for here in tiles:
        back, gain_part = rms_back(token_grad[here, :], x.gains[1:2, :], total[here, :])
        gain_sum = gain_sum + gain_part
        value = g[here, :] + back
        g[here, :] = value
        low[here, :] = value.astype(BF)
    gain_acc[0, 1:2, :] = gain_sum
    tokens_load.start()

    fill_bias(x.enc_q_seg, x.all_k_seg, bias, False, tiles[0].stop)
    wait_all(attend_loads)

    def attention(pair):
        lanes = lanes_of(pair)
        ks[:count, :] = b1[:, lanes]
        vs[:count, :] = b2[:, lanes]
        ks[count : count + memories, :] = x.memory[0, :, lanes]
        vs[count : count + memories, :] = x.memory[1, :, lanes]

        def put(here, value):
            dq[here, lanes] = value

        pair_back(
            pair, width, lambda here: b0[here, lanes], ks[...], vs[...], low, b3[lanes, :],
            lambda here: x.enc_mixed[here, lanes], x.enc_logs, bias, dks, dvs, put,
        )
        dk[:, lanes] = dks[:, :count].T.astype(BF)
        dv[:, lanes] = dvs[:, :count].T.astype(BF)
        dmk[:, lanes] = dks[:, count:].T[:memories].astype(BF)
        dmv[:, lanes] = dvs[:, count:].T[:memories].astype(BF)

        @pl.when(pair == pairs - 1)
        def _():
            low_load.start()
            start_all(qkv_loads)

    loop(pairs, attention)

    def after_squares():
        cross_load.start()
        self_out_load.start()

    squares(
        squares_part,
        [(b0, dq), (b0, dk), (b0, dv), (x.enc_mixed, low), (x.fetched, dmk), (x.fetched, dmv)],
        low_load.wait,
        after_squares,
    )

    def token_gradient():
        wait_all(qkv_loads)
        tokens_load.wait()
        gain_sum = jnp.zeros((1, d), F32)
        for here in tiles:
            value = nt(dq[here, :], b1[...]) + nt(dk[here, :], b2[...]) + nt(dv[here, :], b3[...])
            back, gain_part = rms_back(pg[here, :].astype(F32), x.gains[0:1, :], value)
            gain_sum = gain_sum + gain_part
            token_grad[here, :] = g[here, :] + back
        gain_acc[0, 0:1, :] = gain_sum
        start_all(dec_qkv_loads)

    once(token_gradient)

    def to_first():
        cross_load.wait()
        back, gain_acc[0, 3:4, :] = rms_back(x.first[...], x.gains[3:4, :], nt(dcq[...], b0[...]))
        value = x.dec_new[...] + back
        new2[...] = value
        low2[...] = value.astype(BF)
        fill_bias(x.dec_q_seg, x.dec_k_seg, bias.at[:dec_length, :dec_length], True, dec_length)
        self_out_load.wait()

    once(to_first)

    def self_attention(i):
        for side in range(2):
            pair = 2 * i + side
            lanes = lanes_of(pair)

            def put(here, value):
                dsq[here, lanes] = value

            pair_back(
                pair, dec_length, lambda here: x.self_proj[0, here, lanes],
                x.self_proj[1, :, lanes], x.self_proj[2, :, lanes], low2, low[lanes, :],
                lambda here: x.self_mixed[here, lanes], x.self_logs, bias, dks, dvs, put,
            )
            dsk[:, lanes] = dks[:, :dec_length].T.astype(BF)
            dsv[:, lanes] = dvs[:, :dec_length].T.astype(BF)

    loop(pairs // 2, self_attention)
    squares(
        self_part,
        [(x.self_low, dsq), (x.self_low, dsk), (x.self_low, dsv), (x.self_mixed, low2)],
    )

    def answer_gradient():
        wait_all(dec_qkv_loads)
        value = nt(dsq[...], dq[...]) + nt(dsk[...], dk[...]) + nt(dsv[...], dv[...])
        back, gain_acc[0, 2:3, :] = rms_back(x.answers[...].astype(F32), x.gains[2:3, :], value)
        answer_grad[...] = new2[...] + back

    once(answer_gradient)

    def gain_copy(i):
        return pltpu.make_async_remote_copy(
            src_ref=gain_acc.at[i],
            dst_ref=gain_in.at[i],
            send_sem=gain_send.at[i],
            recv_sem=gain_recv.at[i],
            device_id=reducer.peers[i],
            device_id_type=MESH_ID,
        )

    last = len(reducer.peers)

    def gain_step(i):
        if i:
            gain_copy(i - 1).wait()
            value = gain_acc[i - 1] + gain_in[i - 1]
            if i < last:
                gain_acc[i] = value
            else:
                gain_sums[...] = value
        if i < last:
            gain_copy(i).start()

    gain_step(0)
    for i in range(1, last + 1):
        once(lambda: None)
        gain_step(i)
    loop(reducer.steps - now[0], lambda i: None)


def backward(place, groups, x):
    t, d = x["tokens"].shape
    dec_t = x["answers"].shape[0]
    ff = x["w_in"].shape[1]
    blocks, memories = ff // d, x["fetched"].shape[0]
    width = x["all_k_seg"].shape[1]
    row_bits = place.bits("row")
    counts = [g.shape[1] // CHUNK for g in groups]
    new = [4, blocks, ff // (4 * CHUNK), 6, 4]
    total = sum(counts) + sum(new)
    exchanges = 2 + len(row_bits)
    anywhere = pl.BlockSpec(memory_space=pl.ANY)
    vmem = pl.BlockSpec(memory_space=pltpu.VMEM)
    operands = [(x[name], vmem) for name in NEAR]
    operands += [(x[name], anywhere) for name in FAR + LATER]
    operands += [(chunk_view(g), anywhere) for g in groups]
    chunk = (2, 2, QUARTER, d)
    out_shape = [jax.ShapeDtypeStruct((total,) + chunk, BF)]
    out_shape += [jax.ShapeDtypeStruct((4, n) + chunk, BF) for n in new]
    out_shape += [
        jax.ShapeDtypeStruct((t, d), F32),
        jax.ShapeDtypeStruct((dec_t, d), F32),
        jax.ShapeDtypeStruct((8, d), F32),
    ]
    square = lambda kind: pltpu.VMEM((t, d), kind)
    scratch = (
        [square(F32), square(F32), pltpu.VMEM((d, d), F32)]
        + [square(BF)] * 6
        + [pltpu.VMEM((memories, d), BF)] * 2
        + [pltpu.VMEM((t, width), F32)]
        + [pltpu.VMEM((width, LANES), BF)] * 2
        + [pltpu.VMEM((LANES, width), F32)] * 2
        + [square(BF)] * 4
        + [pltpu.VMEM((dec_t, d), BF), pltpu.VMEM((dec_t, d), F32), pltpu.VMEM((dec_t, d), BF)]
        + [pltpu.VMEM((4,) + chunk, BF), pltpu.VMEM((4,) + chunk, BF)]
        + [pltpu.VMEM((exchanges, 8, d), F32)] * 2
        + [pltpu.SemaphoreType.DMA((14,)), pltpu.SemaphoreType.DMA((len(LATER),))]
        + [pltpu.SemaphoreType.DMA((exchanges,))] * 2
        + [pltpu.VMEM(x[name].shape, x[name].dtype) for name in LATER]
        + Reducer.scratch(row_bits, d)
    )
    results = pl.pallas_call(
        functools.partial(backward_kernel, counts, row_bits, memories),
        in_specs=[spec for _, spec in operands],
        out_specs=[anywhere] * 6 + [vmem] * 3,
        out_shape=out_shape,
        scratch_shapes=scratch,
        compiler_params=pltpu.CompilerParams(
            collective_id=1, has_side_effects=True, vmem_limit_bytes=60 * 2**20
        ),
        cost_estimate=cost(2 * t * d * (4 * ff + 14 * d), 30 * total * CHUNK * d),
        name="backward",
    )(*[array for array, _ in operands])
    return results[0], results[6], results[7], results[8]


def finish_kernel(places, index, sums, gain_sums, *refs):
    outs, gain_outs = refs[: len(places)], refs[len(places) : len(places) + 3]
    wide, store_sem = refs[len(places) + 3 :]
    spots = [(out, at, i) for out, (count, at) in zip(outs, places) for i in range(count)]
    total = len(spots)

    def store(c):
        out, at, i = spots[c]
        return pltpu.make_async_copy(
            wide.at[c % 4], out.at[at(i)], store_sem.at[c % 4]
        )

    size = gain_outs[2].shape[1]
    for shard in range(gain_sums.shape[1] // size):

        @pl.when(index[0] == shard)
        def _(shard=shard):
            lanes = slice(shard * size, (shard + 1) * size)
            gain_outs[0][...] = gain_sums[0:2, lanes]
            gain_outs[1][...] = gain_sums[2:4, lanes]
            gain_outs[2][...] = gain_sums[4:5, lanes]

    for c in range(total):
        if c >= 4:
            store(c - 4).wait()
        wide[c % 4] = sums[c].astype(F32)
        store(c).start()
    for c in range(total - 4, total):
        store(c).wait()


def finish_sums(place, sums, gain_sums, blocks):
    d = gain_sums.shape[1]
    total = sums.shape[0]
    one = lambda i: ()
    lead = lambda i: (i,)
    rows = lambda i: (pl.ds(i * CHUNK, CHUNK), slice(None))
    lanes = lambda i: (slice(None), pl.ds(i * d, d))
    flat, tall, wide = (CHUNK, d), (blocks * CHUNK, d), (CHUNK, blocks * d)
    kinds = [
        (wide, blocks, lanes),
        (tall, blocks, rows),
        (flat, 1, one),
        ((3,) + flat, 3, lead),
        (wide, blocks, lanes),
        (tall, blocks, rows),
        ((3,) + flat, 3, lead),
        (flat, 1, one),
        ((2,) + flat, 2, lead),
        ((3,) + flat, 3, lead),
        (flat, 1, one),
    ]
    anywhere = pl.BlockSpec(memory_space=pl.ANY)
    gain_shapes = [(2, CHUNK), (2, CHUNK), (1, CHUNK)]
    return pl.pallas_call(
        functools.partial(finish_kernel, [(count, at) for _, count, at in kinds]),
        in_specs=[
            pl.BlockSpec(memory_space=pltpu.SMEM),
            full((total, CHUNK, d)),
            full((8, d)),
        ],
        out_specs=[anywhere] * len(kinds) + [full(shape) for shape in gain_shapes],
        out_shape=[jax.ShapeDtypeStruct(shape, F32) for shape, _, _ in kinds]
        + [jax.ShapeDtypeStruct(shape, F32) for shape in gain_shapes],
        scratch_shapes=[
            pltpu.VMEM((4, CHUNK, d), F32),
            pltpu.SemaphoreType.DMA((4,)),
        ],
        compiler_params=params(24),
        cost_estimate=cost(0, 6 * total * CHUNK * d),
        name="finish_sums",
    )(place.index, sums, gain_sums)


def fold_outer(place, value):
    while value.shape[0] > 4:
        half = value.shape[0] // 2
        value = add(value[:half], place.swap(value[half:], "dp", half))
    return value


def gain_group(place, gains):
    shards = place.sizes["dp"]
    count, d = gains.shape
    parts = gains.reshape(count, shards, -1)
    turned = jnp.stack(
        [lax.dynamic_index_in_dim(parts, place.dp ^ turn, 1, False) for turn in range(shards)]
    )
    return jnp.pad(turned.astype(BF), ((0, 0), (0, CHUNK - count), (0, d - parts.shape[2])))


def weights_of(value, count, size):
    value = value[: count * size].reshape(count, size, -1)
    return jnp.swapaxes(value, 1, 2).astype(F32)


def encoder_back(
    place, groups, q_seg, k_seg, dck, dcv, cross, mid, tokens, dec_gain_grads, gains,
    w_in, w_out, slope, hidden, mid_low, qkv, memory, mixed, logs, wo, enc_low, fetched, w_qkv,
):
    pre_grad, grad_low, new, low, mid_gain_grad = ffn_back(
        (dck, dcv), cross, w_in, w_out, slope, mid, gains[1]
    )
    dq, dk, dv, dmk, dmv = attend_back(
        (qkv, 0), (qkv, 1), (qkv, 2), mixed, logs, low, wo, q_seg, k_seg, memory
    )
    parts = [
        ff_out_grads(place, hidden, grad_low),
        ff_in_grads(place, mid_low, pre_grad),
        square_grads(place, [(enc_low, [dq, dk, dv]), (mixed, [low]), (fetched, [dmk, dmv])]),
    ]
    token_grad, _, enc_gain_grad = proj_back(tokens, gains[0], new, w_qkv, [dq, dk, dv])
    gain_part = gain_group(
        place, jnp.concatenate([enc_gain_grad, mid_gain_grad] + dec_gain_grads)
    )
    parts = [fold_outer(place, part) for part in groups + parts + [gain_part]]
    sums = reduce_all(place, parts)
    size = tokens.shape[1] // place.sizes["dp"]
    return sums, token_grad, sums[-1][:5, :size].astype(F32)


def fetch_memory(place, table, ids):
    rows = table.shape[0]
    others = range(1, place.sizes["dp"])
    wanted = [ids] + [place.swap(ids, "dp", turn) for turn in others]
    local = jnp.concatenate(wanted) - place.dp * rows
    chosen = (local[:, None] == jnp.arange(rows)[None, :]).astype(BF)
    picked = nn(chosen, table).astype(BF).reshape(len(wanted), ids.shape[0], -1)
    result = picked[0]
    for turn in others:
        result = result + place.swap(picked[turn], "dp", turn)
    return result


def on_device(
    sizes,
    enc_input,
    dec_input,
    memory_table,
    memory_ids,
    enc_segments,
    dec_segments,
    enc_qkv,
    enc_attn_out,
    mem_proj,
    enc_gains,
    enc_ff_in,
    enc_ff_out,
    dec_qkv,
    dec_self_out,
    dec_cross,
    dec_cross_out,
    dec_gains,
    dec_ff_in,
    dec_ff_out,
    out_grad,
):
    place = Place(sizes)
    direct = sizes["dp"] == 4
    tokens, answers = enc_input[0], dec_input[0]
    fetched = fetch_memory(place, memory_table, memory_ids.reshape(-1))
    memories = fetched.shape[0]
    all_gains = jnp.concatenate([enc_gains, dec_gains]).astype(F32)
    enc_gain = [(all_gains, i) for i in range(2)]
    dec_gain = [(all_gains, i) for i in range(2, 5)]

    enc_at, dec_at = enc_segments[0], dec_segments[0]
    enc_q_seg, dec_q_seg = enc_at[:, None], dec_at[:, None]
    owner = jnp.arange(memories, dtype=jnp.int32) // TOPK
    padding = jnp.full((-memories % LANES,), -1, jnp.int32)
    all_k_seg = jnp.concatenate([enc_at, owner, padding])[None]
    enc_k_seg, dec_k_seg = enc_at[None], dec_at[None]

    self_low, self_proj = project(answers, dec_gain[0], dec_qkv, 0, 3)
    self_q, self_k, self_v = [(self_proj, j) for j in range(3)]
    self_mixed, self_logs = attend(self_q, self_k, self_v, dec_q_seg, dec_k_seg, causal=True)
    first, cross_low, cross_q = project(
        answers, dec_gain[1], dec_cross, 0, 1, self_mixed, dec_self_out
    )
    cross_q = (cross_q, 0)

    enc_low, enc_proj = project(tokens, enc_gain[0], enc_qkv, 0, 3)
    enc_q, enc_k, enc_v = [(enc_proj, j) for j in range(3)]
    memory = project_plain(fetched, mem_proj, 0, 2)
    enc_mixed, enc_logs = attend(enc_q, enc_k, enc_v, enc_q_seg, all_k_seg, memory)
    middle, mid_low, enc_hidden, enc_slope, encoded = ffn_forward(
        tokens, enc_mixed, enc_attn_out, enc_gain[1], enc_ff_in, enc_ff_out, far=True
    )
    pairs = project_plain(encoded, dec_cross, 1, 2)
    cross_k, cross_v = (pairs, 0), (pairs, 1)
    cross_mixed, cross_logs = attend(cross_q, cross_k, cross_v, dec_q_seg, enc_k_seg)
    second, ffn_low, dec_hidden, dec_slope, final = ffn_forward(
        first, cross_mixed, dec_cross_out, dec_gain[2], dec_ff_in, dec_ff_out
    )

    grad = out_grad[0]
    if direct:
        new, low, ffn_gain_grad, dec_ff_out_part, dec_ff_in_part = ffn_back_weights(
            place, grad, dec_ff_in, dec_ff_out, dec_slope, dec_hidden, ffn_low, second, dec_gain[2]
        )
        d = tokens.shape[1]
        result, token_grad, answer_grad, gain_sums = backward(
            place,
            [dec_ff_out_part, dec_ff_in_part],
            dict(
                dec_q_seg=dec_q_seg, enc_k_seg=enc_k_seg, dec_k_seg=dec_k_seg,
                enc_q_seg=enc_q_seg, all_k_seg=all_k_seg, encoded=encoded, cross=dec_cross,
                mid=middle, tokens=tokens, dec_qkv=dec_qkv, w_in=enc_ff_in, w_out=enc_ff_out,
                slope=enc_slope, hidden=enc_hidden, enc_low=enc_low, w_qkv=enc_qkv,
                cross_q=cross_q[0], pairs=pairs, cross_mixed=cross_mixed, cross_out=dec_cross_out,
                self_proj=self_proj, self_mixed=self_mixed, self_out=dec_self_out,
                enc_proj=enc_proj, memory=memory, attn_out=enc_attn_out, cross_logs=cross_logs,
                cross_low=cross_low, self_logs=self_logs, self_low=self_low, dec_low=low,
                dec_new=new, first=first, answers=answers, mid_low=mid_low, enc_mixed=enc_mixed,
                enc_logs=enc_logs, fetched=fetched, ffn_gain_grad=ffn_gain_grad,
                gains=all_gains,
            ),
        )
        (
            dec_out_grad, dec_in_grad, cross_out_grad, cross_grad, out_ff_grad, in_ff_grad,
            qkv_grad, attn_out_grad, mem_grad, self_grad, self_out_grad,
            enc_gain_grad, dec_gain_grad, ffn_gain_grad,
        ) = finish_sums(place, result.reshape(-1, CHUNK, d), gain_sums, enc_ff_in.shape[1] // d)
        turn = lambda value: jnp.swapaxes(value, -1, -2)
        return (
            final[None],
            token_grad[None],
            answer_grad[None],
            turn(qkv_grad),
            turn(attn_out_grad),
            turn(mem_grad),
            enc_gain_grad,
            in_ff_grad,
            turn(out_ff_grad),
            turn(self_grad),
            turn(self_out_grad),
            turn(cross_grad),
            turn(cross_out_grad),
            dec_gain_grad,
            dec_in_grad,
            turn(dec_out_grad),
            ffn_gain_grad[0],
        )

    dec_ff_out_part = ff_out_grads(place, dec_hidden, grad)
    pre_grad, _, new, low, ffn_gain_grad = ffn_back(
        grad, None, dec_ff_in, dec_ff_out, dec_slope, second, all_gains[4:5]
    )
    dec_ff_in_part = ff_in_grads(place, ffn_low, pre_grad)
    dcq, dck, dcv = attend_back(
        cross_q, cross_k, cross_v, cross_mixed, cross_logs, low, dec_cross_out,
        dec_q_seg, enc_k_seg,
    )
    cross_part = square_grads(
        place, [(cross_mixed, [low]), (cross_low, [dcq]), (encoded, [dck, dcv])]
    )
    new, low, cross_gain_grad = proj_back(first, all_gains[3:4], new, dec_cross, [dcq])
    dsq, dsk, dsv = attend_back(
        self_q, self_k, self_v, self_mixed, self_logs, low, dec_self_out,
        dec_q_seg, dec_k_seg, causal=True,
    )
    self_part = square_grads(place, [(self_low, [dsq, dsk, dsv]), (self_mixed, [low])])
    answer_grad, _, self_gain_grad = proj_back(answers, all_gains[2:3], new, dec_qkv, [dsq, dsk, dsv])
    dec_gain_grads = [self_gain_grad, cross_gain_grad, ffn_gain_grad]
    dec_parts = [dec_ff_out_part, dec_ff_in_part, cross_part, self_part]
    sums, token_grad, gains = encoder_back(
        place, dec_parts, enc_q_seg, all_k_seg, dck, dcv, dec_cross, middle, tokens,
        dec_gain_grads, [all_gains[:1], all_gains[1:2]], enc_ff_in, enc_ff_out, enc_slope, enc_hidden, mid_low,
        enc_proj, memory, enc_mixed, enc_logs, enc_attn_out, enc_low, fetched, enc_qkv,
    )
    size = tokens.shape[1] // sizes["dp"]
    blocks = enc_ff_in.shape[1] // tokens.shape[1]
    ff_size = enc_ff_in.shape[1] // sizes["dp"]
    enc_squares = weights_of(sums[6], 6, size)
    self_squares = weights_of(sums[3], 4, size)
    cross_squares = weights_of(sums[2], 4, size)
    return (
        final[None],
        token_grad[None],
        answer_grad[None],
        enc_squares[0:3],
        enc_squares[3],
        enc_squares[4:6],
        gains[0:2],
        weights_of(sums[5], 1, ff_size)[0],
        weights_of(sums[4], blocks, size).reshape(-1, size),
        self_squares[0:3],
        self_squares[3],
        cross_squares[1:4],
        cross_squares[0],
        gains[2:4],
        weights_of(sums[1], 1, ff_size)[0],
        weights_of(sums[0], blocks, size).reshape(-1, size),
        gains[4],
    )


def solution(mesh):
    rows = P(("row", "dp"), None, None)
    in_specs = (
        (rows, rows, P("dp", None), rows, P(("row", "dp"), None), P(("row", "dp"), None))
        + (P(),) * 13
        + (rows,)
    )
    cube, flat = P(None, None, "dp"), P(None, "dp")
    out_specs = (
        (rows, rows, rows)
        + (cube, flat, cube, flat, flat, flat)
        + (cube, flat, cube, flat, flat, flat, flat)
        + (P("dp"),)
    )
    return jax.shard_map(
        functools.partial(on_device, dict(mesh.shape)),
        mesh=mesh,
        in_specs=in_specs,
        out_specs=out_specs,
        check_vma=False,
    )
```

```python
import functools

import jax
import jax.numpy as jnp
from jax import lax
from jax.experimental import pallas as pl
from jax.experimental.pallas import tpu as pltpu
from jax.sharding import PartitionSpec as P

HD = 64
TOPK = 10
LANES = 128
MASKED = -1e30
BF = jnp.bfloat16
F32 = jnp.float32


def nn(left, right):
    return lax.dot_general(left, right, (((1,), (0,)), ((), ())), preferred_element_type=F32)


def nt(left, right):
    return lax.dot_general(left, right, (((1,), (1,)), ((), ())), preferred_element_type=F32)


def tn(left, right):
    return lax.dot_general(left, right, (((0,), (0,)), ((), ())), preferred_element_type=F32)


def full(shape):
    return pl.BlockSpec(shape, lambda *_: (0,) * len(shape))


def params(mib=16):
    return pltpu.CompilerParams(vmem_limit_bytes=mib * 2**20)


def cost(flops, nbytes, exps=0):
    return pl.CostEstimate(flops=int(flops), bytes_accessed=int(nbytes), transcendentals=int(exps))


def rms_scale(x):
    return lax.rsqrt(jnp.mean(x * x, axis=-1, keepdims=True) + 1e-06)


def rms_back(x, gain, dy):
    scale = rms_scale(x)
    gain_grad = jnp.sum(dy * x * scale, axis=0, keepdims=True)
    inner = dy * gain
    mixed = jnp.mean(inner * x, axis=-1, keepdims=True)
    return scale * (inner - x * (scale * scale) * mixed), gain_grad


def proj_kernel(residual, index, x, gains, *refs):
    if residual:
        mixed, wo, w, mid, low, out = refs
    else:
        w, low, out = refs

    @pl.when(pl.program_id(0) == 0)
    def _():
        value = x[...].astype(F32)
        if residual:
            value = value + nn(mixed[...], wo[...])
            mid[...] = value
        low[...] = (value * rms_scale(value) * gains[index : index + 1, :]).astype(BF)

    out[...] = nn(low[...], w[...]).astype(BF)


def project(x, gain, w, first, count, mixed=None, wo=None):
    t, d = x.shape
    gains, index = gain
    residual = mixed is not None
    args = [x, gains]
    specs = [full((t, d)), full(gains.shape)]
    outs = [pltpu.HBM((t, d), BF), pltpu.HBM((count, t, d), BF)]
    out_specs = [full((t, d)), pl.BlockSpec((None, t, d), lambda j: (j, 0, 0))]
    if residual:
        args += [mixed, wo]
        specs += [full((t, d)), full((d, d))]
        outs = [jax.ShapeDtypeStruct((t, d), F32)] + outs
        out_specs = [full((t, d))] + out_specs
    args.append(w)
    specs.append(pl.BlockSpec((None, d, d), lambda j: (first + j, 0, 0)))
    return pl.pallas_call(
        functools.partial(proj_kernel, residual, index),
        grid=(count,),
        in_specs=specs,
        out_specs=out_specs,
        out_shape=outs,
        compiler_params=params(),
        cost_estimate=cost(2 * t * d * d * (count + residual), 2 * d * (t + d) * (count + 2)),
        name="project",
    )(*args)


def pairs_kernel(x, w, out):
    out[...] = nn(x[...], w[...]).astype(BF)


def project_plain(x, w, first, count):
    t, d = x.shape
    return pl.pallas_call(
        pairs_kernel,
        grid=(count,),
        in_specs=[full((t, d)), pl.BlockSpec((None, d, d), lambda j: (first + j, 0, 0))],
        out_specs=pl.BlockSpec((None, t, d), lambda j: (j, 0, 0)),
        out_shape=jax.ShapeDtypeStruct((count, t, d), BF),
        compiler_params=params(),
        cost_estimate=cost(2 * t * d * d * count, 2 * d * (t + d) * count),
        name="project_plain",
    )(x, w)


def proj_back_kernel(count, x, gain, grad, w, *refs):
    parts = refs[:count]
    new, low, gain_grad, total = refs[count:]
    step = pl.program_id(0)
    for j in range(count):

        @pl.when(step == j)
        def _(j=j):
            value = nt(parts[j][...], w[...])
            total[...] = value if j == 0 else total[...] + value

    @pl.when(step == count - 1)
    def _():
        back, gain_grad[...] = rms_back(x[...].astype(F32), gain[...], total[...])
        value = grad[...] + back
        new[...] = value
        low[...] = value.astype(BF)


def proj_back(x, gain, grad, w, parts):
    t, d = x.shape
    count = len(parts)
    return pl.pallas_call(
        functools.partial(proj_back_kernel, count),
        grid=(count,),
        in_specs=[full((t, d)), full((1, d)), full((t, d))]
        + [pl.BlockSpec((None, d, d), lambda j: (j, 0, 0))]
        + [full((t, d))] * count,
        out_specs=[full((t, d)), full((t, d)), full((1, d))],
        out_shape=[
            jax.ShapeDtypeStruct((t, d), F32),
            jax.ShapeDtypeStruct((t, d), BF),
            jax.ShapeDtypeStruct((1, d), F32),
        ],
        scratch_shapes=[pltpu.VMEM((t, d), F32)],
        compiler_params=params(),
        cost_estimate=cost(2 * t * d * d * count, 2 * d * (t + d) * count + 12 * t * d),
        name="proj_back",
    )(x, gain, grad, w, *parts)


GELU_A = 0.7978845608028654
GELU_B = 0.044715


def gelu_parts(pre):
    square = pre * pre
    half = 0.5 + 0.5 * jnp.tanh(pre * (GELU_A + (GELU_A * GELU_B) * square))
    act = pre * half
    slope = half + (act * (1.0 - half)) * (2 * GELU_A + (6 * GELU_A * GELU_B) * square)
    return act.astype(BF), slope.astype(BF)


def tiles_of(length):
    size = min(length, 256)
    return [slice(begin, begin + size) for begin in range(0, length, size)]


def ffn_kernel(index, res, mixed, wo, gains, w_in, w_out, mid, low, hidden, slope, out, total):
    step = pl.program_id(0)
    tiles = tiles_of(res.shape[0])

    @pl.when(step == 0)
    def _():
        for here in tiles:
            value = res[here, :].astype(F32) + nn(mixed[here, :], wo[...])
            mid[here, :] = value
            low[here, :] = (value * rms_scale(value) * gains[index : index + 1, :]).astype(BF)
            total[here, :] = value

    coming = nn(low[tiles[0], :], w_in[...])
    for number, here in enumerate(tiles):
        pre = coming
        if number + 1 < len(tiles):
            coming = nn(low[tiles[number + 1], :], w_in[...])
        act, slope[here, :] = gelu_parts(pre)
        hidden[here, :] = act
        total[here, :] += nn(act, w_out[...])

    @pl.when(step == pl.num_programs(0) - 1)
    def _():
        for here in tiles:
            out[here, :] = total[here, :].astype(BF)


def ffn_forward(res, mixed, wo, gain, w_in, w_out, far=False, block=768):
    t, d = res.shape
    gains, index = gain
    ff = w_in.shape[1]
    kept = pltpu.HBM if far else jax.ShapeDtypeStruct
    return pl.pallas_call(
        functools.partial(ffn_kernel, index),
        grid=(ff // block,),
        in_specs=[
            full((t, d)),
            full((t, d)),
            full((d, d)),
            full(gains.shape),
            pl.BlockSpec((d, block), lambda j: (0, j)),
            pl.BlockSpec((block, d), lambda j: (j, 0)),
        ],
        out_specs=[
            full((t, d)),
            full((t, d)),
            pl.BlockSpec((t, block), lambda j: (0, j)),
            pl.BlockSpec((t, block), lambda j: (0, j)),
            full((t, d)),
        ],
        out_shape=[
            kept((t, d), F32),
            kept((t, d), BF),
            kept((t, ff), BF),
            kept((t, ff), BF),
            jax.ShapeDtypeStruct((t, d), BF),
        ],
        scratch_shapes=[pltpu.VMEM((t, d), F32)],
        compiler_params=params(28),
        cost_estimate=cost(2 * t * d * (2 * ff + d), 4 * d * ff + 4 * t * ff + 12 * t * d, t * ff),
        name="ffn_forward",
    )(res, mixed, wo, gains, w_in, w_out)


def ffn_back_kernel(sourced, *refs):
    if sourced:
        dk, dv, wk, wv, w_in, w_out, slope, mid, gain, pre_grad, g_low, new, low, gain_grad, g, total = refs
    else:
        grad, w_in, w_out, slope, mid, gain, pre_grad, g_low, new, low, gain_grad, g, total = refs
    step = pl.program_id(0)

    @pl.when(step == 0)
    def _():
        if sourced:
            value = nt(dk[...], wk[...]) + nt(dv[...], wv[...])
        else:
            value = grad[...].astype(F32)
        g[...] = value
        g_low[...] = value.astype(BF)
        total[...] = jnp.zeros_like(total)

    block = (nt(g_low[...], w_out[...]) * slope[...].astype(F32)).astype(BF)
    pre_grad[...] = block
    total[...] += nt(block, w_in[...])

    @pl.when(step == pl.num_programs(0) - 1)
    def _():
        back, gain_grad[...] = rms_back(mid[...], gain[...], total[...])
        value = g[...] + back
        new[...] = value
        low[...] = value.astype(BF)


def ffn_back(grads, weights, w_in, w_out, slope, mid, gain, block=512):
    t, d = mid.shape
    ff = w_in.shape[1]
    sourced = weights is not None
    if sourced:
        args = [grads[0], grads[1], weights, weights]
        specs = [
            full((t, d)),
            full((t, d)),
            pl.BlockSpec((None, d, d), lambda j: (1, 0, 0)),
            pl.BlockSpec((None, d, d), lambda j: (2, 0, 0)),
        ]
    else:
        args = [grads]
        specs = [full((t, d))]
    return pl.pallas_call(
        functools.partial(ffn_back_kernel, sourced),
        grid=(ff // block,),
        in_specs=specs
        + [
            pl.BlockSpec((d, block), lambda j: (0, j)),
            pl.BlockSpec((block, d), lambda j: (j, 0)),
            pl.BlockSpec((t, block), lambda j: (0, j)),
            full((t, d)),
            full((1, d)),
        ],
        out_specs=[
            pl.BlockSpec((t, block), lambda j: (0, j)),
            full((t, d)),
            full((t, d)),
            full((t, d)),
            full((1, d)),
        ],
        out_shape=[
            jax.ShapeDtypeStruct((t, ff), BF),
            jax.ShapeDtypeStruct((t, d), BF),
            jax.ShapeDtypeStruct((t, d), F32),
            jax.ShapeDtypeStruct((t, d), BF),
            jax.ShapeDtypeStruct((1, d), F32),
        ],
        scratch_shapes=[pltpu.VMEM((t, d), F32), pltpu.VMEM((t, d), F32)],
        compiler_params=params(32),
        cost_estimate=cost(4 * t * d * ff, 4 * d * ff + 4 * t * ff + 16 * t * d),
        name="ffn_back",
    )(*args, w_in, w_out, slope, mid, gain)


def fill_bias(q_seg, k_seg, bias, causal, rows):
    length, width = bias.shape
    for begin in range(0, length, rows):
        allowed = q_seg[begin : begin + rows, :] == k_seg[...]
        if causal:
            at = lax.broadcasted_iota(jnp.int32, (rows, width), 0) + begin
            key = lax.broadcasted_iota(jnp.int32, (rows, width), 1)
            allowed = allowed & (key <= at)
        bias[begin : begin + rows, :] = jnp.where(allowed, 0.0, MASKED)


def join_keys(refs, count, extra, width):
    keys, values, mem_keys, mem_values, all_keys, all_values = refs
    for source, more, target in ((keys, mem_keys, all_keys), (values, mem_values, all_values)):
        target[:count, :] = source[...]
        target[count : count + extra, :] = more[...]


def attend_kernel(extra, causal, rows, *refs):
    if extra:
        q_seg, k_seg, q, k, v, mk, mv, out, logs, bias, ks, vs = refs
    else:
        q_seg, k_seg, q, k, v, out, logs, bias = refs
    length, width = bias.shape
    count = k.shape[0]
    step = pl.program_id(0)

    @pl.when(step == 0)
    def _():
        fill_bias(q_seg, k_seg, bias, causal, rows)
        logs[...] = jnp.zeros_like(logs)
        if extra:
            ks[count:, :] = jnp.zeros((width - count, LANES), BF)
            vs[count:, :] = jnp.zeros((width - count, LANES), BF)

    if extra:
        join_keys((k, v, mk, mv, ks, vs), count, extra, width)
        k, v = ks, vs
    lane = lax.broadcasted_iota(jnp.int32, (rows, LANES), 1)

    def scores_of(begin, head):
        here = slice(begin, begin + rows)
        mine = (lane < HD) if head == 0 else (lane >= HD)
        queries = jnp.where(mine, q[here, :] * BF(HD**-0.5), BF(0))
        return nt(queries, k[...]) + bias[here, :]

    work = [(begin, head) for begin in range(0, length, rows) for head in range(2)]
    coming = scores_of(*work[0])
    for number, (begin, head) in enumerate(work):
        scores = coming
        if number + 1 < len(work):
            coming = scores_of(*work[number + 1])
        top = jnp.max(scores, axis=1, keepdims=True)
        exponent = jnp.exp(scores - top)
        sums = jnp.sum(exponent, axis=1, keepdims=True)
        side = nn(exponent.astype(BF), v[...]) * (1.0 / sums)
        here = slice(begin, begin + rows)
        kept = logs[here, :] if head == 0 else kept
        kept = jnp.where(lane == 2 * step + head, top + jnp.log(sums), kept)
        if head == 0:
            first = side
        else:
            logs[here, :] = kept
            out[here, :] = jnp.where(lane < HD, first, side).astype(BF)


def part_of(stack, index):
    rows = stack.shape[1]
    return pl.BlockSpec((None, rows, LANES), lambda p: (index, 0, p))


def attend(q, k, v, q_seg, k_seg, memory=None, causal=False, rows=256):
    t, d = q[0].shape[1:]
    count = k[0].shape[1]
    width = k_seg.shape[1]
    args = [q_seg, k_seg, q[0], k[0], v[0]]
    specs = [full(q_seg.shape), full(k_seg.shape), part_of(*q), part_of(*k), part_of(*v)]
    scratch = [pltpu.VMEM((t, width), F32)]
    extra = 0
    if memory is not None:
        extra = memory.shape[1]
        args += [memory, memory]
        specs += [part_of(memory, 0), part_of(memory, 1)]
        scratch += [pltpu.VMEM((width, LANES), BF)] * 2
    return pl.pallas_call(
        functools.partial(attend_kernel, extra, causal, rows),
        grid=(d // LANES,),
        in_specs=specs,
        out_specs=[pl.BlockSpec((t, LANES), lambda p: (0, p)), full((t, LANES))],
        out_shape=[jax.ShapeDtypeStruct((t, d), BF), jax.ShapeDtypeStruct((t, LANES), F32)],
        scratch_shapes=scratch,
        compiler_params=params(),
        cost_estimate=cost(16 * t * width * d, 8 * d * (t + count), t * width * d // HD),
        name="attend",
    )(*args)


def attend_back_kernel(extra, causal, rows, *refs):
    if extra:
        q_seg, k_seg, q, k, v, out, logs, grad, wo, mk, mv = refs[:11]
        dq, dk, dv, dmk, dmv, bias, dks, dvs, ks, vs = refs[11:]
    else:
        q_seg, k_seg, q, k, v, out, logs, grad, wo, dq, dk, dv, bias, dks, dvs = refs
    length, width = bias.shape
    count = k.shape[0]
    step = pl.program_id(0)

    @pl.when(step == 0)
    def _():
        fill_bias(q_seg, k_seg, bias, causal, rows)
        if extra:
            ks[count:, :] = jnp.zeros((width - count, LANES), BF)
            vs[count:, :] = jnp.zeros((width - count, LANES), BF)

    if extra:
        join_keys((k, v, mk, mv, ks, vs), count, extra, width)
        k, v = ks, vs
    lane = lax.broadcasted_iota(jnp.int32, (rows, LANES), 1)
    for begin in range(0, length, rows):
        here = slice(begin, begin + rows)
        queries = q[here, :] * BF(HD**-0.5)
        mixed = nt(grad[here, :], wo[...]).astype(BF)
        product = mixed.astype(F32) * out[here, :].astype(F32)
        kept = logs[here, :]
        sides = []
        for head in range(2):
            mine = (lane < HD) if head == 0 else (lane >= HD)
            own_q = jnp.where(mine, queries, BF(0))
            own_grad = jnp.where(mine, mixed, BF(0))
            log_sum = jnp.sum(jnp.where(lane == 2 * step + head, kept, 0.0), axis=1, keepdims=True)
            center = jnp.sum(jnp.where(mine, product, 0.0), axis=1, keepdims=True)
            probs = jnp.exp(nt(own_q, k[...]) + bias[here, :] - log_sum)
            score_grad = (probs * (nt(own_grad, v[...]) - center)).astype(BF)
            sides.append(nn(score_grad, k[...]))
            value_part = nn(own_grad.T, probs.astype(BF))
            key_part = nn(own_q.T, score_grad)
            if begin == 0 and head == 0:
                dvs[...] = value_part
                dks[...] = key_part
            else:
                dvs[...] += value_part
                dks[...] += key_part
        dq[here, :] = (jnp.where(lane < HD, sides[0], sides[1]) * HD**-0.5).astype(BF)
    dk[...] = dks[:, :count].T.astype(BF)
    dv[...] = dvs[:, :count].T.astype(BF)
    if extra:
        dmk[...] = dks[:, count:].T[:extra].astype(BF)
        dmv[...] = dvs[:, count:].T[:extra].astype(BF)


def attend_back(q, k, v, out, logs, grad, wo, q_seg, k_seg, memory=None, causal=False, rows=256):
    t, d = q[0].shape[1:]
    count = k[0].shape[1]
    width = k_seg.shape[1]
    column = lambda n: pl.BlockSpec((n, LANES), lambda p: (0, p))
    args = [q_seg, k_seg, q[0], k[0], v[0], out, logs, grad, wo]
    specs = [full(q_seg.shape), full(k_seg.shape), part_of(*q), part_of(*k), part_of(*v)]
    specs += [column(t), full((t, LANES)), full((t, d)), pl.BlockSpec((LANES, d), lambda p: (p, 0))]
    scratch = [pltpu.VMEM((t, width), F32)] + [pltpu.VMEM((LANES, width), F32)] * 2
    lengths = [t, count, count]
    extra = 0
    if memory is not None:
        extra = memory.shape[1]
        args += [memory, memory]
        specs += [part_of(memory, 0), part_of(memory, 1)]
        scratch += [pltpu.VMEM((width, LANES), BF)] * 2
        lengths += [extra, extra]
    return pl.pallas_call(
        functools.partial(attend_back_kernel, extra, causal, rows),
        grid=(d // LANES,),
        in_specs=specs,
        out_specs=[column(n) for n in lengths],
        out_shape=[jax.ShapeDtypeStruct((n, d), BF) for n in lengths],
        scratch_shapes=scratch,
        compiler_params=params(),
        cost_estimate=cost(32 * t * width * d, 12 * d * (t + count), t * width * d // HD),
        name="attend_back",
    )(*args)


def share_rows(index, acc, out, shards, size):
    for turn in range(shards):
        shard = index[0] ^ turn
        start = pl.multiple_of(shard * size, 16)
        out[turn] = acc[pl.ds(start, size), :].astype(BF)


def squares_kernel(items, shards, index, *refs):
    out, acc = refs[-2:]
    size = acc.shape[0] // shards
    for j, (a, g) in enumerate(items):

        @pl.when(pl.program_id(0) == j)
        def _(a=a, g=g):
            acc[...] = tn(refs[g][...], refs[a][...])
            share_rows(index, acc, out, shards, size)


def pad_rows(rows):
    return -(-rows // CHUNK) * CHUNK


def square_grads(place, products):
    arrays, items = [], []

    def at(array):
        for i, other in enumerate(arrays):
            if other is array:
                return i
        arrays.append(array)
        return len(arrays) - 1

    for acts, grads in products:
        for grad in grads:
            items.append((at(acts), at(grad)))
    shards = place.sizes["dp"]
    d = products[0][0].shape[1]
    size = d // shards
    work = sum(2 * arrays[a].shape[0] * d * d for a, _ in items)
    return pl.pallas_call(
        functools.partial(squares_kernel, items, shards),
        grid=(len(items),),
        in_specs=[pl.BlockSpec(memory_space=pltpu.SMEM)] + [full(x.shape) for x in arrays],
        out_specs=pl.BlockSpec((shards, size, d), lambda j: (0, j, 0)),
        out_shape=jax.ShapeDtypeStruct((shards, pad_rows(len(items) * size), d), BF),
        scratch_shapes=[pltpu.VMEM((d, d), F32)],
        compiler_params=params(),
        cost_estimate=cost(work, sum(2 * x.size for x in arrays) + 2 * len(items) * d * d),
        name="square_grads",
    )(place.index, *arrays)


def out_kernel(shards, index, acts, grad, out, acc):
    acc[...] = tn(grad[...], acts[...])
    share_rows(index, acc, out, shards, acc.shape[0] // shards)


def ff_out_grads(place, acts, grad):
    shards = place.sizes["dp"]
    t, d = grad.shape
    blocks = acts.shape[1] // d
    size = d // shards
    return pl.pallas_call(
        functools.partial(out_kernel, shards),
        grid=(blocks,),
        in_specs=[
            pl.BlockSpec(memory_space=pltpu.SMEM),
            pl.BlockSpec((t, d), lambda j: (0, j)),
            full((t, d)),
        ],
        out_specs=pl.BlockSpec((shards, size, d), lambda j: (0, j, 0)),
        out_shape=jax.ShapeDtypeStruct((shards, blocks * size, d), BF),
        scratch_shapes=[pltpu.VMEM((d, d), F32)],
        compiler_params=params(),
        cost_estimate=cost(2 * t * d * d * blocks, 2 * (t + d) * d * (blocks + 1)),
        name="ff_out_grads",
    )(place.index, acts, grad)


def in_kernel(per_block, index, grad, acts, out):
    acc = tn(grad[...], acts[...]).astype(BF)
    size = acc.shape[0] // per_block
    for i in range(per_block):
        shard = pl.program_id(0) * per_block + i
        out[index[0] ^ shard] = acc[i * size : (i + 1) * size]


def ff_in_grads(place, acts, grad):
    shards = place.sizes["dp"]
    t, d = acts.shape
    ff = grad.shape[1]
    blocks = ff // d
    size = ff // shards
    return pl.pallas_call(
        functools.partial(in_kernel, d // size),
        grid=(blocks,),
        in_specs=[
            pl.BlockSpec(memory_space=pltpu.SMEM),
            pl.BlockSpec((t, d), lambda j: (0, j)),
            full((t, d)),
        ],
        out_specs=full((shards, size, d)),
        out_shape=jax.ShapeDtypeStruct((shards, size, d), BF),
        compiler_params=params(),
        cost_estimate=cost(2 * t * d * ff, 2 * (t + d) * d * (blocks + 1)),
        name="ff_in_grads",
    )(place.index, grad, acts)


def ffn_back_weights_kernel(
    row, index, grad, w_in, w_out, slope, hidden, low_in, mid, gains,
    new, low, gain_grad, out_part, in_part, total, acc,
):
    step = pl.program_id(0)

    @pl.when(step == 0)
    def _():
        total[...] = jnp.zeros_like(total)

    acc[...] = tn(grad[...], hidden[...])
    share_rows(index, acc, out_part, out_part.shape[0], out_part.shape[1])
    block = (nt(grad[...], w_out[...]) * slope[...].astype(F32)).astype(BF)
    total[...] += nt(block, w_in[...])
    in_part[index[0] ^ step] = tn(low_in[...], block).astype(BF)

    @pl.when(step == pl.num_programs(0) - 1)
    def _():
        back, gain_grad[...] = rms_back(
            mid[...], gains[row : row + 1, :], total[...]
        )
        value = grad[...].astype(F32) + back
        new[...] = value
        low[...] = value.astype(BF)


def ffn_back_weights(place, grad, w_in, w_out, slope, hidden, low_in, mid, gain):
    t, d = mid.shape
    gains, row = gain
    blocks = w_in.shape[1] // d
    shards = place.sizes["dp"]
    size = d // shards
    return pl.pallas_call(
        functools.partial(ffn_back_weights_kernel, row),
        grid=(blocks,),
        in_specs=[
            pl.BlockSpec(memory_space=pltpu.SMEM),
            full((t, d)),
            pl.BlockSpec((d, d), lambda j: (0, j)),
            pl.BlockSpec((d, d), lambda j: (j, 0)),
            pl.BlockSpec((t, d), lambda j: (0, j)),
            pl.BlockSpec((t, d), lambda j: (0, j)),
            full((t, d)),
            full((t, d)),
            full(gains.shape),
        ],
        out_specs=[
            full((t, d)),
            full((t, d)),
            full((1, d)),
            pl.BlockSpec((shards, size, d), lambda j: (0, j, 0)),
            full((shards, d, d)),
        ],
        out_shape=[
            jax.ShapeDtypeStruct((t, d), F32),
            jax.ShapeDtypeStruct((t, d), BF),
            jax.ShapeDtypeStruct((1, d), F32),
            pltpu.HBM((shards, blocks * size, d), BF),
            pltpu.HBM((shards, d, d), BF),
        ],
        scratch_shapes=[pltpu.VMEM((t, d), F32), pltpu.VMEM((d, d), F32)],
        compiler_params=params(32),
        cost_estimate=cost(8 * t * d * d * blocks, 8 * d * d * blocks + 24 * t * d),
        name="ffn_back_weights",
    )(place.index, grad, w_in, w_out, slope, hidden, low_in, mid, gains)


def flip(index, bit):
    return index + bit - 2 * bit * ((index // bit) % 2)


class Place:
    def __init__(self, sizes):
        self.sizes = sizes
        self.dp = lax.axis_index("dp")
        self.row = lax.axis_index("row")
        self.index = self.dp.astype(jnp.int32)[None]

    def swap(self, value, axis, turn):
        return lax.ppermute(value, axis, [(i, i ^ turn) for i in range(self.sizes[axis])])

    def bits(self, axis):
        return [1 << i for i in range(self.sizes[axis].bit_length() - 1)]


QUARTER = 48
CHUNK = 4 * QUARTER
AHEAD = 3
DELAY = 1
FAR_RING = DELAY + 2
Y_RING = DELAY + 4
RING = 5
MESH_ID = pl.DeviceIdType.MESH


def add(left, right):
    return (left.astype(F32) + right.astype(F32)).astype(BF)


class Step:
    def __init__(self, value, low=None, high=None):
        self.value = value
        self.low = value if low is None else low
        self.high = value if high is None else high

    def __add__(self, other):
        return Step(self.value + other, self.low + other, self.high + other)


def within(step, low, high):
    if low <= step.low and step.high < high:
        return lambda function: function()
    if step.high < low or step.low >= high:
        return lambda function: None
    return pl.when((step.value >= low) & (step.value < high))


class Reducer:
    def __init__(self, groups, counts, row_bits, out, refs):
        self.groups, self.counts, self.out = groups, counts, out
        self.total = sum(counts)
        others = len(row_bits) - 2
        (self.own, self.core_in, self.far, self.near, self.y_in, self.x_in, self.z_in, self.kept) = refs[:8]
        self.w_in = refs[8 : 8 + others]
        sems = list(refs[8 + others :])
        self.load_sem, self.kept_sem, self.core_send, self.core_recv = sems[:4]
        self.core_free, self.send_sem, self.recv, self.free = sems[4], sems[5::3], sems[6::3], sems[7::3]
        row, dp = lax.axis_index("row"), lax.axis_index("dp")
        self.x, self.z = row % 2, (row // 2) % 2
        self.core_peer = (row, flip(dp, 1))
        self.y_peer = (row, flip(dp, 2))
        self.row_peers = [(flip(row, bit), dp) for bit in row_bits]
        self.x_peer, self.z_peer = self.row_peers[:2]
        self.peers = [self.core_peer, self.y_peer] + self.row_peers
        self.stages = [self.y_stage, self.x_stage, self.z_stage]
        self.stages += [functools.partial(self.w_stage, i) for i in range(others)]
        self.stages += [self.back_z_stage, self.back_x_stage]
        self.steps = self.total + DELAY + len(self.stages) - 1

    @staticmethod
    def scratch(row_bits, d):
        others = len(row_bits) - 2
        chunk = (2, 2, QUARTER, d)
        shapes = [
            (AHEAD, 2) + chunk,
            (AHEAD, 2) + chunk,
            (FAR_RING,) + chunk,
            (FAR_RING,) + chunk,
            (Y_RING,) + chunk,
            (RING,) + chunk[1:],
            (RING,) + chunk[2:],
            (RING,) + chunk[2:],
        ] + [(RING,) + chunk[2:]] * others
        dma = pltpu.SemaphoreType.DMA
        regular = pltpu.SemaphoreType.REGULAR
        rings = [Y_RING, RING, RING] + [RING] * others + [RING, RING]
        sems = [dma((AHEAD, 2)), dma((RING,)), dma((AHEAD, 2)), dma((AHEAD, 2)), regular]
        for ring in rings:
            sems += [dma((ring,)), dma((ring,)), regular]
        return [pltpu.VMEM(shape, BF) for shape in shapes] + sems

    def greet(self):
        barrier = pltpu.get_barrier_semaphore()
        for peer in self.peers:
            pl.semaphore_signal(barrier, inc=1, device_id=peer, device_id_type=MESH_ID)
        pl.semaphore_wait(barrier, len(self.peers))

    def start(self):
        for c in range(min(AHEAD, self.total)):
            self.begin(Step(c))

    def send(self, t):
        @within(t, 0, self.total)
        def _():
            self.core_stage(t)

    def step(self, t):
        for i, stage in enumerate(self.stages):
            c = t + (-DELAY - i)

            @within(c, 0, self.total)
            def _(c=c, stage=stage):
                stage(c)

    def load_next(self, t):
        @within(t, 0, self.total - AHEAD)
        def _():
            pl.semaphore_wait(self.core_free, 1)
            self.begin(t + AHEAD)

    def remote(self, stage, ring, c, source, target, peer):
        return pltpu.make_async_remote_copy(
            src_ref=source,
            dst_ref=target,
            send_sem=self.send_sem[stage].at[c.value % ring],
            recv_sem=self.recv[stage].at[c.value % ring],
            device_id=peer,
            device_id_type=MESH_ID,
        )

    def give(self, stage, ring, c, peer):
        @within(c, 0, self.total - ring)
        def _():
            pl.semaphore_signal(
                self.free[stage], inc=1, device_id=peer, device_id_type=MESH_ID
            )

    def take(self, stage, ring, c):
        @within(c, ring, self.total)
        def _():
            pl.semaphore_wait(self.free[stage], 1)

    def core_copy(self, c, side, source):
        return pltpu.make_async_remote_copy(
            src_ref=source,
            dst_ref=self.core_in.at[c.value % AHEAD, side],
            send_sem=self.core_send.at[c.value % AHEAD, side],
            recv_sem=self.core_recv.at[c.value % AHEAD, side],
            device_id=self.core_peer,
            device_id_type=MESH_ID,
        )

    def load(self, c, side, source):
        return pltpu.make_async_copy(
            source, self.own.at[c.value % AHEAD, side], self.load_sem.at[c.value % AHEAD, side]
        )

    def begin(self, c):
        first = 0
        for group, count in zip(self.groups, self.counts):

            @within(c, first, first + count)
            def _(group=group, first=first):
                at = c.value - first
                for side in range(2):
                    self.core_copy(c, side, group.at[2 * side + 1, at]).start()
                for side in range(2):
                    self.load(c, side, group.at[2 * side, at]).start()

            first += count

    def y_copy(self, c):
        return self.remote(0, Y_RING, c, self.far.at[c.value % FAR_RING], self.y_in.at[c.value % Y_RING], self.y_peer)

    def x_copy(self, c):
        source = self.y_in.at[c.value % Y_RING, 1 - self.x]
        return self.remote(1, RING, c, source, self.x_in.at[c.value % RING], self.x_peer)

    def z_copy(self, c):
        source = self.x_in.at[c.value % RING, 1 - self.z]
        return self.remote(2, RING, c, source, self.z_in.at[c.value % RING], self.z_peer)

    def w_copy(self, i, c):
        source = self.z_in if i == 0 else self.w_in[i - 1]
        return self.remote(
            3 + i, RING, c, source.at[c.value % RING], self.w_in[i].at[c.value % RING], self.row_peers[2 + i]
        )

    def back_z_copy(self, c, place):
        at = self.out.at[c.value, self.x, place]
        return self.remote(3 + len(self.w_in), RING, c, self.kept.at[c.value % RING], at, self.z_peer)

    def kept_copy(self, c):
        at = self.out.at[c.value, self.x, self.z]
        return pltpu.make_async_copy(self.kept.at[c.value % RING], at, self.kept_sem.at[c.value % RING])

    def back_x_copy(self, c, place):
        at = self.out.at[c.value, place]
        return self.remote(4 + len(self.w_in), RING, c, at, at, self.x_peer)

    def core_stage(self, c):
        slot, at = c.value % AHEAD, c.value % FAR_RING
        for side in range(2):
            self.load(c, side, self.own.at[slot, side]).wait()
            self.core_copy(c, side, self.own.at[slot, side]).wait()
        self.far[at] = add(self.own[slot, 1], self.core_in[slot, 1])
        self.take(0, Y_RING, c)
        self.y_copy(c).start()
        self.near[at] = add(self.own[slot, 0], self.core_in[slot, 0])

        @within(c, 0, self.total - AHEAD)
        def _():
            pl.semaphore_signal(
                self.core_free, inc=1, device_id=self.core_peer, device_id_type=MESH_ID
            )

    def y_stage(self, c):
        self.y_copy(c).wait()
        slot = c.value % Y_RING
        self.y_in[slot] = add(self.y_in[slot], self.near[c.value % FAR_RING])
        self.take(1, RING, c)
        self.x_copy(c).start()

    def x_stage(self, c):
        self.x_copy(c).wait()
        slot = c.value % RING
        self.x_in[slot] = add(self.x_in[slot], self.y_in[c.value % Y_RING, self.x])
        self.give(0, Y_RING, c, self.y_peer)
        self.take(2, RING, c)
        self.z_copy(c).start()

    def z_stage(self, c):
        self.z_copy(c).wait()
        slot = c.value % RING
        self.z_in[slot] = add(self.z_in[slot], self.x_in[slot, self.z])
        self.give(1, RING, c, self.x_peer)
        self.take(3, RING, c)
        self.w_copy(0, c).start()

    def w_stage(self, i, c):
        self.w_copy(i, c).wait()
        slot = c.value % RING
        source = self.z_in if i == 0 else self.w_in[i - 1]
        value = add(self.w_in[i][slot], source[slot])
        giver = self.z_peer if i == 0 else self.row_peers[1 + i]
        self.give(2 + i, RING, c, giver)
        if i + 1 < len(self.w_in):
            self.w_in[i][slot] = value
            self.take(4 + i, RING, c)
            self.w_copy(i + 1, c).start()
        else:
            self.kept[slot] = value
            self.give(3 + i, RING, c, self.row_peers[2 + i])
            self.kept_copy(c).start()
            self.back_z_copy(c, self.z).start()

    def back_z_stage(self, c):
        self.kept_copy(c).wait()
        self.back_z_copy(c, self.z).wait_send()
        self.back_z_copy(c, 1 - self.z).wait_recv()
        self.back_x_copy(c, self.x).start()

    def back_x_stage(self, c):
        self.back_x_copy(c, self.x).wait_send()
        self.back_x_copy(c, 1 - self.x).wait_recv()


def reduce_kernel(counts, row_bits, *refs):
    count = len(counts)
    reducer = Reducer(refs[:count], counts, row_bits, refs[count], refs[count + 1 :])
    reducer.greet()
    reducer.start()

    def step(t, carry):
        t = Step(t, 0, reducer.steps - 1)
        reducer.send(t)
        reducer.step(t)
        reducer.load_next(t)
        return carry

    lax.fori_loop(0, reducer.steps, step, 0)


def chunk_view(group):
    turns, rows, d = group.shape
    return group.reshape(turns, rows // CHUNK, 2, 2, QUARTER, d)


def split_sums(result, counts):
    d = result.shape[-1]
    sums, first = [], 0
    for n in counts:
        sums.append(result[first : first + n].reshape(n * CHUNK, d))
        first += n
    return sums


def reduce_all(place, groups):
    d = groups[0].shape[-1]
    counts = [g.shape[1] // CHUNK for g in groups]
    row_bits = place.bits("row")
    result = pl.pallas_call(
        functools.partial(reduce_kernel, counts, row_bits),
        in_specs=[pl.BlockSpec(memory_space=pl.ANY)] * len(groups),
        out_specs=pl.BlockSpec(memory_space=pl.ANY),
        out_shape=jax.ShapeDtypeStruct((sum(counts), 2, 2, QUARTER, d), BF),
        scratch_shapes=Reducer.scratch(row_bits, d),
        compiler_params=pltpu.CompilerParams(
            collective_id=0, has_side_effects=True, vmem_limit_bytes=48 * 2**20
        ),
        cost_estimate=cost(0, 4 * sum(counts) * CHUNK * d),
        name="reduce_all",
    )(*[chunk_view(g) for g in groups])
    return split_sums(result, counts)


def xor(left, right, bits):
    total = 0
    for bit in bits:
        a, b = (left // bit) % 2, (right // bit) % 2
        total = total + bit * (a + b - 2 * a * b)
    return total


HALF = 2 * CHUNK


def pair_back(pair, width, q, k, v, grad, wo, mixed, logs, bias, dks, dvs, put):
    length = logs.shape[0]
    for number, here in enumerate(tiles_of(length)):
        lane = lax.broadcasted_iota(jnp.int32, (here.stop - here.start, LANES), 1)
        queries = q(here) * BF(HD**-0.5)
        grads = nt(grad[here, :], wo).astype(BF)
        product = grads.astype(F32) * mixed(here).astype(F32)
        kept = logs[here, :]
        sides = []
        for head in range(2):
            mine = (lane < HD) if head == 0 else (lane >= HD)
            own_q = jnp.where(mine, queries, BF(0))
            own_grad = jnp.where(mine, grads, BF(0))
            chosen = lane == 2 * pair + head
            log_sum = jnp.sum(jnp.where(chosen, kept, 0.0), axis=1, keepdims=True)
            center = jnp.sum(jnp.where(mine, product, 0.0), axis=1, keepdims=True)
            probs = jnp.exp(nt(own_q, k) + bias[here, :width] - log_sum)
            score_grad = (probs * (nt(own_grad, v) - center)).astype(BF)
            sides.append(nn(score_grad, k))
            value_part = nn(own_grad.T, probs.astype(BF))
            key_part = nn(own_q.T, score_grad)
            if number == 0 and head == 0:
                dvs[:, :width] = value_part
                dks[:, :width] = key_part
            else:
                dvs[:, :width] += value_part
                dks[:, :width] += key_part
        put(here, (jnp.where(lane < HD, sides[0], sides[1]) * HD**-0.5).astype(BF))


NEAR = (
    "dec_q_seg", "enc_k_seg", "dec_k_seg", "enc_q_seg", "all_k_seg", "cross_q", "cross_mixed",
    "cross_logs", "cross_low", "dec_low", "memory", "ffn_gain_grad", "gains",
)
LATER = (
    "mid_low", "enc_mixed", "enc_logs", "fetched", "self_proj", "self_mixed", "self_logs",
    "self_low", "dec_new", "first", "answers",
)
FAR = (
    "encoded", "pairs", "cross", "cross_out", "mid", "tokens", "dec_qkv", "w_in", "w_out", "slope",
    "hidden", "enc_low", "w_qkv", "enc_proj", "attn_out", "self_out",
)


class Named:
    pass


def backward_kernel(counts, row_bits, memories, *refs):
    x, refs = Named(), list(refs)
    for name in NEAR + FAR:
        setattr(x, name, refs.pop(0))
    later_sources = [refs.pop(0) for _ in LATER]
    groups = [refs.pop(0) for _ in counts]
    out, cross_part, ff_out_part, ff_in_part, squares_part, self_part = refs[:6]
    token_grad, answer_grad, gain_sums = refs[6:9]
    (g, total, acc, low, g_low, pg, dq, dk, dv, dmk, dmv, bias, ks, vs, dks, dvs) = refs[9:25]
    (b0, b1, b2, b3, dcq, new2, low2, stage_a, stage_b) = refs[25:34]
    gain_acc, gain_in, copy_sem, later_sem, gain_send, gain_recv = refs[34:40]
    refs = refs[40:]
    later_targets = [refs.pop(0) for _ in LATER]
    for name, target in zip(LATER, later_targets):
        setattr(x, name, target)
    parts = [cross_part, ff_out_part, ff_in_part, squares_part, self_part]
    all_counts = list(counts) + [part.shape[1] for part in parts]
    reducer = Reducer(list(groups) + parts, all_counts, row_bits, out, refs)
    me = lax.axis_index("dp")
    d = g.shape[1]
    length, dec_length, count, width = g.shape[0], dcq.shape[0], b1.shape[0], bias.shape[1]
    blocks, pairs = ff_out_part.shape[1], d // LANES
    tiles = tiles_of(length)
    dsq, dsk, dsv = [g_low.at[i * dec_length : (i + 1) * dec_length] for i in range(3)]

    def fetch(source, target, i):
        return pltpu.make_async_copy(source, target, copy_sem.at[i])

    def lanes_of(pair):
        return pl.ds(pl.multiple_of(pair * LANES, LANES), LANES)

    later = [
        pltpu.make_async_copy(source, target, later_sem.at[i])
        for i, (source, target) in enumerate(zip(later_sources, later_targets))
    ]
    first_loads = [
        fetch(x.pairs.at[0], b1, 7),
        fetch(x.pairs.at[1], b2, 8),
        fetch(x.cross_out, b3, 9),
    ]
    encoded_load = fetch(x.encoded, b0, 6)
    early = [fetch(x.cross.at[1], dv, 0), fetch(x.cross.at[2], pg, 1), fetch(x.mid, token_grad, 2)]
    attend_loads = [
        fetch(x.enc_proj.at[0], b0, 6),
        fetch(x.enc_proj.at[1], b1, 7),
        fetch(x.enc_proj.at[2], b2, 8),
        fetch(x.attn_out, b3, 9),
    ]
    low_load = fetch(x.enc_low, b0, 6)
    qkv_loads = [fetch(x.w_qkv.at[i], target, 7 + i) for i, target in enumerate((b1, b2, b3))]
    tokens_load = fetch(x.tokens, pg, 10)
    cross_load = fetch(x.cross.at[0], b0, 6)
    self_out_load = fetch(x.self_out, low, 3)
    dec_qkv_loads = [fetch(x.dec_qkv.at[i], target, 11 + i) for i, target in enumerate((dq, dk, dv))]

    def ff_blocks(j):
        lanes = pl.ds(pl.multiple_of(j * d, d), d)
        return [
            fetch(x.w_in.at[:, lanes], b0, 6),
            fetch(x.w_out.at[lanes], b1, 7),
            fetch(x.slope.at[:, lanes], b2, 8),
            fetch(x.hidden.at[:, lanes], b3, 9),
        ]

    def start_all(copies):
        for copy in copies:
            copy.start()

    def wait_all(copies):
        for copy in copies:
            copy.wait()

    def product_to_acc(acts, grads):
        for n in range(0, d, HALF):
            acc[n : n + HALF, :] = tn(grads[:, n : n + HALF], acts[...])

    def shares(stage):
        for turn in range(4):
            shard = xor(me, turn, (1, 2))
            for i in range(4):
                start = pl.multiple_of(shard * CHUNK + i * QUARTER, 16)
                stage[turn, i // 2, i % 2] = acc[pl.ds(start, QUARTER), :].astype(BF)

    now = [0]

    def once(compute, copies=()):
        t = Step(now[0])
        now[0] += 1
        reducer.send(t)
        compute()
        start_all(copies)
        reducer.step(t)
        wait_all(copies)
        reducer.load_next(t)

    def loop(number, compute, copies=lambda i: ()):
        first = now[0]
        now[0] += number

        def body(i, carry):
            t = Step(first + i, first, first + number - 1)
            reducer.send(t)
            compute(i)
            reducer.step(t)
            wait_all(copies(i))
            reducer.load_next(t)
            return carry

        lax.fori_loop(0, number, body, 0)

    def squares(part, items, before=None, after=None):
        for n in range(0, len(items), 2):

            def compute(n=n):
                if n == 0 and before:
                    before()
                for stage, (acts, grads) in zip((stage_a, stage_b), items[n : n + 2]):
                    product_to_acc(acts, grads)
                    shares(stage)
                if n + 2 >= len(items) and after:
                    after()

            once(
                compute,
                [fetch(stage_a, part.at[:, n], 4), fetch(stage_b, part.at[:, n + 1], 5)],
            )

    start_all(first_loads)
    encoded_load.start()
    start_all(early)
    start_all(later)
    reducer.greet()
    reducer.start()
    ks[count:, :] = jnp.zeros((width - count, LANES), BF)
    vs[count:, :] = jnp.zeros((width - count, LANES), BF)
    gain_acc[0] = jnp.zeros_like(gain_acc[0])
    gain_acc[0, 4:5, :] = x.ffn_gain_grad[...]
    fill_bias(x.dec_q_seg, x.enc_k_seg, bias.at[:dec_length, :count], False, dec_length)
    wait_all(first_loads)

    def cross_attention(i):
        for side in range(2):
            pair = 2 * i + side
            lanes = lanes_of(pair)

            def put(here, value):
                dcq[here, lanes] = value

            pair_back(
                pair, count, lambda here: x.cross_q[0, here, lanes], b1[:, lanes], b2[:, lanes],
                x.dec_low, b3[lanes, :], lambda here: x.cross_mixed[here, lanes], x.cross_logs,
                bias, dks, dvs, put,
            )
            dq[:, lanes] = dks[:, :count].T.astype(BF)
            dk[:, lanes] = dvs[:, :count].T.astype(BF)

    loop(pairs // 2, cross_attention)
    squares(
        cross_part,
        [(x.cross_mixed, x.dec_low), (x.cross_low, dcq), (b0, dq), (b0, dk)],
        encoded_load.wait,
        lambda: start_all(ff_blocks(0)),
    )

    wait_all(early)
    wait_all(later)
    for here in tiles:
        value = nt(dq[here, :], dv[...]) + nt(dk[here, :], pg[...])
        g[here, :] = value
        g_low[here, :] = value.astype(BF)
        total[here, :] = jnp.zeros_like(value)

    def ff_copies(j):
        return [
            fetch(stage_a, ff_out_part.at[:, j], 4),
            fetch(stage_b, ff_in_part.at[xor(me, j, (1, 2))], 5),
        ]

    def feed_forward(j):
        wait_all(ff_blocks(j))
        for here in tiles:
            block = (nt(g_low[here, :], b1[...]) * b2[here, :].astype(F32)).astype(BF)
            pg[here, :] = block
            total[here, :] += nt(block, b0[...])
        product_to_acc(b3, g_low)
        shares(stage_a)
        for n in range(0, d, HALF):
            value = tn(x.mid_low[:, n : n + HALF], pg[...])
            for i in range(8):
                stage_b[n // CHUNK + i // 4, (i // 2) % 2, i % 2] = value[
                    i * QUARTER : (i + 1) * QUARTER, :
                ].astype(BF)
        start_all(ff_copies(j))

        @pl.when(j < blocks - 1)
        def _():
            start_all(ff_blocks(j + 1))

        @pl.when(j == blocks - 1)
        def _():
            start_all(attend_loads)

    loop(blocks, feed_forward, ff_copies)

    gain_sum = jnp.zeros((1, d), F32)
    for here in tiles:
        back, gain_part = rms_back(token_grad[here, :], x.gains[1:2, :], total[here, :])
        gain_sum = gain_sum + gain_part
        value = g[here, :] + back
        g[here, :] = value
        low[here, :] = value.astype(BF)
    gain_acc[0, 1:2, :] = gain_sum
    tokens_load.start()

    fill_bias(x.enc_q_seg, x.all_k_seg, bias, False, tiles[0].stop)
    wait_all(attend_loads)

    def attention(pair):
        lanes = lanes_of(pair)
        ks[:count, :] = b1[:, lanes]
        vs[:count, :] = b2[:, lanes]
        ks[count : count + memories, :] = x.memory[0, :, lanes]
        vs[count : count + memories, :] = x.memory[1, :, lanes]

        def put(here, value):
            dq[here, lanes] = value

        pair_back(
            pair, width, lambda here: b0[here, lanes], ks[...], vs[...], low, b3[lanes, :],
            lambda here: x.enc_mixed[here, lanes], x.enc_logs, bias, dks, dvs, put,
        )
        dk[:, lanes] = dks[:, :count].T.astype(BF)
        dv[:, lanes] = dvs[:, :count].T.astype(BF)
        dmk[:, lanes] = dks[:, count:].T[:memories].astype(BF)
        dmv[:, lanes] = dvs[:, count:].T[:memories].astype(BF)

        @pl.when(pair == pairs - 1)
        def _():
            low_load.start()
            start_all(qkv_loads)

    loop(pairs, attention)

    def after_squares():
        cross_load.start()
        self_out_load.start()

    squares(
        squares_part,
        [(b0, dq), (b0, dk), (b0, dv), (x.enc_mixed, low), (x.fetched, dmk), (x.fetched, dmv)],
        low_load.wait,
        after_squares,
    )

    def token_gradient():
        wait_all(qkv_loads)
        tokens_load.wait()
        gain_sum = jnp.zeros((1, d), F32)
        for here in tiles:
            value = nt(dq[here, :], b1[...]) + nt(dk[here, :], b2[...]) + nt(dv[here, :], b3[...])
            back, gain_part = rms_back(pg[here, :].astype(F32), x.gains[0:1, :], value)
            gain_sum = gain_sum + gain_part
            token_grad[here, :] = g[here, :] + back
        gain_acc[0, 0:1, :] = gain_sum
        start_all(dec_qkv_loads)

    once(token_gradient)

    def to_first():
        cross_load.wait()
        back, gain_acc[0, 3:4, :] = rms_back(x.first[...], x.gains[3:4, :], nt(dcq[...], b0[...]))
        value = x.dec_new[...] + back
        new2[...] = value
        low2[...] = value.astype(BF)
        fill_bias(x.dec_q_seg, x.dec_k_seg, bias.at[:dec_length, :dec_length], True, dec_length)
        self_out_load.wait()

    once(to_first)

    def self_attention(i):
        for side in range(2):
            pair = 2 * i + side
            lanes = lanes_of(pair)

            def put(here, value):
                dsq[here, lanes] = value

            pair_back(
                pair, dec_length, lambda here: x.self_proj[0, here, lanes],
                x.self_proj[1, :, lanes], x.self_proj[2, :, lanes], low2, low[lanes, :],
                lambda here: x.self_mixed[here, lanes], x.self_logs, bias, dks, dvs, put,
            )
            dsk[:, lanes] = dks[:, :dec_length].T.astype(BF)
            dsv[:, lanes] = dvs[:, :dec_length].T.astype(BF)

    loop(pairs // 2, self_attention)
    squares(
        self_part,
        [(x.self_low, dsq), (x.self_low, dsk), (x.self_low, dsv), (x.self_mixed, low2)],
    )

    def answer_gradient():
        wait_all(dec_qkv_loads)
        value = nt(dsq[...], dq[...]) + nt(dsk[...], dk[...]) + nt(dsv[...], dv[...])
        back, gain_acc[0, 2:3, :] = rms_back(x.answers[...].astype(F32), x.gains[2:3, :], value)
        answer_grad[...] = new2[...] + back

    once(answer_gradient)

    def gain_copy(i):
        return pltpu.make_async_remote_copy(
            src_ref=gain_acc.at[i],
            dst_ref=gain_in.at[i],
            send_sem=gain_send.at[i],
            recv_sem=gain_recv.at[i],
            device_id=reducer.peers[i],
            device_id_type=MESH_ID,
        )

    last = len(reducer.peers)

    def gain_step(i):
        if i:
            gain_copy(i - 1).wait()
            value = gain_acc[i - 1] + gain_in[i - 1]
            if i < last:
                gain_acc[i] = value
            else:
                gain_sums[...] = value
        if i < last:
            gain_copy(i).start()

    gain_step(0)
    for i in range(1, last + 1):
        once(lambda: None)
        gain_step(i)
    loop(reducer.steps - now[0], lambda i: None)


def backward(place, groups, x):
    t, d = x["tokens"].shape
    dec_t = x["answers"].shape[0]
    ff = x["w_in"].shape[1]
    blocks, memories = ff // d, x["fetched"].shape[0]
    width = x["all_k_seg"].shape[1]
    row_bits = place.bits("row")
    counts = [g.shape[1] // CHUNK for g in groups]
    new = [4, blocks, ff // (4 * CHUNK), 6, 4]
    total = sum(counts) + sum(new)
    exchanges = 2 + len(row_bits)
    anywhere = pl.BlockSpec(memory_space=pl.ANY)
    vmem = pl.BlockSpec(memory_space=pltpu.VMEM)
    operands = [(x[name], vmem) for name in NEAR]
    operands += [(x[name], anywhere) for name in FAR + LATER]
    operands += [(chunk_view(g), anywhere) for g in groups]
    chunk = (2, 2, QUARTER, d)
    out_shape = [jax.ShapeDtypeStruct((total,) + chunk, BF)]
    out_shape += [jax.ShapeDtypeStruct((4, n) + chunk, BF) for n in new]
    out_shape += [
        jax.ShapeDtypeStruct((t, d), F32),
        jax.ShapeDtypeStruct((dec_t, d), F32),
        jax.ShapeDtypeStruct((8, d), F32),
    ]
    square = lambda kind: pltpu.VMEM((t, d), kind)
    scratch = (
        [square(F32), square(F32), pltpu.VMEM((d, d), F32)]
        + [square(BF)] * 6
        + [pltpu.VMEM((memories, d), BF)] * 2
        + [pltpu.VMEM((t, width), F32)]
        + [pltpu.VMEM((width, LANES), BF)] * 2
        + [pltpu.VMEM((LANES, width), F32)] * 2
        + [square(BF)] * 4
        + [pltpu.VMEM((dec_t, d), BF), pltpu.VMEM((dec_t, d), F32), pltpu.VMEM((dec_t, d), BF)]
        + [pltpu.VMEM((4,) + chunk, BF), pltpu.VMEM((4,) + chunk, BF)]
        + [pltpu.VMEM((exchanges, 8, d), F32)] * 2
        + [pltpu.SemaphoreType.DMA((14,)), pltpu.SemaphoreType.DMA((len(LATER),))]
        + [pltpu.SemaphoreType.DMA((exchanges,))] * 2
        + [pltpu.VMEM(x[name].shape, x[name].dtype) for name in LATER]
        + Reducer.scratch(row_bits, d)
    )
    results = pl.pallas_call(
        functools.partial(backward_kernel, counts, row_bits, memories),
        in_specs=[spec for _, spec in operands],
        out_specs=[anywhere] * 6 + [vmem] * 3,
        out_shape=out_shape,
        scratch_shapes=scratch,
        compiler_params=pltpu.CompilerParams(
            collective_id=1, has_side_effects=True, vmem_limit_bytes=60 * 2**20
        ),
        cost_estimate=cost(2 * t * d * (4 * ff + 14 * d), 30 * total * CHUNK * d),
        name="backward",
    )(*[array for array, _ in operands])
    return results[0], results[6], results[7], results[8]


def finish_kernel(places, index, sums, gain_sums, *refs):
    outs, gain_outs = refs[: len(places)], refs[len(places) : len(places) + 3]
    wide, store_sem = refs[len(places) + 3 :]
    spots = [(out, at, i) for out, (count, at) in zip(outs, places) for i in range(count)]
    total = len(spots)

    def store(c):
        out, at, i = spots[c]
        return pltpu.make_async_copy(
            wide.at[c % 4], out.at[at(i)], store_sem.at[c % 4]
        )

    size = gain_outs[2].shape[1]
    for shard in range(gain_sums.shape[1] // size):

        @pl.when(index[0] == shard)
        def _(shard=shard):
            lanes = slice(shard * size, (shard + 1) * size)
            gain_outs[0][...] = gain_sums[0:2, lanes]
            gain_outs[1][...] = gain_sums[2:4, lanes]
            gain_outs[2][...] = gain_sums[4:5, lanes]

    for c in range(total):
        if c >= 4:
            store(c - 4).wait()
        wide[c % 4] = sums[c].astype(F32)
        store(c).start()
    for c in range(total - 4, total):
        store(c).wait()


def finish_sums(place, sums, gain_sums, blocks):
    d = gain_sums.shape[1]
    total = sums.shape[0]
    one = lambda i: ()
    lead = lambda i: (i,)
    rows = lambda i: (pl.ds(i * CHUNK, CHUNK), slice(None))
    lanes = lambda i: (slice(None), pl.ds(i * d, d))
    flat, tall, wide = (CHUNK, d), (blocks * CHUNK, d), (CHUNK, blocks * d)
    kinds = [
        (wide, blocks, lanes),
        (tall, blocks, rows),
        (flat, 1, one),
        ((3,) + flat, 3, lead),
        (wide, blocks, lanes),
        (tall, blocks, rows),
        ((3,) + flat, 3, lead),
        (flat, 1, one),
        ((2,) + flat, 2, lead),
        ((3,) + flat, 3, lead),
        (flat, 1, one),
    ]
    anywhere = pl.BlockSpec(memory_space=pl.ANY)
    gain_shapes = [(2, CHUNK), (2, CHUNK), (1, CHUNK)]
    return pl.pallas_call(
        functools.partial(finish_kernel, [(count, at) for _, count, at in kinds]),
        in_specs=[
            pl.BlockSpec(memory_space=pltpu.SMEM),
            full((total, CHUNK, d)),
            full((8, d)),
        ],
        out_specs=[anywhere] * len(kinds) + [full(shape) for shape in gain_shapes],
        out_shape=[jax.ShapeDtypeStruct(shape, F32) for shape, _, _ in kinds]
        + [jax.ShapeDtypeStruct(shape, F32) for shape in gain_shapes],
        scratch_shapes=[
            pltpu.VMEM((4, CHUNK, d), F32),
            pltpu.SemaphoreType.DMA((4,)),
        ],
        compiler_params=params(24),
        cost_estimate=cost(0, 6 * total * CHUNK * d),
        name="finish_sums",
    )(place.index, sums, gain_sums)


def fold_outer(place, value):
    while value.shape[0] > 4:
        half = value.shape[0] // 2
        value = add(value[:half], place.swap(value[half:], "dp", half))
    return value


def gain_group(place, gains):
    shards = place.sizes["dp"]
    count, d = gains.shape
    parts = gains.reshape(count, shards, -1)
    turned = jnp.stack(
        [lax.dynamic_index_in_dim(parts, place.dp ^ turn, 1, False) for turn in range(shards)]
    )
    return jnp.pad(turned.astype(BF), ((0, 0), (0, CHUNK - count), (0, d - parts.shape[2])))


def weights_of(value, count, size):
    value = value[: count * size].reshape(count, size, -1)
    return jnp.swapaxes(value, 1, 2).astype(F32)


def encoder_back(
    place, groups, q_seg, k_seg, dck, dcv, cross, mid, tokens, dec_gain_grads, gains,
    w_in, w_out, slope, hidden, mid_low, qkv, memory, mixed, logs, wo, enc_low, fetched, w_qkv,
):
    pre_grad, grad_low, new, low, mid_gain_grad = ffn_back(
        (dck, dcv), cross, w_in, w_out, slope, mid, gains[1]
    )
    dq, dk, dv, dmk, dmv = attend_back(
        (qkv, 0), (qkv, 1), (qkv, 2), mixed, logs, low, wo, q_seg, k_seg, memory
    )
    parts = [
        ff_out_grads(place, hidden, grad_low),
        ff_in_grads(place, mid_low, pre_grad),
        square_grads(place, [(enc_low, [dq, dk, dv]), (mixed, [low]), (fetched, [dmk, dmv])]),
    ]
    token_grad, _, enc_gain_grad = proj_back(tokens, gains[0], new, w_qkv, [dq, dk, dv])
    gain_part = gain_group(
        place, jnp.concatenate([enc_gain_grad, mid_gain_grad] + dec_gain_grads)
    )
    parts = [fold_outer(place, part) for part in groups + parts + [gain_part]]
    sums = reduce_all(place, parts)
    size = tokens.shape[1] // place.sizes["dp"]
    return sums, token_grad, sums[-1][:5, :size].astype(F32)


def fetch_memory(place, table, ids):
    rows = table.shape[0]
    others = range(1, place.sizes["dp"])
    wanted = [ids] + [place.swap(ids, "dp", turn) for turn in others]
    local = jnp.concatenate(wanted) - place.dp * rows
    chosen = (local[:, None] == jnp.arange(rows)[None, :]).astype(BF)
    picked = nn(chosen, table).astype(BF).reshape(len(wanted), ids.shape[0], -1)
    result = picked[0]
    for turn in others:
        result = result + place.swap(picked[turn], "dp", turn)
    return result


def on_device(
    sizes,
    enc_input,
    dec_input,
    memory_table,
    memory_ids,
    enc_segments,
    dec_segments,
    enc_qkv,
    enc_attn_out,
    mem_proj,
    enc_gains,
    enc_ff_in,
    enc_ff_out,
    dec_qkv,
    dec_self_out,
    dec_cross,
    dec_cross_out,
    dec_gains,
    dec_ff_in,
    dec_ff_out,
    out_grad,
):
    place = Place(sizes)
    direct = sizes["dp"] == 4
    tokens, answers = enc_input[0], dec_input[0]
    fetched = fetch_memory(place, memory_table, memory_ids.reshape(-1))
    memories = fetched.shape[0]
    all_gains = jnp.concatenate([enc_gains, dec_gains]).astype(F32)
    enc_gain = [(all_gains, i) for i in range(2)]
    dec_gain = [(all_gains, i) for i in range(2, 5)]

    enc_at, dec_at = enc_segments[0], dec_segments[0]
    enc_q_seg, dec_q_seg = enc_at[:, None], dec_at[:, None]
    owner = jnp.arange(memories, dtype=jnp.int32) // TOPK
    padding = jnp.full((-memories % LANES,), -1, jnp.int32)
    all_k_seg = jnp.concatenate([enc_at, owner, padding])[None]
    enc_k_seg, dec_k_seg = enc_at[None], dec_at[None]

    self_low, self_proj = project(answers, dec_gain[0], dec_qkv, 0, 3)
    self_q, self_k, self_v = [(self_proj, j) for j in range(3)]
    self_mixed, self_logs = attend(self_q, self_k, self_v, dec_q_seg, dec_k_seg, causal=True)
    first, cross_low, cross_q = project(
        answers, dec_gain[1], dec_cross, 0, 1, self_mixed, dec_self_out
    )
    cross_q = (cross_q, 0)

    enc_low, enc_proj = project(tokens, enc_gain[0], enc_qkv, 0, 3)
    enc_q, enc_k, enc_v = [(enc_proj, j) for j in range(3)]
    memory = project_plain(fetched, mem_proj, 0, 2)
    enc_mixed, enc_logs = attend(enc_q, enc_k, enc_v, enc_q_seg, all_k_seg, memory)
    middle, mid_low, enc_hidden, enc_slope, encoded = ffn_forward(
        tokens, enc_mixed, enc_attn_out, enc_gain[1], enc_ff_in, enc_ff_out, far=True
    )
    pairs = project_plain(encoded, dec_cross, 1, 2)
    cross_k, cross_v = (pairs, 0), (pairs, 1)
    cross_mixed, cross_logs = attend(cross_q, cross_k, cross_v, dec_q_seg, enc_k_seg)
    second, ffn_low, dec_hidden, dec_slope, final = ffn_forward(
        first, cross_mixed, dec_cross_out, dec_gain[2], dec_ff_in, dec_ff_out
    )

    grad = out_grad[0]
    if direct:
        new, low, ffn_gain_grad, dec_ff_out_part, dec_ff_in_part = ffn_back_weights(
            place, grad, dec_ff_in, dec_ff_out, dec_slope, dec_hidden, ffn_low, second, dec_gain[2]
        )
        d = tokens.shape[1]
        result, token_grad, answer_grad, gain_sums = backward(
            place,
            [dec_ff_out_part, dec_ff_in_part],
            dict(
                dec_q_seg=dec_q_seg, enc_k_seg=enc_k_seg, dec_k_seg=dec_k_seg,
                enc_q_seg=enc_q_seg, all_k_seg=all_k_seg, encoded=encoded, cross=dec_cross,
                mid=middle, tokens=tokens, dec_qkv=dec_qkv, w_in=enc_ff_in, w_out=enc_ff_out,
                slope=enc_slope, hidden=enc_hidden, enc_low=enc_low, w_qkv=enc_qkv,
                cross_q=cross_q[0], pairs=pairs, cross_mixed=cross_mixed, cross_out=dec_cross_out,
                self_proj=self_proj, self_mixed=self_mixed, self_out=dec_self_out,
                enc_proj=enc_proj, memory=memory, attn_out=enc_attn_out, cross_logs=cross_logs,
                cross_low=cross_low, self_logs=self_logs, self_low=self_low, dec_low=low,
                dec_new=new, first=first, answers=answers, mid_low=mid_low, enc_mixed=enc_mixed,
                enc_logs=enc_logs, fetched=fetched, ffn_gain_grad=ffn_gain_grad,
                gains=all_gains,
            ),
        )
        (
            dec_out_grad, dec_in_grad, cross_out_grad, cross_grad, out_ff_grad, in_ff_grad,
            qkv_grad, attn_out_grad, mem_grad, self_grad, self_out_grad,
            enc_gain_grad, dec_gain_grad, ffn_gain_grad,
        ) = finish_sums(place, result.reshape(-1, CHUNK, d), gain_sums, enc_ff_in.shape[1] // d)
        turn = lambda value: jnp.swapaxes(value, -1, -2)
        return (
            final[None],
            token_grad[None],
            answer_grad[None],
            turn(qkv_grad),
            turn(attn_out_grad),
            turn(mem_grad),
            enc_gain_grad,
            in_ff_grad,
            turn(out_ff_grad),
            turn(self_grad),
            turn(self_out_grad),
            turn(cross_grad),
            turn(cross_out_grad),
            dec_gain_grad,
            dec_in_grad,
            turn(dec_out_grad),
            ffn_gain_grad[0],
        )

    dec_ff_out_part = ff_out_grads(place, dec_hidden, grad)
    pre_grad, _, new, low, ffn_gain_grad = ffn_back(
        grad, None, dec_ff_in, dec_ff_out, dec_slope, second, all_gains[4:5]
    )
    dec_ff_in_part = ff_in_grads(place, ffn_low, pre_grad)
    dcq, dck, dcv = attend_back(
        cross_q, cross_k, cross_v, cross_mixed, cross_logs, low, dec_cross_out,
        dec_q_seg, enc_k_seg,
    )
    cross_part = square_grads(
        place, [(cross_mixed, [low]), (cross_low, [dcq]), (encoded, [dck, dcv])]
    )
    new, low, cross_gain_grad = proj_back(first, all_gains[3:4], new, dec_cross, [dcq])
    dsq, dsk, dsv = attend_back(
        self_q, self_k, self_v, self_mixed, self_logs, low, dec_self_out,
        dec_q_seg, dec_k_seg, causal=True,
    )
    self_part = square_grads(place, [(self_low, [dsq, dsk, dsv]), (self_mixed, [low])])
    answer_grad, _, self_gain_grad = proj_back(answers, all_gains[2:3], new, dec_qkv, [dsq, dsk, dsv])
    dec_gain_grads = [self_gain_grad, cross_gain_grad, ffn_gain_grad]
    dec_parts = [dec_ff_out_part, dec_ff_in_part, cross_part, self_part]
    sums, token_grad, gains = encoder_back(
        place, dec_parts, enc_q_seg, all_k_seg, dck, dcv, dec_cross, middle, tokens,
        dec_gain_grads, [all_gains[:1], all_gains[1:2]], enc_ff_in, enc_ff_out, enc_slope, enc_hidden, mid_low,
        enc_proj, memory, enc_mixed, enc_logs, enc_attn_out, enc_low, fetched, enc_qkv,
    )
    size = tokens.shape[1] // sizes["dp"]
    blocks = enc_ff_in.shape[1] // tokens.shape[1]
    ff_size = enc_ff_in.shape[1] // sizes["dp"]
    enc_squares = weights_of(sums[6], 6, size)
    self_squares = weights_of(sums[3], 4, size)
    cross_squares = weights_of(sums[2], 4, size)
    return (
        final[None],
        token_grad[None],
        answer_grad[None],
        enc_squares[0:3],
        enc_squares[3],
        enc_squares[4:6],
        gains[0:2],
        weights_of(sums[5], 1, ff_size)[0],
        weights_of(sums[4], blocks, size).reshape(-1, size),
        self_squares[0:3],
        self_squares[3],
        cross_squares[1:4],
        cross_squares[0],
        gains[2:4],
        weights_of(sums[1], 1, ff_size)[0],
        weights_of(sums[0], blocks, size).reshape(-1, size),
        gains[4],
    )


def solution(mesh):
    rows = P(("row", "dp"), None, None)
    in_specs = (
        (rows, rows, P("dp", None), rows, P(("row", "dp"), None), P(("row", "dp"), None))
        + (P(),) * 13
        + (rows,)
    )
    cube, flat = P(None, None, "dp"), P(None, "dp")
    out_specs = (
        (rows, rows, rows)
        + (cube, flat, cube, flat, flat, flat)
        + (cube, flat, cube, flat, flat, flat, flat)
        + (P("dp"),)
    )
    return jax.shard_map(
        functools.partial(on_device, dict(mesh.shape)),
        mesh=mesh,
        in_specs=in_specs,
        out_specs=out_specs,
        check_vma=False,
    )
```
